32 devices in a mesh: dp: 8 (over z, y), tensor: 4 (over x, core).
Axes of the slice: x: 2, y: 2, z: 4, core: 2. Of those that a mesh axis runs over, the one named last changes fastest.
Arguments:
- tokens: bfloat16 [8, 16, 16, 1152], P('dp'), may hold values from -6 to 6
- lengths: int32 [8], P('dp'), may hold values from 8 to 16
- timesteps: int32 [8], P('dp'), may hold values from 0 to 999
- labels: int32 [8], P('dp'), may hold values from 0 to 100
- class_table: bfloat16 [101, 1152], P(None, 'tensor'), may hold values from -6 to 6
- ada_weight: bfloat16 [1152, 6912], P(None, 'tensor'), may hold values from -0.1875 to 0.1875
- ada_bias: bfloat16 [6912], P('tensor'), may hold values from -3 to 3
- qkv_weight: bfloat16 [1152, 3456], P(None, 'tensor'), may hold values from -0.1875 to 0.1875
- qv_bias: bfloat16 [2304], P('tensor'), may hold values from -3 to 3
- out_weight: bfloat16 [1152, 1152], P(None, 'tensor'), may hold values from -0.375 to 0.375
- proj_bias: bfloat16 [1152], replicated, may hold values from -3 to 3
- up_weight: bfloat16 [1152, 4608], P(None, 'tensor'), may hold values from -0.1875 to 0.1875
- fc1_bias: bfloat16 [4608], P('tensor'), may hold values from -3 to 3
- down_weight: bfloat16 [1152, 4608], P(None, 'tensor'), may hold values from -0.09375 to 0.09375
- fc2_bias: bfloat16 [1152], replicated, may hold values from -3 to 3
- cotangent: bfloat16 [8, 16, 16, 1152], P('dp'), may hold values from -6 to 6
Outputs:
- result: bfloat16 [8, 16, 16, 1152], P('dp')
- tokens_grad: bfloat16 [8, 16, 16, 1152], P('dp')
- qkv_weight_grad: float32 [1152, 3456], P('dp', 'tensor')
- out_weight_grad: float32 [1152, 1152], P('dp', 'tensor')
- up_weight_grad: float32 [1152, 4608], P('dp', 'tensor')
- down_weight_grad: float32 [1152, 4608], P('dp', 'tensor')
- ada_weight_grad: float32 [1152, 6912], P('dp', 'tensor')
- class_table_grad: float32 [101, 1152], P(None, 'tensor')
- qv_bias_grad: float32 [2304], P('tensor')
- proj_bias_grad: float32 [1152], replicated
- fc1_bias_grad: float32 [4608], P('tensor')
- fc2_bias_grad: float32 [1152], replicated
- ada_bias_grad: float32 [6912], P('tensor')
The draws below stay inside these ranges and needn't reach their ends.
Inputs may be any that keep to these rules, and one draw needn't show every extreme that they name: Frames of clip c at positions below lengths[c] hold data, the others of the 16 slots are padding.
All inputs are finite; a program needn't handle non-finite values.
Results may differ from the reference program's by a relative error of at most 0.019.
Values may be sent and summed in bfloat16 or wider, within the bound.
No kernel may reach another device: no remote copies, remote signals or barrier semaphores. Data moves between devices by JAX's collectives and lax.ppermute only.
A program may use at most 128 MiB of HBM per device.

```python
import math
import jax
import jax.numpy as jnp
from jax import lax

D = 1152
HEADS = 16
HEAD_DIM = 72
FF = 4608
CLASSES = 101
FRAMES = 16
PATCH = 16
CLIPS_DEV = 1
CLIPS = 8
N_DP = 8


def place_ends(values, stream_key, low, largest):
    spot = [jax.random.randint(jax.random.fold_in(stream_key, axis), (), 0, length) for axis, length in enumerate(values.shape)]
    main_axis = values.shape.index(max(values.shape))
    next_to = spot[:main_axis] + [(spot[main_axis] + 1) % values.shape[main_axis]] + spot[main_axis + 1:]
    return values.at[tuple(spot)].set(low).at[tuple(next_to)].set(largest)


def with_spikes(array, rng, source, target, blocks, factor):
    def block_of(position):
        return (jnp.arange(array.shape[position]) // (array.shape[position] // blocks)).reshape((-1,) + (1,) * (array.ndim - 1 - position))

    one_side = jax.random.permutation(rng, blocks)[block_of(target)]
    other_side = (block_of(target) + blocks // 2) % blocks
    return jnp.where((block_of(source) == one_side) | (block_of(source) == other_side), factor * array, array)


def level_of(rng, dims, shards, least, high):
    loudness = 1.0
    for axis_at, blocks in shards:
        heights = jax.random.uniform(jax.random.fold_in(jax.random.fold_in(rng, 6), axis_at), (blocks,), jnp.float32, least / len(shards), high / len(shards))
        loudness = loudness * jnp.repeat(jnp.exp(heights), dims[axis_at] // blocks).reshape((-1,) + (1,) * (len(dims) - 1 - axis_at))
    return loudness


def bell_draw(own_key, shape, scale, limit, cuts=(), kind=jnp.bfloat16):
    entries = jax.random.normal(own_key, shape, jnp.float32) * scale
    if len(cuts) > 0:
        entries = level_of(own_key, shape, cuts, -0.22, 0.18) * entries
    return jnp.clip(entries, min=-limit, max=limit).astype(kind)


def noise_with(rng, extent, scale, bound, shards, heavy, kind=jnp.bfloat16):
    array = scale * jax.random.normal(rng, extent, jnp.float32)
    if shards:
        array = array * level_of(rng, extent, shards, -0.22, 0.18)
    return jnp.clip(with_spikes(array, jax.random.fold_in(rng, 3), *heavy), -bound, bound).astype(kind)


def setup_inputs(seed: int = 0) -> dict:
    arg_keys = jax.random.split(jax.random.key(seed), 17)
    tokens = bell_draw(arg_keys[0], (CLIPS, PATCH, FRAMES, D), 1.0, 6.0, ((0, 8),))
    lengths = place_ends(jax.random.randint(arg_keys[1], (CLIPS,), 8, 17), jax.random.fold_in(arg_keys[1], 1), 8, 16).astype(jnp.int32)
    timesteps = place_ends(jax.random.randint(arg_keys[2], (CLIPS,), 0, 1000), jax.random.fold_in(arg_keys[2], 1), 0, 999).astype(jnp.int32)
    labels = place_ends(jax.random.randint(arg_keys[3], (CLIPS,), 0, CLASSES), jax.random.fold_in(arg_keys[3], 1), 0, CLASSES - 1).astype(jnp.int32)
    class_table = bell_draw(arg_keys[4], (CLASSES, D), 1.0, 6.0, ((1, 4),))
    ada_weight = bell_draw(arg_keys[5], (D, 6 * D), D ** -0.5, 0.1875, ((1, 4),))
    ada_bias = bell_draw(arg_keys[6], (6 * D,), 0.5, 3.0, ((0, 4),))
    qkv_weight = bell_draw(arg_keys[7], (D, 3 * HEADS * HEAD_DIM), D ** -0.5, 0.1875, ((1, 4),))
    qv_bias = bell_draw(arg_keys[8], (2 * HEADS * HEAD_DIM,), 0.5, 3.0, ((0, 4),))
    out_weight = bell_draw(arg_keys[9], (D, HEADS * HEAD_DIM), (HEADS * HEAD_DIM // 4) ** -0.5, 0.375, ((1, 4),))
    proj_bias = bell_draw(arg_keys[10], (D,), 0.5, 3.0)
    up_weight = bell_draw(arg_keys[11], (D, FF), D ** -0.5, 0.1875, ((1, 4),))
    fc1_bias = bell_draw(arg_keys[12], (FF,), 0.5, 3.0, ((0, 4),))
    down_weight = bell_draw(arg_keys[13], (D, FF), FF ** -0.5, 0.09375, ((1, 4),))
    fc2_bias = bell_draw(arg_keys[14], (D,), 0.5, 3.0)
    cotangent = noise_with(arg_keys[15], (CLIPS, PATCH, FRAMES, D), 1.0, 6.0, ((0, 8),), (0, 3, 8, 2.0))
    return {"tokens": tokens, "lengths": lengths, "timesteps": timesteps, "labels": labels, "class_table": class_table, "ada_weight": ada_weight, "ada_bias": ada_bias, "qkv_weight": qkv_weight, "qv_bias": qv_bias, "out_weight": out_weight, "proj_bias": proj_bias, "up_weight": up_weight, "fc1_bias": fc1_bias, "down_weight": down_weight, "fc2_bias": fc2_bias, "cotangent": cotangent}


@jax.custom_vjp
def low(v):
    return lax.optimization_barrier(v.astype(jnp.bfloat16)).astype(jnp.float32)

@jax.custom_vjp
def low_back(v):
    return v

def low_keep(v):
    return (low(v), None)

def low_pass(kept, grad):
    return (grad,)

def back_keep(v):
    return (v, None)

def back_low(kept, grad):
    return (low(grad),)
low.defvjp(low_keep, low_pass)
low_back.defvjp(back_keep, back_low)

def matmul(left, right):
    return jnp.dot(left, right, precision=lax.Precision.HIGHEST, preferred_element_type=jnp.float32)

def matmul_trans(left, right):
    return lax.dot_general(left, right, (((1,), (1,)), ((), ())), precision=lax.Precision.HIGHEST, preferred_element_type=jnp.float32)

def time_embedding(times, width):
    half = width // 2
    freqs = jnp.exp(-math.log(10000.0) * jnp.arange(half, dtype=jnp.float32) / half)
    angles = times.astype(jnp.float32)[:, None] * freqs[None, :]
    return jnp.concatenate([jnp.cos(angles), jnp.sin(angles)], axis=1)

def layer_norm(value):
    center = value - lax.optimization_barrier(jnp.mean(value, axis=-1, keepdims=True))
    spread = lax.optimization_barrier(jnp.mean(center * center, axis=-1, keepdims=True))
    return center * lax.rsqrt(spread + 1e-06)

def forward(tokens, lengths, timesteps, labels, class_table, ada_weight, ada_bias, qkv_weight, qv_bias, out_weight, proj_bias, up_weight, fc1_bias, down_weight, fc2_bias):
    clips, patches, frames, width = tokens.shape
    seqs = clips * patches
    rows = seqs * frames
    cond = time_embedding(timesteps, width) + jnp.take(class_table, labels, axis=0)
    act_cond = low(jax.nn.silu(cond))
    modulation = low_back(matmul(act_cond, ada_weight) + ada_bias)
    mods = modulation.reshape(clips, 6, width)[:, :, None, None, :]
    valid = jnp.arange(frames, dtype=jnp.int32)[None, :] < lengths[:, None]
    keep = valid[:, None, :, None]
    normed1 = low(layer_norm(tokens) * (1.0 + mods[:, 1]) + mods[:, 0]).reshape(rows, width)
    qkv = matmul(normed1, qkv_weight).reshape(seqs, frames, HEADS, 3, HEAD_DIM)
    biases = qv_bias.reshape(HEADS, 2, HEAD_DIM)
    query = low(low_back(qkv[:, :, :, 0] + biases[:, 0]))
    key = low(low_back(qkv[:, :, :, 1]))
    value = low(low_back(qkv[:, :, :, 2] + biases[:, 1]))
    scores = low_back(jnp.einsum('sqhe,skhe->shqk', query, key, precision=lax.Precision.HIGHEST) * HEAD_DIM ** (-0.5))
    key_valid = jnp.broadcast_to(valid[:, None, :], (clips, patches, frames)).reshape(seqs, 1, 1, frames)
    scores = jnp.where(key_valid, scores, -1e+30)
    probs = low(jax.nn.softmax(scores, axis=-1))
    attended = jnp.einsum('shqk,skhe->sqhe', probs, value, precision=lax.Precision.HIGHEST)
    attended = low(low_back(attended)).reshape(rows, HEADS * HEAD_DIM)
    branch1 = low_back(matmul_trans(attended, out_weight) + proj_bias).reshape(tokens.shape)
    mid = tokens + mods[:, 2] * branch1
    normed2 = low(layer_norm(mid) * (1.0 + mods[:, 4]) + mods[:, 3]).reshape(rows, width)
    pre = low_back(matmul(normed2, up_weight) + fc1_bias)
    act_low = low(jax.nn.gelu(pre, approximate=True))
    branch2 = low_back(matmul_trans(act_low, down_weight) + fc2_bias).reshape(tokens.shape)
    final = mid + mods[:, 5] * branch2
    return jnp.where(keep, final, tokens)

def reference(tokens, lengths, timesteps, labels, class_table, ada_weight, ada_bias, qkv_weight, qv_bias, out_weight, proj_bias, up_weight, fc1_bias, down_weight, fc2_bias, cotangent):
    params = tuple((p.astype(jnp.float32) for p in (class_table, ada_weight, ada_bias, qkv_weight, qv_bias, out_weight, proj_bias, up_weight, fc1_bias, down_weight, fc2_bias)))
    shape_group = (N_DP, CLIPS_DEV, PATCH, FRAMES, D)
    inputs = (tokens.reshape(shape_group), lengths.reshape(N_DP, CLIPS_DEV), timesteps.reshape(N_DP, CLIPS_DEV), labels.reshape(N_DP, CLIPS_DEV), cotangent.reshape(shape_group))

    def group_step(carry, group):
        group_tokens, group_lengths, group_times, group_labels, group_cot = group

        def local_forward(value, *weights):
            return forward(value, group_lengths, group_times, group_labels, *weights)
        outputs, pullback = jax.vjp(local_forward, group_tokens.astype(jnp.float32), *params)
        grads = pullback(group_cot.astype(jnp.float32))
        summed = tuple((a + b for a, b in zip(carry, grads[1:])))
        return (summed, (outputs.astype(jnp.bfloat16), grads[0].astype(jnp.bfloat16)))
    start = tuple((jnp.zeros_like(p) for p in params))
    totals, (outputs, token_grads) = lax.scan(group_step, start, inputs)
    full = (CLIPS_DEV * N_DP, PATCH, FRAMES, D)
    return (outputs.reshape(full), token_grads.reshape(full), totals[3], totals[5], totals[7], totals[9], totals[1], totals[0], totals[4], totals[6], totals[8], totals[10], totals[2])
```

```python
import math

import jax
import jax.numpy as jnp
from jax import lax
from jax.sharding import PartitionSpec as P

HEAD_DIM = 72
BF = jnp.bfloat16
F32 = jnp.float32


def dot(left, right):
    return jnp.dot(left, right, preferred_element_type=F32)


def dot_trans(left, right):
    return lax.dot_general(left, right, (((1,), (1,)), ((), ())), preferred_element_type=F32)


def dot_rows(left, right):
    return lax.dot_general(left, right, (((0,), (0,)), ((), ())), preferred_element_type=F32)


def swap(value, axis, bit):
    size = lax.axis_size(axis)
    return lax.ppermute(value, axis, [(i, i ^ (1 << bit)) for i in range(size)])


def gather_bits(value, axis):
    rank = lax.axis_index(axis)
    for bit in range((lax.axis_size(axis) - 1).bit_length()):
        other = swap(value, axis, bit)
        mine_high = (rank >> bit) & 1
        value = jnp.where(
            mine_high == 0,
            jnp.concatenate([value, other], axis=0),
            jnp.concatenate([other, value], axis=0),
        )
    return value


def layer_norm(value):
    center = value - jnp.mean(value, axis=-1, keepdims=True)
    spread = jnp.mean(center * center, axis=-1, keepdims=True)
    inv = lax.rsqrt(spread + 1e-06)
    return center * inv, inv


def layer_norm_back(grad, scale, normed, inv):
    g = grad * (1.0 + scale)
    back = (
        g
        - jnp.mean(g, axis=-1, keepdims=True)
        - normed * jnp.mean(g * normed, axis=-1, keepdims=True)
    ) * inv
    return back, jnp.sum(grad, axis=0), jnp.sum(grad * normed, axis=0)


def gelu_pair(value):
    k = math.sqrt(2.0 / math.pi)
    square = value * value
    t = jnp.tanh(k * (value + 0.044715 * value * square))
    act = 0.5 * value * (1.0 + t)
    slope = 0.5 * (1.0 + t) + 0.5 * value * (1.0 - t * t) * k * (1.0 + 3 * 0.044715 * square)
    return act, slope


def shards(
    tokens,
    lengths,
    timesteps,
    labels,
    class_table,
    ada_weight,
    ada_bias,
    qkv_weight,
    qv_bias,
    out_weight,
    proj_bias,
    up_weight,
    fc1_bias,
    down_weight,
    fc2_bias,
    cotangent,
):
    clips, patches, frames, width = tokens.shape
    assert clips == 1
    rows = patches * frames
    half = rows // 2
    heads = out_weight.shape[1] // HEAD_DIM
    factor = HEAD_DIM ** (-0.5)
    columns = class_table.shape[1]
    ada_cols = ada_weight.shape[1]
    t_rank = lax.axis_index("tensor")
    d_rank = lax.axis_index("dp")
    n_dp = lax.axis_size("dp")
    core = t_rank & 1

    pair = lambda w: (w, swap(w, "tensor", 0))
    qkv_ws = pair(qkv_weight)
    qv_bs = pair(qv_bias.reshape(1, -1))
    out_ws = pair(out_weight)
    up_ws = pair(up_weight)
    fc1_bs = pair(fc1_bias.reshape(1, -1))
    down_ws = pair(down_weight)

    picked = lax.dynamic_slice_in_dim(class_table, labels[0], 1, 0)
    half_width = width // 2
    freqs = jnp.exp(-math.log(10000.0) * jnp.arange(half_width, dtype=F32) / half_width)
    angles = timesteps.astype(F32)[:, None] * freqs[None, :]
    clock = jnp.concatenate([jnp.cos(angles), jnp.sin(angles)], axis=1)
    embedded = gather_bits(picked.reshape(1, columns), "tensor").reshape(1, width)
    cond = clock + embedded.astype(F32)
    act_cond = jax.nn.silu(cond).astype(BF)
    mod_part = dot(act_cond, ada_weight) + ada_bias.astype(F32)
    mods = gather_bits(mod_part, "tensor").reshape(6, width)
    known = jnp.concatenate([cond, labels.astype(F32).reshape(1, 1)], axis=1)
    known = gather_bits(known, "dp")

    my_half = lambda v: lax.dynamic_slice_in_dim(v.reshape(rows, width), core * half, half, 0)
    inputs = my_half(tokens).astype(F32)
    upstream = my_half(cotangent).astype(F32)
    length = lengths[0]
    keep = (lax.broadcasted_iota(jnp.int32, (half, 1), 0) % frames) < length
    row_id = lax.broadcasted_iota(jnp.int32, (half, half), 0)
    col_id = lax.broadcasted_iota(jnp.int32, (half, half), 1)
    seen = ((row_id // frames) == (col_id // frames)) & ((col_id % frames) < length)

    norm1, inv1 = layer_norm(inputs)
    normed1 = (norm1 * (1.0 + mods[1:2]) + mods[0:1]).astype(BF)
    saved, attended, part1 = [], [], 0.0
    for w, b, o in zip(qkv_ws, qv_bs, out_ws):
        qkv = dot(normed1, w).reshape(half, heads, 3, HEAD_DIM)
        bias = b.astype(F32).reshape(heads, 2, HEAD_DIM)
        query = (qkv[:, :, 0] + bias[:, 0]).astype(BF)
        key = qkv[:, :, 1].astype(BF)
        value = (qkv[:, :, 2] + bias[:, 1]).astype(BF)
        scores = jnp.einsum("qhe,khe->hqk", query, key, preferred_element_type=F32) * factor
        scores = jnp.where(seen[None], scores, -1e30)
        raised = jnp.exp(scores - jnp.max(scores, axis=-1, keepdims=True))
        probs = raised / jnp.sum(raised, axis=-1, keepdims=True)
        att = jnp.einsum("hqk,khe->qhe", probs.astype(BF), value, preferred_element_type=F32)
        att = att.astype(BF).reshape(half, heads * HEAD_DIM)
        saved.append((query, key, value, probs))
        attended.append(att)
        part1 = part1 + dot_trans(att, o)
    part1 = part1.astype(BF)
    part1_other = swap(part1, "tensor", 1)

    final_grad = jnp.where(keep, upstream, 0.0)
    branch2_grad = (mods[5:6] * final_grad).astype(BF)
    act_grads = [dot(branch2_grad, w) for w in down_ws]

    branch1 = part1.astype(F32) + part1_other.astype(F32) + proj_bias.astype(F32)
    mid = inputs + mods[2:3] * branch1
    norm2, inv2 = layer_norm(mid)
    normed2 = (norm2 * (1.0 + mods[4:5]) + mods[3:4]).astype(BF)
    act_low, pre_low = [], []
    part2, part3 = 0.0, 0.0
    for u, b, w, g in zip(up_ws, fc1_bs, down_ws, act_grads):
        pre = dot(normed2, u) + b.astype(F32)
        act, slope = gelu_pair(pre)
        act_low.append(act.astype(BF))
        pre_low.append((g * slope).astype(BF))
        part3 = part3 + dot_trans(pre_low[-1], u)
        part2 = part2 + dot_trans(act_low[-1], w)
    part3 = part3.astype(BF)
    part3_other = swap(part3, "tensor", 1)
    part2 = part2.astype(BF)
    part2_other = swap(part2, "tensor", 1)

    both = lambda v: jnp.concatenate([v, swap(v, "tensor", 0)], axis=0)
    mine = lambda two: jnp.concatenate([two[0], swap(two[1], "tensor", 0)], axis=0)

    def scatter(grad):
        cols = grad.shape[1]
        grad = grad.reshape(n_dp, width // n_dp, cols)
        for bit in range((n_dp - 1).bit_length()):
            my_bit = (d_rank >> bit) & 1
            grad = grad.reshape(grad.shape[0] // 2, 2, width // n_dp, cols)
            send = lax.dynamic_index_in_dim(grad, 1 - my_bit, 1, keepdims=False).astype(BF)
            stay = lax.dynamic_index_in_dim(grad, my_bit, 1, keepdims=False)
            grad = stay + swap(send, "dp", bit).astype(F32)
        return grad.reshape(width // n_dp, cols)

    down_grad = scatter(dot_rows(both(branch2_grad), mine(act_low)))
    pre_mine = mine(pre_low)
    up_grad = scatter(dot_rows(both(normed2), pre_mine))
    fc1_grad = jnp.sum(pre_mine.astype(F32), axis=0, keepdims=True)
    fc2_part = jnp.sum(branch2_grad.astype(F32), axis=0)

    normed2_grad = part3.astype(F32) + part3_other.astype(F32)
    mid_ln_grad, shift2_part, scale2_part = layer_norm_back(normed2_grad, mods[4:5], norm2, inv2)
    mid_grad = final_grad + mid_ln_grad
    gate1_part = jnp.sum(mid_grad * branch1, axis=0)
    branch1_grad = (mods[2:3] * mid_grad).astype(BF)
    proj_part = jnp.sum(branch1_grad.astype(F32), axis=0)
    stacked, part4 = [], 0.0
    for (query, key, value, probs), w, o in zip(saved, qkv_ws, out_ws):
        att_grad = dot(branch1_grad, o).astype(BF).reshape(half, heads, HEAD_DIM)
        value_grad = jnp.einsum(
            "hqk,qhe->khe", probs.astype(BF), att_grad, preferred_element_type=F32
        ).astype(BF)
        probs_grad = jnp.einsum("qhe,khe->hqk", att_grad, value, preferred_element_type=F32)
        scores_grad = probs * (probs_grad - jnp.sum(probs * probs_grad, axis=-1, keepdims=True))
        low = scores_grad.astype(BF)
        query_grad = jnp.einsum("hqk,khe->qhe", low, key, preferred_element_type=F32) * factor
        key_grad = jnp.einsum("hqk,qhe->khe", low, query, preferred_element_type=F32) * factor
        stack = jnp.stack([query_grad.astype(BF), key_grad.astype(BF), value_grad], axis=2)
        stacked.append(stack.reshape(half, heads * 3 * HEAD_DIM))
        part4 = part4 + dot_trans(stacked[-1], w)
    part4 = part4.astype(BF)
    part4_other = swap(part4, "tensor", 1)

    out_grad = scatter(dot_rows(both(branch1_grad), mine(attended)))
    stacked_mine = mine(stacked)
    qkv_grad = scatter(dot_rows(both(normed1), stacked_mine))
    stack_sum = jnp.sum(stacked_mine.astype(F32), axis=0).reshape(heads, 3, HEAD_DIM)
    qv_grad = jnp.stack([stack_sum[:, 0], stack_sum[:, 2]], axis=1).reshape(1, -1)

    branch2 = part2.astype(F32) + part2_other.astype(F32) + fc2_bias.astype(F32)
    gate2_part = jnp.sum(final_grad * branch2, axis=0)
    result = jnp.where(keep, mid + mods[5:6] * branch2, inputs).astype(BF)

    def whole_rows(value):
        other = swap(value, "tensor", 0)
        return jnp.where(
            core == 0,
            jnp.concatenate([value, other], axis=0),
            jnp.concatenate([other, value], axis=0),
        ).reshape(tokens.shape)

    result = whole_rows(result)

    normed1_grad = part4.astype(F32) + part4_other.astype(F32)
    input_ln_grad, shift1_part, scale1_part = layer_norm_back(
        normed1_grad, mods[1:2], norm1, inv1
    )
    tokens_grad = (mid_grad + input_ln_grad + jnp.where(keep, 0.0, upstream)).astype(BF)
    tokens_grad = whole_rows(tokens_grad)

    sums = jnp.stack(
        [
            shift1_part,
            scale1_part,
            gate1_part,
            shift2_part,
            scale2_part,
            gate2_part,
            fc2_part,
            proj_part,
        ]
    )
    sums = sums + swap(sums, "tensor", 0)
    mod_grad = sums[:6].astype(BF).astype(F32).reshape(1, 6 * width)
    mod_cols = lax.dynamic_slice_in_dim(mod_grad, t_rank * ada_cols, ada_cols, 1)
    totals = jnp.concatenate([sums[6:].reshape(1, -1), fc1_grad, qv_grad], axis=1)
    for bit in range((n_dp - 1).bit_length()):
        other = swap(jnp.concatenate([totals, mod_cols.reshape(1, -1)], axis=1), "dp", bit)
        totals = totals + other[:, : totals.shape[1]]
        other = other[:, totals.shape[1] :].reshape(mod_cols.shape)
        mod_cols = jnp.where(
            ((d_rank >> bit) & 1) == 0,
            jnp.concatenate([mod_cols, other], axis=0),
            jnp.concatenate([other, mod_cols], axis=0),
        )
    ada_bias_grad = jnp.sum(mod_cols, axis=0)
    mod_low = mod_cols.astype(BF)
    cond_rows, labels_all = known[:, :width], known[:, width]
    act_rows = lax.dynamic_slice_in_dim(
        jax.nn.silu(cond_rows), d_rank * (width // n_dp), width // n_dp, 1
    ).astype(BF)
    ada_grad = dot_rows(act_rows, mod_low)
    cond_part = dot_trans(mod_low, ada_weight)
    for bit in (1, 0):
        my_bit = (t_rank >> bit) & 1
        two = cond_part.reshape(n_dp, 2, -1)
        stay = lax.dynamic_index_in_dim(two, my_bit, 1, keepdims=False)
        send = lax.dynamic_index_in_dim(two, 1 - my_bit, 1, keepdims=False)
        cond_part = stay + swap(send, "tensor", bit)
    cond_cols = lax.dynamic_slice_in_dim(cond_rows, t_rank * columns, columns, 1)
    gate = jax.nn.sigmoid(cond_cols)
    cond_grad = cond_part * gate * (1.0 + cond_cols * (1.0 - gate))
    classes = jnp.arange(class_table.shape[0], dtype=F32)
    onehot = (labels_all[:, None] == classes[None, :]).astype(F32)
    table_grad = lax.dot_general(
        onehot,
        cond_grad,
        (((0,), (0,)), ((), ())),
        precision=lax.Precision.HIGHEST,
        preferred_element_type=F32,
    )
    ends = [width, 2 * width, 2 * width + fc1_grad.shape[1]]
    fc2_grad, proj_grad, fc1_grad, qv_grad = jnp.split(totals[0], ends)
    return (
        result,
        tokens_grad,
        qkv_grad,
        out_grad,
        up_grad,
        down_grad,
        ada_grad,
        table_grad,
        qv_grad,
        proj_grad,
        fc1_grad,
        fc2_grad,
        ada_bias_grad,
    )


def solution(mesh):
    placed = (
        P("dp", None, None, None),
        P("dp"),
        P("dp"),
        P("dp"),
        P(None, "tensor"),
        P(None, "tensor"),
        P("tensor"),
        P(None, "tensor"),
        P("tensor"),
        P(None, "tensor"),
        P(),
        P(None, "tensor"),
        P("tensor"),
        P(None, "tensor"),
        P(),
        P("dp", None, None, None),
    )
    return jax.shard_map(
        shards,
        mesh=mesh,
        in_specs=placed,
        out_specs=(
            P("dp", None, None, None),
            P("dp", None, None, None),
            P("dp", "tensor"),
            P("dp", "tensor"),
            P("dp", "tensor"),
            P("dp", "tensor"),
            P("dp", "tensor"),
            P(None, "tensor"),
            P("tensor"),
            P(),
            P("tensor"),
            P(),
            P("tensor"),
        ),
        check_vma=False,
    )
```

```python
import math

import jax
import jax.numpy as jnp
from jax import lax
from jax.experimental import pallas as pl
from jax.experimental.pallas import tpu as pltpu
from jax.sharding import PartitionSpec as P

HEAD_DIM = 72
BF = jnp.bfloat16
F32 = jnp.float32


def dot(left, right):
    return jnp.dot(left, right, preferred_element_type=F32)


def dot_trans(left, right):
    return lax.dot_general(left, right, (((1,), (1,)), ((), ())), preferred_element_type=F32)


def dot_rows(left, right):
    return lax.dot_general(left, right, (((0,), (0,)), ((), ())), preferred_element_type=F32)


def swap(value, axis, flip):
    size = lax.axis_size(axis)
    return lax.ppermute(value, axis, [(i, i ^ flip) for i in range(size)])


def call(body, name, us, outs, args, scratch=(), limit=24, after=(), anywhere=()):
    specs = [
        pl.BlockSpec(
            memory_space=pltpu.SMEM
            if a.dtype == jnp.int32
            else (pl.ANY if i in anywhere else pltpu.VMEM)
        )
        for i, a in enumerate(args)
    ]
    specs += [pl.BlockSpec(memory_space=pl.ANY)] * len(after)
    n_args, n_after = len(args), len(after)
    return pl.pallas_call(
        lambda *refs: body(*refs[:n_args], *refs[n_args + n_after :]),
        out_shape=[jax.ShapeDtypeStruct(s, d) for s, d in outs],
        in_specs=specs,
        out_specs=[pl.BlockSpec(memory_space=pltpu.VMEM)] * len(outs),
        scratch_shapes=list(scratch),
        compiler_params=pltpu.CompilerParams(vmem_limit_bytes=limit << 20),
        cost_estimate=pl.CostEstimate(
            flops=int(us * 1.1e7), bytes_accessed=1024, transcendentals=0
        ),
        name=name,
    )(*args, *after)


def behind(value, *others):
    return lax.optimization_barrier((value, *others))[0]


def pad_lanes(width):
    return -(-width // 128) * 128


def standardize(value):
    center = value - jnp.mean(value, axis=-1, keepdims=True)
    spread = jnp.mean(center * center, axis=-1, keepdims=True)
    inv = lax.rsqrt(spread + 1e-06)
    return center * inv, inv


def standardize_back(grad, scale, normed, inv):
    g = grad * (1.0 + scale)
    return (
        g
        - jnp.mean(g, axis=-1, keepdims=True)
        - normed * jnp.mean(g * normed, axis=-1, keepdims=True)
    ) * inv


def gelu_pair(value):
    k = math.sqrt(2.0 / math.pi)
    square = value * value
    t = jnp.tanh(k * (value + 0.044715 * value * square))
    act = 0.5 * value * (1.0 + t)
    slope = 0.5 * (1.0 + t) + 0.5 * value * (1.0 - t * t) * k * (1.0 + 3 * 0.044715 * square)
    return act, slope


def column_sum(value):
    return jnp.sum(value, axis=0, keepdims=True)


def my_rows(ref):
    half = ref.shape[0] // 2
    start = pl.multiple_of((lax.axis_index("tensor") & 1) * half, half)
    return ref[pl.ds(start, half), :].astype(F32)


def kept_rows(length_ref, half, frames):
    frame = lax.broadcasted_iota(jnp.int32, (half, 1), 0) % frames
    return frame < length_ref[0]


def split_chunks(value, n_dp, bit):
    r = value.shape[1] // n_dp
    low, high = (
        jnp.concatenate(
            [value[:, i * r : i * r + r] for i in range(n_dp) if (i >> bit) & 1 == side], axis=1
        )
        for side in range(2)
    )
    mine_low = ((lax.axis_index("dp") >> bit) & 1) == 0
    return jnp.where(mine_low, low, high), jnp.where(mine_low, high, low)


def start_kernel(tokens, weight, normed, inv, weight_out, sem):
    copy = pltpu.make_async_copy(weight, weight_out, sem)
    copy.start()
    normed[...], inv[...] = standardize(my_rows(tokens))
    copy.wait()


def modulation_kernel(e0, e1, e2, e3, clock, weight, bias, cond_out, part, rows):
    rank = lax.axis_index("tensor")
    for flip, piece in enumerate((e0, e1, e2, e3)):
        rows[pl.ds(rank ^ flip, 1), :] = piece[...].astype(F32)
    cond = clock[...] + jnp.concatenate([rows[i : i + 1, :] for i in range(4)], axis=1)
    cond_out[...] = cond
    act = (cond / (1.0 + jnp.exp(-cond))).astype(BF)
    act = jnp.broadcast_to(act, (16, act.shape[1]))
    part[...] = dot_trans(act, weight[...])[0:1, :] + bias[...].astype(F32)


def attention_kernel(
    frames, length, normed, m0, m1, m2, m3, qkv_a, qkv_b, bias_a, bias_b, out_a, out_b,
    part, mods, normed_low, saved_a, saved_b, probs_out, att_a, att_b, rows,
):
    rank = lax.axis_index("tensor")
    width = normed.shape[1]
    for flip, piece in enumerate((m0, m1, m2, m3)):
        rows[pl.ds(rank ^ flip, 1), :] = piece[...]
    cols = rows.shape[1]
    extra = cols - width
    for side in range(2):
        a, b = rows[2 * side : 2 * side + 1, :], rows[2 * side + 1 : 2 * side + 2, :]
        mods[3 * side : 3 * side + 1, :] = a[:, :width]
        mods[3 * side + 1 : 3 * side + 2, :] = jnp.concatenate([a[:, width:], b[:, :extra]], axis=1)
        mods[3 * side + 2 : 3 * side + 3, :] = b[:, extra:]
    mods[6:8, :] = jnp.zeros((2, width), F32)
    low = (normed[...] * (1.0 + mods[1:2, :]) + mods[0:1, :]).astype(BF)
    normed_low[...] = low
    half = low.shape[0]
    row_id = lax.broadcasted_iota(jnp.int32, (half, half), 0)
    col_id = lax.broadcasted_iota(jnp.int32, (half, half), 1)
    seen = ((row_id // frames) == (col_id // frames)) & ((col_id % frames) < length[0])
    factor = HEAD_DIM ** (-0.5)
    heads = out_a.shape[0] // HEAD_DIM
    total = None
    blocks = ((qkv_a, bias_a, out_a, saved_a, att_a), (qkv_b, bias_b, out_b, saved_b, att_b))
    for block, (w, b, o, saved, att_ref) in enumerate(blocks):
        qkv = dot_trans(low, w[...]) + b[...].astype(F32)
        saved[...] = qkv.astype(BF)
        for h in range(heads):
            base = h * 3 * HEAD_DIM
            q, k, v = (
                qkv[:, base + j * HEAD_DIM : base + (j + 1) * HEAD_DIM].astype(BF)
                for j in range(3)
            )
            scores = jnp.where(seen, dot_trans(q, k) * factor, -1e30)
            raised = jnp.exp(scores - jnp.max(scores, axis=-1, keepdims=True))
            probs = raised / jnp.sum(raised, axis=-1, keepdims=True)
            probs_out[block * heads + h] = probs
            att_ref[:, h * HEAD_DIM : (h + 1) * HEAD_DIM] = dot(probs.astype(BF), v).astype(BF)
        term = dot(att_ref[...], o[...])
        total = term if total is None else total + term
    part[...] = total.astype(BF)


def early_back_kernel(
    frames, n_dp, length, mods, cotangent, down_a, down_b, normed_low, att_a, att_b,
    grad_a, grad_b, pack_far, pack_core, chunks_far, chunks_core, fc2_sum,
):
    upstream = my_rows(cotangent)
    half, width = upstream.shape
    keep = kept_rows(length, half, frames)
    low32 = (mods[5:6, :] * jnp.where(keep, upstream, 0.0)).astype(BF).astype(F32)
    low = low32.astype(BF)
    grad_a[...] = dot(low, down_a[...])
    grad_b[...] = dot(low, down_b[...])
    fc2_sum[...] = column_sum(low32)
    n_att = att_a.shape[1]
    part = width // 2
    mine, other = split_chunks(normed_low[...].astype(F32), n_dp, 0)
    pack_far[:, 0:n_att] = att_a[...]
    pack_far[:, n_att : 2 * n_att] = att_b[...]
    at = pad_lanes(2 * n_att)
    pack_far[:, at : at + part] = other.astype(BF)
    pack_core[:, 0:n_att] = att_b[...]
    at = pad_lanes(n_att)
    pack_core[:, at : at + part] = mine.astype(BF)
    mine, other = split_chunks(low32, n_dp, 2)
    chunks_far[:, 0:part] = other.astype(BF)
    chunks_core[:, 0:part] = mine.astype(BF)


def mlp_kernel(
    n_dp, tokens, part1, part1_other, proj_bias, mods, up_a, up_b, fc1_a, fc1_b, grad_a, grad_b,
    chunks_far, part3, pack_act, pack_pre, chunks_core, branch_out, normed_out, inv_out,
):
    branch = part1[...].astype(F32) + part1_other[...].astype(F32) + proj_bias[...].astype(F32)
    branch_out[...] = branch
    mid = my_rows(tokens) + mods[2:3, :] * branch
    normed, inv = standardize(mid)
    normed_out[...] = normed
    inv_out[...] = inv
    low32 = normed * (1.0 + mods[4:5, :]) + mods[3:4, :]
    low = low32.astype(BF)
    total = None
    cols = up_a.shape[1]
    for block, (u, b, g) in enumerate(((up_a, fc1_a, grad_a), (up_b, fc1_b, grad_b))):
        act, slope = gelu_pair(dot(low, u[...]) + b[...].astype(F32))
        pack_act[:, block * cols : (block + 1) * cols] = act.astype(BF)
        pre = (g[...] * slope).astype(BF)
        pack_pre[:, block * cols : (block + 1) * cols] = pre
        term = dot_trans(pre, u[...])
        total = term if total is None else total + term
    part3[...] = total.astype(BF)
    mine, other = split_chunks(low32, n_dp, 0)
    part = mine.shape[1]
    pack_pre[:, 2 * cols : 2 * cols + part] = other.astype(BF)
    chunks_core[:, 0:part] = mine.astype(BF)
    pack_act[:, 2 * cols :] = chunks_far[...]


def mlp_tail_kernel(
    pack_act, pack_pre, down_a, down_b, chunks_act, chunks_pre, part2, core_act, core_pre, sums
):
    cols = down_a.shape[1]
    part2[...] = (
        dot_trans(pack_act[:, 0:cols], down_a[...]) + dot_trans(pack_act[:, cols : 2 * cols], down_b[...])
    ).astype(BF)
    core_act[:, 0:cols] = pack_act[:, cols : 2 * cols]
    core_act[:, cols:] = chunks_act[...]
    core_pre[:, 0:cols] = pack_pre[:, cols : 2 * cols]
    core_pre[:, cols:] = chunks_pre[...]
    sums[0:1, :] = column_sum(pack_pre[:, 0:cols].astype(F32))
    sums[1:2, :] = column_sum(pack_pre[:, cols : 2 * cols].astype(F32))


def attention_back_kernel(
    frames, length, part3, part3_other, mods, normed, inv, branch, cotangent,
    out_a, out_b, qkv_a, qkv_b, saved_a, saved_b, probs_in,
    part4, mid_grad_out, low_out, stacked, sums,
):
    upstream = my_rows(cotangent)
    half, width = upstream.shape
    keep = kept_rows(length, half, frames)
    grad = part3[...].astype(F32) + part3_other[...].astype(F32)
    norm = normed[...]
    mid_grad = jnp.where(keep, upstream, 0.0) + standardize_back(grad, mods[4:5, :], norm, inv[...])
    mid_grad_out[...] = mid_grad
    low = (mods[2:3, :] * mid_grad).astype(BF)
    low_out[...] = low
    sums[0:1, :] = column_sum(grad)
    sums[1:2, :] = column_sum(grad * norm)
    sums[2:3, :] = column_sum(mid_grad * branch[...])
    sums[3:4, :] = column_sum(low.astype(F32))
    factor = HEAD_DIM ** (-0.5)
    heads = out_a.shape[0] // HEAD_DIM
    cols = heads * 3 * HEAD_DIM
    wide = pad_lanes(cols)
    total = None
    for block, (w, o, saved) in enumerate(((qkv_a, out_a, saved_a), (qkv_b, out_b, saved_b))):
        att_grad = dot_trans(low, o[...])
        qkv = saved[...].astype(F32)
        for h in range(heads):
            base = h * 3 * HEAD_DIM
            q, k, v = (
                qkv[:, base + j * HEAD_DIM : base + (j + 1) * HEAD_DIM].astype(BF)
                for j in range(3)
            )
            ag = att_grad[:, h * HEAD_DIM : (h + 1) * HEAD_DIM].astype(BF)
            probs = probs_in[block * heads + h]
            value_grad = dot_rows(probs.astype(BF), ag)
            probs_grad = dot_trans(ag, v)
            inner = jnp.sum(probs * probs_grad, axis=-1, keepdims=True)
            scores_low = (probs * (probs_grad - inner)).astype(BF)
            query_grad = dot(scores_low, k) * factor
            key_grad = dot_rows(scores_low, q) * factor
            at = block * wide + base
            for j, piece in enumerate((query_grad, key_grad, value_grad)):
                stacked[:, at + j * HEAD_DIM : at + (j + 1) * HEAD_DIM] = piece.astype(BF)
        mine = stacked[:, block * wide : block * wide + cols]
        sums[4 + block : 5 + block, 0:cols] = column_sum(mine.astype(F32))
        term = dot(mine, w[...])
        total = term if total is None else total + term
    part4[...] = total.astype(BF)


def pack_back_kernel(n_dp, low, stacked, pack_far, pack_core):
    mine, other = split_chunks(low[...].astype(F32), n_dp, 0)
    part, cols = mine.shape[1], stacked.shape[1]
    pack_far[:, 0:cols] = stacked[...]
    pack_far[:, cols : cols + part] = other.astype(BF)
    pack_core[:, 0 : cols // 2] = stacked[:, cols // 2 :]
    pack_core[:, cols // 2 : cols // 2 + part] = mine.astype(BF)


def output_kernel(
    frames, length, tokens, part2, part2_other, fc2_bias, mods, branch1, cotangent, result, gate_sum
):
    inputs, upstream = my_rows(tokens), my_rows(cotangent)
    keep = kept_rows(length, inputs.shape[0], frames)
    branch = part2[...].astype(F32) + part2_other[...].astype(F32) + fc2_bias[...].astype(F32)
    mid = inputs + mods[2:3, :] * branch1[...]
    result[...] = jnp.where(keep, mid + mods[5:6, :] * branch, inputs).astype(BF)
    gate_sum[...] = column_sum(jnp.where(keep, upstream, 0.0) * branch)


def input_back_kernel(
    frames, length, part4, part4_other, mods, normed, inv, mid_grad, cotangent,
    back_sums, gate2_sum, fc2_sum, pre_sums, tokens_grad, sums,
):
    upstream = my_rows(cotangent)
    keep = kept_rows(length, upstream.shape[0], frames)
    grad = part4[...].astype(F32) + part4_other[...].astype(F32)
    norm = normed[...]
    back = standardize_back(grad, mods[1:2, :], norm, inv[...])
    tokens_grad[...] = (mid_grad[...] + back + jnp.where(keep, 0.0, upstream)).astype(BF)
    sums[0:1, :] = column_sum(grad)
    sums[1:2, :] = column_sum(grad * norm)
    sums[2:3, :] = back_sums[2:3, :]
    sums[3:5, :] = back_sums[0:2, :]
    sums[5:6, :] = gate2_sum[...]
    sums[6:7, :] = fc2_sum[...]
    sums[7:8, :] = back_sums[3:4, :]
    sums[8:10, :] = pre_sums[0:2, :]
    sums[10:12, :] = back_sums[4:6, :]
    sums[12:16, :] = jnp.zeros((4, sums.shape[1]), F32)


def vector_kernel(layout, label, mine, other, cond, vector):
    rank = lax.axis_index("tensor")
    width = mine.shape[1]
    both = mine[...] + other[...]
    upper = rank >= 2
    pick = lambda i: jnp.where(upper, both[3 + i : 4 + i, :], both[i : i + 1, :])
    cols = layout["mod"][1]
    extra = cols - width
    shift, scale, gate = pick(0), pick(1), pick(2)
    even = jnp.concatenate([shift, scale[:, :extra]], axis=1)
    odd = jnp.concatenate([scale[:, extra:], gate], axis=1)
    vector[...] = jnp.zeros(vector.shape, F32)

    def put(name, value):
        at, size = layout[name]
        vector[:, at : at + size] = value

    put("mod", jnp.where((rank & 1) == 0, even, odd).astype(BF).astype(F32))
    put("fc2", both[6:7, :])
    put("proj", both[7:8, :])
    put("fc1", (mine[8:9, :] + other[9:10, :])[:, : layout["fc1"][1]])
    put("stack", (mine[10:11, :] + other[11:12, :])[:, : layout["stack"][1]])
    put("cond", cond[...])
    put("label", jnp.full((1, 128), label[0], jnp.int32).astype(F32))


def gathered_kernel(layout, n_dp, rows_out, blocks, weight, *refs):
    sources, refs = refs[:blocks], refs[blocks:]
    ada_grad, totals, c0, c1, c23, cond_cols, labels, table = refs
    rank, place = lax.axis_index("tensor"), lax.axis_index("dp")
    slot = 0
    for source in sources:
        for i in range(source.shape[0]):
            table[pl.ds(place ^ slot, 1), :] = source[i : i + 1, :]
            slot += 1

    def get(name):
        at, size = layout[name]
        return table[:, at : at + size]

    totals[...] = column_sum(table[...])
    mod = get("mod").astype(BF)
    cond = get("cond")
    act = cond / (1.0 + jnp.exp(-cond))
    width = act.shape[1]
    mine = pltpu.roll(act, (width - place * rows_out) % width, 1)[:, :rows_out].astype(BF)
    ada_grad[...] = dot_rows(mine, mod)
    columns = c0.shape[1]
    cond_part = dot(mod, weight[...])
    wide = pad_lanes(columns)
    outs = (c0, c1, c23.at[:, 0:columns], c23.at[:, wide : wide + columns])
    for flip, out in enumerate(outs):
        out[...] = pltpu.roll(cond_part, (width - (rank ^ flip) * columns) % width, 1)[:, :columns]
    cond_cols[...] = pltpu.roll(cond, (width - rank * columns) % width, 1)[:, :columns]
    labels[...] = get("label")


def table_kernel(c0, c1, c2, c3, cond_cols, labels, out):
    cond = cond_cols[...]
    columns = cond.shape[1]
    wide = pad_lanes(columns)
    gate = 1.0 / (1.0 + jnp.exp(-cond))
    grad = c0[...] + c1[...] + c2[:, :columns] + c3[:, wide : wide + columns]
    grad = grad * gate * (1.0 + cond * (1.0 - gate))
    classes = lax.broadcasted_iota(jnp.int32, (cond.shape[0], out.shape[1]), 1).astype(F32)
    onehot = jnp.where(labels[:, : out.shape[1]] == classes, 1.0, 0.0)
    out[...] = lax.dot_general(
        grad,
        onehot,
        (((0,), (0,)), ((), ())),
        precision=lax.Precision.HIGHEST,
        preferred_element_type=F32,
    )


def forward_kernel(spans, *refs):
    for (at, size, chunks), source, out in zip(spans, refs[: len(spans)], refs[len(spans) :]):
        out[:, 0:size] = source[:, at : at + size]
        out[:, size:] = source[:, chunks : chunks + out.shape[1] - size]


def weight_kernel(n_dp, split_bit, products, *refs):
    n_sets = 1 + max(max(p[0][0], p[1][0]) for p in products)
    sets = [refs[5 * i : 5 * i + 5] for i in range(n_sets)]
    outs, lefts = refs[5 * n_sets : -len(products)], refs[-len(products) :]
    half = sets[0][0].shape[0]
    part = lefts[0].shape[0]
    r = part // (n_dp // 2)
    at = 0
    for left, product in zip(lefts, products):
        (l_set, l_far, l_core), (r_set, r_far, r_core), cols = product
        own, core, core_in, far, far_core = sets[l_set]
        rows = (
            core[:, l_core : l_core + part],
            core_in[:, l_core : l_core + part],
            far[:, l_far : l_far + part],
            far_core[:, l_core : l_core + part],
        )
        for i, value in enumerate(rows):
            left[:, i * half : (i + 1) * half] = value.astype(F32).T.astype(BF)
        own, core, core_in, far, far_core = sets[r_set]
        right = jnp.concatenate(
            [
                own[:, r_far : r_far + cols],
                core_in[:, r_core : r_core + cols],
                far[:, r_far : r_far + cols],
                far_core[:, r_core : r_core + cols],
            ],
            axis=0,
        )
        if split_bit is None:
            outs[0][:, at : at + cols] = dot(left[...], right)
        else:
            stay, send = outs
            mine = (lax.axis_index("dp") >> split_bit) & 1
            for k in range(n_dp // 4):
                for out, side in ((stay, mine), (send, 1 - mine)):
                    start = pl.multiple_of((2 * k + side) * r, r)
                    out[k, :, at : at + cols] = dot(left[pl.ds(start, r), :], right).astype(out.dtype)
        at += cols


def halve_kernel(bit, stay, other, out_stay, out_send):
    mine = (lax.axis_index("dp") >> bit) & 1
    out_stay[...] = stay[mine] + other[mine].astype(F32)
    out_send[...] = (stay[1 - mine] + other[1 - mine].astype(F32)).astype(BF)


def add_kernel(widths, stay, other, *outs):
    total = stay[...] + other[...].astype(F32)
    at = 0
    for out, cols in zip(outs, widths):
        out[...] = total[:, at : at + cols]
        at += cols


def join_kernel(mine, other, mine2, other2, out, out2):
    half = mine.shape[0]
    core = lax.axis_index("tensor") & 1
    for part, side in (((mine, mine2), core), ((other, other2), 1 - core)):
        for source, target in zip(part, (out, out2)):
            target[pl.ds(pl.multiple_of(side * half, half), half), :] = source[...]


def shards(
    tokens,
    lengths,
    timesteps,
    labels,
    class_table,
    ada_weight,
    ada_bias,
    qkv_weight,
    qv_bias,
    out_weight,
    proj_bias,
    up_weight,
    fc1_bias,
    down_weight,
    fc2_bias,
    cotangent,
):
    clips, patches, frames, width = tokens.shape
    assert clips == 1 and lax.axis_size("tensor") == 4
    rows = patches * frames
    half = rows // 2
    n_att = out_weight.shape[1]
    heads = n_att // HEAD_DIM
    n_qkv = qkv_weight.shape[1]
    hidden = up_weight.shape[1]
    columns = class_table.shape[1]
    ada_cols = ada_weight.shape[1]
    n_classes = class_table.shape[0]
    t_rank = lax.axis_index("tensor")
    d_rank = lax.axis_index("dp")
    n_dp = lax.axis_size("dp")
    chunk = width // n_dp
    part = width // 2
    wide = pad_lanes(part)

    tokens2 = tokens.reshape(rows, width)
    cot2 = cotangent.reshape(rows, width)
    proj_row = proj_bias.reshape(1, width)
    fc2_row = fc2_bias.reshape(1, width)

    def gather_tensor(own, *others):
        across = behind(swap(own, "tensor", 2), *others)
        return [own, swap(own, "tensor", 1), across, swap(across, "tensor", 1)]

    picked = lax.dynamic_slice_in_dim(class_table, labels[0], 1, 0)
    pieces = gather_tensor(picked)
    normed1, inv1, ada_rows = call(
        start_kernel,
        "start",
        1.0,
        [((half, width), F32), ((half, 1), F32), ((ada_cols, width), BF)],
        [tokens2, ada_weight.T],
        [pltpu.SemaphoreType.DMA],
        anywhere=(1,),
    )

    def pair(weight, *others):
        return weight, swap(behind(weight, *others), "tensor", 1)

    two = qv_bias.reshape(heads, 2, HEAD_DIM)
    bias_row = jnp.stack([two[:, 0], jnp.zeros_like(two[:, 0]), two[:, 1]], axis=1)
    qkv_ws = pair(qkv_weight.T, pieces[3])
    bias_ws = pair(bias_row.reshape(1, n_qkv))
    fc1_ws = pair(fc1_bias.reshape(1, hidden))
    out_ws = pair(out_weight.T, pieces[3])

    half_width = width // 2
    freqs = jnp.exp(-math.log(10000.0) * jnp.arange(half_width, dtype=F32) / half_width)
    angles = timesteps.astype(F32)[:, None] * freqs[None, :]
    clock = jnp.concatenate([jnp.cos(angles), jnp.sin(angles)], axis=1)
    cond, mod_part = call(
        modulation_kernel,
        "modulation",
        1.0,
        [((1, width), F32), ((1, ada_cols), F32)],
        [*pieces, clock, ada_rows, ada_bias.reshape(1, ada_cols)],
        [pltpu.VMEM((8, columns), F32)],
    )
    mod_pieces = gather_tensor(mod_part, qkv_ws[1], out_ws[1], bias_ws[1], fc1_ws[1])
    up_ws = pair(up_weight, *mod_pieces)
    down_ws = pair(down_weight, *mod_pieces)

    part1, mods, low1, saved_a, saved_b, probs, att_a, att_b = call(
        lambda *refs: attention_kernel(frames, *refs),
        "attention",
        4.0,
        [
            ((half, width), BF),
            ((8, width), F32),
            ((half, width), BF),
            ((half, n_qkv), BF),
            ((half, n_qkv), BF),
            ((2 * heads, half, half), F32),
            ((half, n_att), BF),
            ((half, n_att), BF),
        ],
        [lengths, normed1, *mod_pieces, *qkv_ws, *bias_ws, *out_ws],
        [pltpu.VMEM((8, ada_cols), F32)],
    )
    part1_other = swap(part1, "tensor", 2)

    att_far, att_core = pad_lanes(2 * n_att), pad_lanes(n_att)
    grad_a, grad_b, *pack1, chunks_far, chunks_act, fc2_sum = call(
        lambda *refs: early_back_kernel(frames, n_dp, *refs),
        "early_back",
        2.0,
        [
            ((half, hidden), F32),
            ((half, hidden), F32),
            ((half, att_far + wide), BF),
            ((half, att_core + wide), BF),
            ((half, wide), BF),
            ((half, wide), BF),
            ((1, width), F32),
        ],
        [lengths, mods, cot2, *down_ws, low1, att_a, att_b],
    )

    part3, pack_act, pack_pre, chunks_pre, branch1, normed2, inv2 = call(
        lambda *refs: mlp_kernel(n_dp, *refs),
        "mlp",
        3.0,
        [
            ((half, width), BF),
            ((half, 2 * hidden + wide), BF),
            ((half, 2 * hidden + wide), BF),
            ((half, wide), BF),
            ((half, width), F32),
            ((half, width), F32),
            ((half, 1), F32),
        ],
        [
            tokens2, part1, part1_other, proj_row, mods, *up_ws, *fc1_ws, grad_a, grad_b,
            chunks_far,
        ],
    )
    part3_other = swap(part3, "tensor", 2)

    part2, core_act, core_pre, pre_sums = call(
        mlp_tail_kernel,
        "mlp_tail",
        2.0,
        [
            ((half, width), BF),
            ((half, hidden + wide), BF),
            ((half, hidden + wide), BF),
            ((2, hidden), F32),
        ],
        [pack_act, pack_pre, *down_ws, chunks_act, chunks_pre],
    )
    part2_other = swap(part2, "tensor", 2)

    def cross(pack, bit):
        own, core = pack
        return [own, core, swap(core, "tensor", 1), swap(own, "dp", 1 << bit)]

    def forward(name, sets, spans, after):
        outs = call(
            lambda *refs: forward_kernel(spans, *refs),
            name,
            0.5,
            [((half, at_size + wide), BF) for _, at_size, _ in spans],
            [s[3] for s in sets],
            after=after,
        )
        for one, out in zip(sets, outs):
            one.append(swap(out, "tensor", 1))
        return outs

    set1 = cross(pack1, 0)
    set_act = cross((pack_act, core_act), 2)
    set_pre = cross((pack_pre, core_pre), 0)
    part4, mid_grad, low_back, stacked, back_sums = call(
        lambda *refs: attention_back_kernel(frames, *refs),
        "attention_back",
        5.0,
        [
            ((half, width), BF),
            ((half, width), F32),
            ((half, width), BF),
            ((half, 2 * pad_lanes(n_qkv)), BF),
            ((8, width), F32),
        ],
        [
            lengths, part3, part3_other, mods, normed2, inv2, branch1, cot2,
            *out_ws, *qkv_ws, saved_a, saved_b, probs,
        ],
    )
    part4_other = swap(part4, "tensor", 2)
    s_wide = pad_lanes(n_qkv)
    second = forward("forward1", [set1], [(n_att, pad_lanes(n_att), att_far)], [part4])
    second += forward(
        "forward2", [set_act, set_pre], [(hidden, hidden, 2 * hidden)] * 2, [part4]
    )

    result, gate2_sum = call(
        lambda *refs: output_kernel(frames, *refs),
        "output",
        1.0,
        [((half, width), BF), ((1, width), F32)],
        [lengths, tokens2, part2, part2_other, fc2_row, mods, branch1, cot2],
    )

    result_other = swap(result, "tensor", 1)

    tokens_grad, sums = call(
        lambda *refs: input_back_kernel(frames, *refs),
        "input_back",
        1.0,
        [((half, width), BF), ((16, width), F32)],
        [
            lengths, part4, part4_other, mods, normed1, inv1, mid_grad, cot2,
            back_sums, gate2_sum, fc2_sum, pre_sums,
        ],
        after=second,
    )
    sums_other = swap(sums, "tensor", 1)
    tokens_grad_other = swap(tokens_grad, "tensor", 1)

    layout, at = {}, 0
    for name, size in (
        ("mod", ada_cols), ("fc2", width), ("proj", width), ("fc1", hidden), ("stack", n_qkv),
        ("cond", width), ("label", 128),
    ):
        layout[name] = (at, size)
        at += pad_lanes(size)
    (vector,) = call(
        lambda *refs: vector_kernel(layout, *refs),
        "vector",
        0.5,
        [((1, at), F32)],
        [labels, sums, sums_other, cond],
    )
    pack3 = call(
        lambda *refs: pack_back_kernel(n_dp, *refs),
        "pack_back",
        0.5,
        [((half, 2 * s_wide + wide), BF), ((half, s_wide + wide), BF)],
        [low_back, stacked],
        after=[vector],
    )

    set3 = cross(pack3, 0)

    vector = jnp.concatenate([vector, swap(vector, "dp", 1)], axis=0)
    if n_dp == 8:
        sources = [vector] + [swap(vector, "dp", flip) for flip in (2, 4, 6)]
    else:
        flip = 2
        while flip < n_dp:
            vector = jnp.concatenate([vector, swap(vector, "dp", flip)], axis=0)
            flip *= 2
        sources = [vector]
    def first_grads(name, us, bit, products, sets, after):
        cols = sum(p[2] for p in products)
        args = [a for s in sets for a in s]
        scratch = [pltpu.VMEM((part, 4 * half), BF)] * len(products)
        if n_dp != 8:
            return call(
                lambda *refs: weight_kernel(n_dp, None, products, *refs),
                name, us, [((part, cols), F32)], args, scratch,
            ) * 2
        second = 0 if bit else 1
        assert n_dp == 8
        return call(
            lambda *refs: weight_kernel(n_dp, second, products, *refs),
            name, us, [((2, chunk, cols), F32), ((2, chunk, cols), BF)], args, scratch, after=after,
        )

    def second_grads(name, bit, stay, send, after):
        if n_dp != 8:
            return stay, send
        second = 0 if bit else 1
        return call(
            lambda *refs: halve_kernel(1 if bit == 2 else 2, *refs),
            name,
            0.5,
            [((chunk, stay.shape[2]), F32), ((chunk, stay.shape[2]), BF)],
            [stay, swap(send, "dp", 1 << second)],
            after=after,
        )

    def last_grads(name, bit, widths, stay, send, after):
        if n_dp != 8:
            grad = stay.reshape(n_dp // 2, chunk, -1)
            for b in range((n_dp - 1).bit_length()):
                if b != bit:
                    my_bit = (d_rank >> b) & 1
                    grad = grad.reshape(grad.shape[0] // 2, 2, chunk, grad.shape[2])
                    send = lax.dynamic_index_in_dim(grad, 1 - my_bit, 1, keepdims=False).astype(BF)
                    stay = lax.dynamic_index_in_dim(grad, my_bit, 1, keepdims=False)
                    grad = stay + swap(send, "dp", 1 << b).astype(F32)
            ends = [sum(widths[:i]) for i in range(1, len(widths))]
            return jnp.split(grad[0] if grad.ndim == 3 else grad, ends, axis=1)
        return call(
            lambda *refs: add_kernel(widths, *refs),
            name,
            0.5,
            [((chunk, w), F32) for w in widths],
            [stay, swap(send, "dp", 2 if bit == 2 else 4)],
            after=after,
        )

    mlp_spec = [((0, 2 * hidden, hidden), (0, 0, 0), hidden)]
    down_stay, down_send = first_grads("down_grad", 2.0, 2, mlp_spec, [set_act], sources[:1])
    up_stay, up_send = first_grads("up_grad", 2.0, 0, mlp_spec, [set_pre], sources[:1])
    ada_grad, totals, c0, c1, c23, cond_cols, labels_all = call(
        lambda *refs: gathered_kernel(layout, n_dp, chunk, len(sources), *refs),
        "gathered",
        2.0,
        [((chunk, ada_cols), F32), ((1, at), F32)]
        + [((n_dp, columns), F32)] * 2
        + [((n_dp, 2 * pad_lanes(columns)), F32), ((n_dp, columns), F32), ((n_dp, 128), F32)],
        [ada_rows, *sources],
        [pltpu.VMEM((n_dp, at), F32)],
        after=[down_stay, up_stay],
    )
    c23 = swap(c23, "tensor", 2)
    forward("forward3", [set3], [(s_wide, s_wide, 2 * s_wide)], [c1])
    qkv_stay, qkv_send = first_grads(
        "qkv_grad",
        2.0,
        0,
        [
            ((0, att_far, att_core), (1, 0, 0), n_qkv),
            ((1, 2 * s_wide, s_wide), (0, 0, 0), n_att),
        ],
        [set1, set3],
        [],
    )
    down_stay, down_send = second_grads("down_halve", 2, down_stay, down_send, [qkv_stay])
    up_stay, up_send = second_grads("up_halve", 0, up_stay, up_send, [down_stay])
    (table_grad,) = call(
        table_kernel,
        "table",
        0.5,
        [((columns, n_classes), F32)],
        [c0, swap(c1, "tensor", 1), c23, swap(c23, "tensor", 1), cond_cols, labels_all],
        after=[up_stay],
    )

    def take(name):
        start, size = layout[name]
        return totals[0, start : start + size]

    qv_grad = take("stack").reshape(heads, 3, HEAD_DIM)
    qv_grad = jnp.stack([qv_grad[:, 0], qv_grad[:, 2]], axis=1).reshape(-1)

    result, tokens_grad = call(
        join_kernel,
        "join",
        0.8,
        [((rows, width), BF)] * 2,
        [result, result_other, tokens_grad, tokens_grad_other],
        after=[up_stay],
    )
    result, tokens_grad = result.reshape(tokens.shape), tokens_grad.reshape(tokens.shape)
    qkv_stay, qkv_send = second_grads("qkv_halve", 0, qkv_stay, qkv_send, [table_grad])
    (down_grad,) = last_grads("down_add", 2, [hidden], down_stay, down_send, [qkv_stay])
    (up_grad,) = last_grads("up_add", 0, [hidden], up_stay, up_send, [down_grad])
    qkv_grad, out_grad = last_grads("qkv_add", 0, [n_qkv, n_att], qkv_stay, qkv_send, [up_grad])
    return (
        result,
        tokens_grad,
        qkv_grad,
        out_grad,
        up_grad,
        down_grad,
        ada_grad,
        table_grad.T,
        qv_grad,
        take("proj"),
        take("fc1"),
        take("fc2"),
        take("mod"),
    )


def solution(mesh):
    placed = (
        P("dp", None, None, None),
        P("dp"),
        P("dp"),
        P("dp"),
        P(None, "tensor"),
        P(None, "tensor"),
        P("tensor"),
        P(None, "tensor"),
        P("tensor"),
        P(None, "tensor"),
        P(),
        P(None, "tensor"),
        P("tensor"),
        P(None, "tensor"),
        P(),
        P("dp", None, None, None),
    )
    return jax.shard_map(
        shards,
        mesh=mesh,
        in_specs=placed,
        out_specs=(
            P("dp", None, None, None),
            P("dp", None, None, None),
            P("dp", "tensor"),
            P("dp", "tensor"),
            P("dp", "tensor"),
            P("dp", "tensor"),
            P("dp", "tensor"),
            P(None, "tensor"),
            P("tensor"),
            P(),
            P("tensor"),
            P(),
            P("tensor"),
        ),
        check_vma=False,
    )
```

```python
import math

import jax
import jax.numpy as jnp
import numpy as np
from jax import lax
from jax.experimental import pallas as pl
from jax.experimental.pallas import tpu as pltpu
from jax.sharding import PartitionSpec as P

HEAD_DIM = 72
BF = jnp.bfloat16
F32 = jnp.float32


def dot(left, right):
    return jnp.dot(left, right, preferred_element_type=F32)


def dot_trans(left, right):
    return lax.dot_general(left, right, (((1,), (1,)), ((), ())), preferred_element_type=F32)


def dot_rows(left, right):
    return lax.dot_general(left, right, (((0,), (0,)), ((), ())), preferred_element_type=F32)


def swap(value, axis, flip):
    size = lax.axis_size(axis)
    return lax.ppermute(value, axis, [(i, i ^ flip) for i in range(size)])


def call(order, body, name, us, outs, args, scratch=(), also=(), limit=24, free=False):
    specs = [
        pl.BlockSpec(
            memory_space=pltpu.SMEM if a.dtype == jnp.int32 else pltpu.VMEM
        )
        for a in args
    ]
    marks = [*(order[:1] if free else order), *also]
    specs += [pl.BlockSpec(memory_space=pl.ANY)] * len(marks)
    n_args, n_outs = len(args), len(outs)
    first_out = n_args + len(marks)

    def whole(*refs):
        body(*refs[:n_args], *refs[first_out : first_out + n_outs], *refs[first_out + n_outs + 1 :])
        refs[first_out + n_outs][...] = jnp.zeros((8, 128), F32)

    *results, mark = pl.pallas_call(
        whole,
        out_shape=[jax.ShapeDtypeStruct(s, d) for s, d in [*outs, ((8, 128), F32)]],
        in_specs=specs,
        out_specs=[pl.BlockSpec(memory_space=pltpu.VMEM)] * (n_outs + 1),
        scratch_shapes=list(scratch),
        compiler_params=pltpu.CompilerParams(vmem_limit_bytes=limit << 20),
        cost_estimate=pl.CostEstimate(
            flops=int(us * 1.1e9), bytes_accessed=1024, transcendentals=0
        ),
        name=name,
    )(*args, *marks)
    if not free:
        order.clear()
    order.append(mark)
    return results


def behind(value, *others):
    return lax.optimization_barrier((value, *others))[0]


def pad_lanes(width):
    return -(-width // 128) * 128


def standardize(value):
    center = value - jnp.mean(value, axis=-1, keepdims=True)
    spread = jnp.mean(center * center, axis=-1, keepdims=True)
    inv = lax.rsqrt(spread + 1e-06)
    return center * inv, inv


def standardize_back(grad, scale, normed, inv):
    g = grad * (1.0 + scale)
    return (
        g
        - jnp.mean(g, axis=-1, keepdims=True)
        - normed * jnp.mean(g * normed, axis=-1, keepdims=True)
    ) * inv


def gelu_pair(value):
    k = math.sqrt(2.0 / math.pi)
    square = value * value
    t = jnp.tanh(k * (value + 0.044715 * value * square))
    act = 0.5 * value * (1.0 + t)
    slope = 0.5 * (1.0 + t) + 0.5 * value * (1.0 - t * t) * k * (1.0 + 3 * 0.044715 * square)
    return act, slope


def row_part(ref, spots, name):
    at, size = spots[name]
    return ref[:, at : at + size].astype(F32)


def column_sum(value):
    return jnp.sum(value, axis=0, keepdims=True)


def kept_rows(length_ref, half, frames):
    frame = lax.broadcasted_iota(jnp.int32, (half, 1), 0) % frames
    return frame < length_ref[0]


def split_chunks(value, n_dp, bit):
    r = value.shape[1] // n_dp
    low, high = (
        jnp.concatenate(
            [value[:, i * r : i * r + r] for i in range(n_dp) if (i >> bit) & 1 == side], axis=1
        )
        for side in range(2)
    )
    mine_low = ((lax.axis_index("dp") >> bit) & 1) == 0
    return jnp.where(mine_low, low, high), jnp.where(mine_low, high, low)


def clock_kernel(spots, times, row, clock):
    freqs = row_part(row, spots, "freqs")
    angles = jnp.full(freqs.shape, times[0], jnp.int32).astype(F32) * freqs
    clock[...] = jnp.concatenate([jnp.cos(angles), jnp.sin(angles)], axis=1)


def start_kernel(tokens, cotangent, normed, inv, tok_half, cot_half):
    half = tok_half.shape[0]
    rows = pl.ds(pl.multiple_of((lax.axis_index("tensor") & 1) * half, half), half)
    tok_half[...] = tokens[rows, :]
    cot_half[...] = cotangent[rows, :]
    normed[...], inv[...] = standardize(tok_half[...].astype(F32))


def modulation_kernel(spots, e0, e1, e2, e3, clock, weight, bias, cond_out, part, rows):
    rank = lax.axis_index("tensor")
    for flip, piece in enumerate((e0, e1, e2, e3)):
        rows[pl.ds(rank ^ flip, 1), :] = piece[...].astype(F32)
    cond = clock[...] + jnp.concatenate([rows[i : i + 1, :] for i in range(4)], axis=1)
    cond_out[...] = cond
    act = (cond / (1.0 + jnp.exp(-cond))).astype(BF)
    act = jnp.broadcast_to(act, (16, act.shape[1]))
    part[...] = dot_trans(act, weight[...])[0:1, :] + row_part(bias, spots, "ada")


def attention_kernel(
    frames, spots, length, normed, m0, m1, m2, m3, qkv_a, qkv_b, bias_a, bias_b, out_a, out_b,
    part, mods, normed_low, saved_a, saved_b, probs_out, att_a, att_b, rows,
):
    rank = lax.axis_index("tensor")
    width = normed.shape[1]
    for flip, piece in enumerate((m0, m1, m2, m3)):
        rows[pl.ds(rank ^ flip, 1), :] = piece[...]
    cols = rows.shape[1]
    extra = cols - width
    for side in range(2):
        a, b = rows[2 * side : 2 * side + 1, :], rows[2 * side + 1 : 2 * side + 2, :]
        mods[3 * side : 3 * side + 1, :] = a[:, :width]
        mods[3 * side + 1 : 3 * side + 2, :] = jnp.concatenate([a[:, width:], b[:, :extra]], axis=1)
        mods[3 * side + 2 : 3 * side + 3, :] = b[:, extra:]
    mods[6:8, :] = jnp.zeros((2, width), F32)
    low = (normed[...] * (1.0 + mods[1:2, :]) + mods[0:1, :]).astype(BF)
    normed_low[...] = low
    half = low.shape[0]
    row_id = lax.broadcasted_iota(jnp.int32, (half, half), 0)
    col_id = lax.broadcasted_iota(jnp.int32, (half, half), 1)
    seen = ((row_id // frames) == (col_id // frames)) & ((col_id % frames) < length[0])
    factor = HEAD_DIM ** (-0.5)
    heads = out_a.shape[0] // HEAD_DIM
    total = None
    blocks = ((qkv_a, bias_a, out_a, saved_a, att_a), (qkv_b, bias_b, out_b, saved_b, att_b))
    for block, (w, b, o, saved, att_ref) in enumerate(blocks):
        qv = row_part(b, spots, "qv")
        zero = jnp.zeros((1, HEAD_DIM), F32)
        pieces = [
            piece
            for h in range(heads)
            for piece in (
                qv[:, 2 * h * HEAD_DIM : (2 * h + 1) * HEAD_DIM],
                zero,
                qv[:, (2 * h + 1) * HEAD_DIM : (2 * h + 2) * HEAD_DIM],
            )
        ]
        qkv = dot_trans(low, w[...]) + jnp.concatenate(pieces, axis=1)
        saved[...] = qkv.astype(BF)
        for h in range(heads):
            base = h * 3 * HEAD_DIM
            q, k, v = (
                qkv[:, base + j * HEAD_DIM : base + (j + 1) * HEAD_DIM].astype(BF)
                for j in range(3)
            )
            scores = jnp.where(seen, dot_trans(q, k) * factor, -1e30)
            raised = jnp.exp(scores - jnp.max(scores, axis=-1, keepdims=True))
            probs = raised / jnp.sum(raised, axis=-1, keepdims=True)
            probs_out[block * heads + h] = probs
            att_ref[:, h * HEAD_DIM : (h + 1) * HEAD_DIM] = dot(probs.astype(BF), v).astype(BF)
        term = dot(att_ref[...], o[...])
        total = term if total is None else total + term
    part[...] = total.astype(BF)


def early_back_kernel(
    frames, n_dp, length, mods, cotangent, down_a, down_b, normed_low, att_a, att_b,
    grad_a, grad_b, pack_far, own_chunks, chunks_far, chunks_core, fc2_sum,
):
    upstream = cotangent[...].astype(F32)
    half, width = upstream.shape
    keep = kept_rows(length, half, frames)
    low32 = (mods[5:6, :] * jnp.where(keep, upstream, 0.0)).astype(BF).astype(F32)
    low = low32.astype(BF)
    grad_a[...] = dot(low, down_a[...])
    grad_b[...] = dot(low, down_b[...])
    fc2_sum[...] = column_sum(low32)
    n_att = att_a.shape[1]
    part = width // 2
    mine, other = split_chunks(normed_low[...].astype(F32), n_dp, 1)
    pack_far[:, 0:n_att] = att_a[...]
    pack_far[:, n_att : 2 * n_att] = att_b[...]
    at = pad_lanes(2 * n_att)
    pack_far[:, at : at + part] = other.astype(BF)
    own_chunks[:, 0:part] = mine.astype(BF)
    mine, other = split_chunks(low32, n_dp, 2)
    chunks_far[:, 0:part] = other.astype(BF)
    chunks_core[:, 0:part] = mine.astype(BF)


def mlp_kernel(
    n_dp, spots, tokens, part1, part1_other, mods, up_a, up_b, fc1_a, fc1_b, grad_a, grad_b,
    chunks_far, part3, pack_act, pack_pre, chunks_core, branch_out, normed_out, inv_out,
):
    branch = part1[...].astype(F32) + part1_other[...].astype(F32) + row_part(fc1_a, spots, "proj")
    branch_out[...] = branch
    mid = tokens[...].astype(F32) + mods[2:3, :] * branch
    normed, inv = standardize(mid)
    normed_out[...] = normed
    inv_out[...] = inv
    low32 = normed * (1.0 + mods[4:5, :]) + mods[3:4, :]
    low = low32.astype(BF)
    total = None
    cols = up_a.shape[1]
    for block, (u, b, g) in enumerate(((up_a, fc1_a, grad_a), (up_b, fc1_b, grad_b))):
        act, slope = gelu_pair(dot(low, u[...]) + row_part(b, spots, "fc1"))
        pack_act[:, block * cols : (block + 1) * cols] = act.astype(BF)
        pre = (g[...] * slope).astype(BF)
        pack_pre[:, block * cols : (block + 1) * cols] = pre
        term = dot_trans(pre, u[...])
        total = term if total is None else total + term
    part3[...] = total.astype(BF)
    mine, other = split_chunks(low32, n_dp, 0)
    part = mine.shape[1]
    pack_pre[:, 2 * cols : 2 * cols + part] = other.astype(BF)
    chunks_core[:, 0:part] = mine.astype(BF)
    pack_act[:, 2 * cols :] = chunks_far[...]


def mlp_tail_kernel(
    spans, pack_act, pack_pre, down_a, down_b, chunks_act, chunks_pre, far1, pack1, chunks1,
    part2, core, sums,
):
    cols = down_a.shape[1]
    part2[...] = (
        dot_trans(pack_act[:, 0:cols], down_a[...]) + dot_trans(pack_act[:, cols : 2 * cols], down_b[...])
    ).astype(BF)
    forward_kernel([spans], pack_act, pack_pre, chunks_act, chunks_pre, far1, pack1, chunks1, core)
    sums[0:1, :] = column_sum(pack_pre[:, 0:cols].astype(F32))
    sums[1:2, :] = column_sum(pack_pre[:, cols : 2 * cols].astype(F32))


def attention_back_kernel(
    frames, length, part3, part3_other, mods, normed, inv, branch, cotangent,
    out_a, out_b, qkv_a, qkv_b, saved_a, saved_b, probs_in,
    part4, mid_grad_out, low_out, stacked, sums,
):
    upstream = cotangent[...].astype(F32)
    half, width = upstream.shape
    keep = kept_rows(length, half, frames)
    grad = part3[...].astype(F32) + part3_other[...].astype(F32)
    norm = normed[...]
    mid_grad = jnp.where(keep, upstream, 0.0) + standardize_back(grad, mods[4:5, :], norm, inv[...])
    mid_grad_out[...] = mid_grad
    low = (mods[2:3, :] * mid_grad).astype(BF)
    low_out[...] = low
    sums[0:1, :] = column_sum(grad)
    sums[1:2, :] = column_sum(grad * norm)
    sums[2:3, :] = column_sum(mid_grad * branch[...])
    sums[3:4, :] = column_sum(low.astype(F32))
    factor = HEAD_DIM ** (-0.5)
    heads = out_a.shape[0] // HEAD_DIM
    cols = heads * 3 * HEAD_DIM
    wide = pad_lanes(cols)
    total = None
    for block, (w, o, saved) in enumerate(((qkv_a, out_a, saved_a), (qkv_b, out_b, saved_b))):
        att_grad = dot_trans(low, o[...])
        qkv = saved[...].astype(F32)
        for h in range(heads):
            base = h * 3 * HEAD_DIM
            q, k, v = (
                qkv[:, base + j * HEAD_DIM : base + (j + 1) * HEAD_DIM].astype(BF)
                for j in range(3)
            )
            ag = att_grad[:, h * HEAD_DIM : (h + 1) * HEAD_DIM].astype(BF)
            probs = probs_in[block * heads + h]
            value_grad = dot_rows(probs.astype(BF), ag)
            probs_grad = dot_trans(ag, v)
            inner = jnp.sum(probs * probs_grad, axis=-1, keepdims=True)
            scores_low = (probs * (probs_grad - inner)).astype(BF)
            query_grad = dot(scores_low, k) * factor
            key_grad = dot_rows(scores_low, q) * factor
            at = block * wide + base
            for j, piece in enumerate((query_grad, key_grad, value_grad)):
                stacked[:, at + j * HEAD_DIM : at + (j + 1) * HEAD_DIM] = piece.astype(BF)
        mine = stacked[:, block * wide : block * wide + cols]
        sums[4 + block : 5 + block, 0:cols] = column_sum(mine.astype(F32))
        term = dot(mine, w[...])
        total = term if total is None else total + term
    part4[...] = total.astype(BF)


def pack_back_kernel(n_dp, low, stacked, pack_far, own_chunks):
    mine, other = split_chunks(low[...].astype(F32), n_dp, 1)
    part, cols = mine.shape[1], stacked.shape[1]
    pack_far[:, 0:cols] = stacked[...]
    pack_far[:, cols : cols + part] = other.astype(BF)
    own_chunks[:, 0:part] = mine.astype(BF)


def output_kernel(
    frames, spots, length, tokens, part2, part2_other, bias, mods, branch1, cotangent,
    result, gate_sum,
):
    inputs, upstream = tokens[...].astype(F32), cotangent[...].astype(F32)
    keep = kept_rows(length, inputs.shape[0], frames)
    branch = part2[...].astype(F32) + part2_other[...].astype(F32) + row_part(bias, spots, "fc2")
    mid = inputs + mods[2:3, :] * branch1[...]
    result[...] = jnp.where(keep, mid + mods[5:6, :] * branch, inputs).astype(BF)
    gate_sum[...] = column_sum(jnp.where(keep, upstream, 0.0) * branch)


def input_back_kernel(
    frames, length, part4, part4_other, mods, normed, inv, mid_grad, cotangent,
    back_sums, gate2_sum, fc2_sum, pre_sums, result, both, sums,
):
    upstream = cotangent[...].astype(F32)
    keep = kept_rows(length, upstream.shape[0], frames)
    grad = part4[...].astype(F32) + part4_other[...].astype(F32)
    norm = normed[...]
    back = standardize_back(grad, mods[1:2, :], norm, inv[...])
    width = norm.shape[1]
    both[:, :width] = result[...]
    both[:, width:] = (mid_grad[...] + back + jnp.where(keep, 0.0, upstream)).astype(BF)
    sums[0:1, :] = column_sum(grad)
    sums[1:2, :] = column_sum(grad * norm)
    sums[2:3, :] = back_sums[2:3, :]
    sums[3:5, :] = back_sums[0:2, :]
    sums[5:6, :] = gate2_sum[...]
    sums[6:7, :] = fc2_sum[...]
    sums[7:8, :] = back_sums[3:4, :]
    sums[8:10, :] = pre_sums[0:2, :]
    sums[10:12, :] = back_sums[4:6, :]
    sums[12:16, :] = jnp.zeros((4, sums.shape[1]), F32)


def vector_kernel(layout, label, mine, other, cond, vector):
    rank = lax.axis_index("tensor")
    width = mine.shape[1]
    both = mine[...] + other[...]
    upper = rank >= 2
    pick = lambda i: jnp.where(upper, both[3 + i : 4 + i, :], both[i : i + 1, :])
    cols = layout["mod"][1]
    extra = cols - width
    shift, scale, gate = pick(0), pick(1), pick(2)
    even = jnp.concatenate([shift, scale[:, :extra]], axis=1)
    odd = jnp.concatenate([scale[:, extra:], gate], axis=1)
    vector[...] = jnp.zeros(vector.shape, F32)

    def put(name, value):
        at, size = layout[name]
        vector[:, at : at + size] = value

    put("mod", jnp.where((rank & 1) == 0, even, odd).astype(BF).astype(F32))
    put("fc2", both[6:7, :])
    put("proj", both[7:8, :])
    put("fc1", (mine[8:9, :] + other[9:10, :])[:, : layout["fc1"][1]])
    put("stack", (mine[10:11, :] + other[11:12, :])[:, : layout["stack"][1]])
    put("cond", cond[...])
    put("label", jnp.full((1, 128), label[0], jnp.int32).astype(F32))


def gathered_kernel(layout, n_dp, rows_out, weight, source, *refs):
    ada_grad, ada_bias, qv, proj, fc1, fc2, stay, send, cond_cols, labels, table = refs
    rank, place = lax.axis_index("tensor"), lax.axis_index("dp")
    for i in range(n_dp):
        table[pl.ds(place ^ i, 1), :] = source[i : i + 1, :]

    def get(name):
        at, size = layout[name]
        return table[:, at : at + size]

    sums = lambda name: column_sum(get(name))
    for name, out in (("mod", ada_bias), ("proj", proj), ("fc1", fc1), ("fc2", fc2)):
        out[...] = sums(name).reshape(out.shape)
    stack = sums("stack")
    pieces = [
        stack[:, i * HEAD_DIM : (i + 1) * HEAD_DIM]
        for i in range(stack.shape[1] // HEAD_DIM)
        if i % 3 != 1
    ]
    qv[...] = jnp.concatenate(pieces, axis=1).reshape(qv.shape)
    mod = get("mod").astype(BF)
    cond = get("cond")
    act = cond / (1.0 + jnp.exp(-cond))
    width = act.shape[1]
    mine = pltpu.roll(act, (width - place * rows_out) % width, 1)[:, :rows_out].astype(BF)
    ada_grad[...] = dot_rows(mine, mod)
    columns = cond_cols.shape[1]
    cond_part = dot(mod, weight[...])
    wide = pad_lanes(columns)
    for flip in range(4):
        out, at = (stay, send)[flip & 1], (flip >> 1) * wide
        piece = pltpu.roll(cond_part, (width - (rank ^ flip) * columns) % width, 1)[:, :columns]
        out[:, at : at + columns] = piece
    cond_cols[...] = pltpu.roll(cond, (width - rank * columns) % width, 1)[:, :columns]
    labels[...] = get("label")


def middle_kernel(stay, other, mine, send):
    columns = mine.shape[1]
    wide = pad_lanes(columns)
    mine[...] = stay[:, 0:columns] + other[:, 0:columns]
    send[...] = stay[:, wide : wide + columns] + other[:, wide : wide + columns]


def table_kernel(mine, other, cond_cols, labels, out):
    cond = cond_cols[...]
    gate = 1.0 / (1.0 + jnp.exp(-cond))
    grad = (mine[...] + other[...]) * gate * (1.0 + cond * (1.0 - gate))
    classes = lax.broadcasted_iota(jnp.int32, (cond.shape[0], out.shape[1]), 1).astype(F32)
    onehot = jnp.where(labels[:, : out.shape[1]] == classes, 1.0, 0.0)
    out[...] = lax.dot_general(
        grad,
        onehot,
        (((0,), (0,)), ((), ())),
        precision=lax.Precision.HIGHEST,
        preferred_element_type=F32,
    )


def forward_kernel(spans, *refs):
    for parts, out in zip(spans, refs[-len(spans) :]):
        at = 0
        for i, start, size in parts:
            out[:, at : at + size] = refs[i][:, start : start + size]
            at += size


def weight_kernel(n_dp, split_bit, products, n_in, *refs):
    outs, lefts = refs[n_in : -len(products)], refs[-len(products) :]
    half = refs[0].shape[0]
    part = lefts[0].shape[0]
    r = part // (n_dp // 2)
    at = 0
    for left, (left_rows, right_rows, cols) in zip(lefts, products):
        for i, (j, start) in enumerate(left_rows):
            value = refs[j][:, start : start + part]
            left[:, i * half : (i + 1) * half] = value.astype(F32).T.astype(BF)
        right = [refs[j][:, start : start + cols] for j, start in right_rows]
        right = jnp.concatenate(right, axis=0)
        if split_bit is None:
            outs[0][:, at : at + cols] = dot(left[...], right)
        else:
            stay, send = outs
            mine = (lax.axis_index("dp") >> split_bit) & 1
            for k in range(n_dp // 4):
                for out, side in ((stay, mine), (send, 1 - mine)):
                    start = pl.multiple_of((2 * k + side) * r, r)
                    out[k, :, at : at + cols] = dot(left[pl.ds(start, r), :], right).astype(out.dtype)
        at += cols


def halve_kernel(bit, stay, other, out_stay, out_send):
    mine = (lax.axis_index("dp") >> bit) & 1
    out_stay[...] = stay[mine] + other[mine].astype(F32)
    out_send[...] = (stay[1 - mine] + other[1 - mine].astype(F32)).astype(BF)


def add_kernel(widths, stay, other, *outs):
    total = stay[...] + other[...].astype(F32)
    at = 0
    for out, cols in zip(outs, widths):
        out[...] = total[:, at : at + cols]
        at += cols


def join_kernel(mine, other, *outs):
    half, width = mine.shape[0], outs[0].shape[1]
    core = lax.axis_index("tensor") & 1
    for source, side in ((mine, core), (other, 1 - core)):
        rows = pl.ds(pl.multiple_of(side * half, half), half)
        for i, out in enumerate(outs):
            out[rows, :] = source[:, i * width : (i + 1) * width]


def stack_kernel(mine, other, out):
    n = mine.shape[0]
    out[0:n, :] = mine[...]
    out[n : 2 * n, :] = other[...]


def shards(
    tokens,
    lengths,
    timesteps,
    labels,
    class_table,
    ada_weight,
    ada_bias,
    qkv_weight,
    qv_bias,
    out_weight,
    proj_bias,
    up_weight,
    fc1_bias,
    down_weight,
    fc2_bias,
    cotangent,
):
    clips, patches, frames, width = tokens.shape
    assert clips == 1 and lax.axis_size("tensor") == 4
    rows = patches * frames
    half = rows // 2
    n_att = out_weight.shape[1]
    heads = n_att // HEAD_DIM
    n_qkv = qkv_weight.shape[1]
    hidden = up_weight.shape[1]
    columns = class_table.shape[1]
    ada_cols = ada_weight.shape[1]
    n_classes = class_table.shape[0]
    t_rank = lax.axis_index("tensor")
    d_rank = lax.axis_index("dp")
    n_dp = lax.axis_size("dp")
    order = []
    chunk = width // n_dp
    part = width // 2
    wide = pad_lanes(part)

    tokens2 = tokens.reshape(rows, width)
    cot2 = cotangent.reshape(rows, width)
    half_width = width // 2
    freqs = np.exp(-math.log(10000.0) * np.arange(half_width) / half_width)
    small = (
        ("ada", ada_bias), ("qv", qv_bias), ("fc1", fc1_bias), ("proj", proj_bias),
        ("fc2", fc2_bias), ("freqs", jnp.asarray(freqs, F32)),
    )
    spots, n_row = {}, 0
    for name, v in small:
        spots[name] = (n_row, v.shape[0])
        n_row += pad_lanes(v.shape[0])
    bias_row = sum(
        jnp.pad(v.astype(F32), (spots[name][0], n_row - spots[name][0] - v.shape[0]))
        for name, v in small
    ).reshape(1, n_row)

    def gather_tensor(own, *others):
        across = behind(swap(own, "tensor", 2), *others)
        return [own, swap(own, "tensor", 1), across, swap(across, "tensor", 1)]

    def pair(weight, *others):
        return weight, swap(behind(weight, *others), "tensor", 1)

    picked = lax.dynamic_slice_in_dim(class_table, labels[0], 1, 0)
    (clock,) = call(
        order,
        lambda *refs: clock_kernel(spots, *refs),
        "clock",
        5.0,
        [((1, width), F32)],
        [timesteps, bias_row],
    )
    pieces = gather_tensor(picked, clock, bias_row)
    bias_ws = pair(bias_row)
    cond, mod_part = call(
        order,
        lambda *refs: modulation_kernel(spots, *refs),
        "modulation",
        1.0,
        [((1, width), F32), ((1, ada_cols), F32)],
        [*pieces, clock, ada_weight.T, bias_row],
        [pltpu.VMEM((8, columns), F32)],
    )
    normed1, inv1, tok, cot = call(
        order,
        start_kernel,
        "start",
        1.0,
        [((half, width), F32), ((half, 1), F32), ((half, width), BF), ((half, width), BF)],
        [tokens2, cot2],
    )
    qkv_ws = pair(qkv_weight.T, pieces[1], pieces[3])
    out_ws = pair(out_weight.T, pieces[1], pieces[3])
    mod_pieces = gather_tensor(mod_part, bias_ws[1], qkv_ws[1], out_ws[1], normed1)
    up_ws = pair(up_weight, *mod_pieces)
    down_ws = pair(down_weight, *mod_pieces)

    part1, mods, low1, saved_a, saved_b, probs, att_a, att_b = call(
        order,
        lambda *refs: attention_kernel(frames, spots, *refs),
        "attention",
        4.0,
        [
            ((half, width), BF),
            ((8, width), F32),
            ((half, width), BF),
            ((half, n_qkv), BF),
            ((half, n_qkv), BF),
            ((2 * heads, half, half), F32),
            ((half, n_att), BF),
            ((half, n_att), BF),
        ],
        [lengths, normed1, *mod_pieces, *qkv_ws, *bias_ws, *out_ws],
        [pltpu.VMEM((8, ada_cols), F32)],
    )
    part1_other = swap(part1, "tensor", 2)

    att_far, att_core = pad_lanes(2 * n_att), pad_lanes(n_att)
    grad_a, grad_b, pack1, chunks1, chunks_far, chunks_act, fc2_sum = call(
        order,
        lambda *refs: early_back_kernel(frames, n_dp, *refs),
        "early_back",
        2.0,
        [
            ((half, hidden), F32),
            ((half, hidden), F32),
            ((half, att_far + wide), BF),
            ((half, wide), BF),
            ((half, wide), BF),
            ((half, wide), BF),
            ((1, width), F32),
        ],
        [lengths, mods, cot, *down_ws, low1, att_a, att_b],
    )

    part3, pack_act, pack_pre, chunks_pre, branch1, normed2, inv2 = call(
        order,
        lambda *refs: mlp_kernel(n_dp, spots, *refs),
        "mlp",
        3.0,
        [
            ((half, width), BF),
            ((half, 2 * hidden + wide), BF),
            ((half, 2 * hidden + wide), BF),
            ((half, wide), BF),
            ((half, width), F32),
            ((half, width), F32),
            ((half, 1), F32),
        ],
        [
            tok, part1, part1_other, mods, *up_ws, *bias_ws, grad_a, grad_b,
            chunks_far,
        ],
    )
    part3_other = swap(part3, "tensor", 2)

    def forward(name, spans, sources, also=()):
        outs = [((half, sum(size for _, _, size in parts)), BF) for parts in spans]
        outs = call(
            order, lambda *refs: forward_kernel(spans, *refs), name, 0.02, outs, sources, also=also
        )
        return [swap(out, "tensor", 1) for out in outs]

    def first_grads(name, bit, products, args):
        cols = sum(p[2] for p in products)
        scratch = [pltpu.VMEM((part, 4 * half), BF)] * len(products)
        split, outs = None, [((part, cols), F32)]
        if n_dp == 8:
            split = 0 if bit else 1
            outs = [((2, chunk, cols), F32), ((2, chunk, cols), BF)]
        outs = call(
            order,
            lambda *refs: weight_kernel(n_dp, split, products, len(args), *refs),
            name,
            0.02,
            outs,
            args,
            scratch,
        )
        return outs[0], swap(outs[1], "dp", 1 << split) if n_dp == 8 else None

    def second_grads(name, bit, stay, other):
        if n_dp != 8:
            return stay, other
        last = 1 if bit == 2 else 2
        shape = (chunk, stay.shape[2])
        stay, send = call(
            order, lambda *refs: halve_kernel(last, *refs), name, 0.02, [(shape, F32), (shape, BF)], [stay, other]
        )
        return stay, swap(send, "dp", 1 << last)

    def last_grads(name, bit, widths, stay, other):
        if n_dp == 8:
            return call(
                order,
                lambda *refs: add_kernel(widths, *refs),
                name,
                0.02,
                [((chunk, w), F32) for w in widths],
                [stay, other],
            )
        grad = stay.reshape(n_dp // 2, chunk, -1)
        for b in range((n_dp - 1).bit_length()):
            if b != bit:
                my_bit = (d_rank >> b) & 1
                grad = grad.reshape(grad.shape[0] // 2, 2, chunk, grad.shape[2])
                send = lax.dynamic_index_in_dim(grad, 1 - my_bit, 1, keepdims=False).astype(BF)
                stay = lax.dynamic_index_in_dim(grad, my_bit, 1, keepdims=False)
                grad = stay + swap(send, "dp", 1 << b).astype(F32)
        return jnp.split(grad[0], [sum(widths[:i]) for i in range(1, len(widths))], axis=1)

    far1 = swap(pack1, "dp", 2)
    n_mix = hidden + wide
    n_mix1 = att_core + wide
    at1 = 2 * n_mix
    core_spans = [
        (0, hidden, hidden), (2, 0, wide), (1, hidden, hidden), (3, 0, wide),
        (4, n_att, att_core), (4, att_far, wide), (5, n_att, att_core), (6, 0, wide),
    ]
    part2, core_mlp, pre_sums = call(
        order,
        lambda *refs: mlp_tail_kernel(core_spans, *refs),
        "mlp_tail",
        2.0,
        [((half, width), BF), ((half, 2 * n_mix + 2 * n_mix1), BF), ((2, hidden), F32)],
        [pack_act, pack_pre, *down_ws, chunks_act, chunks_pre, far1, pack1, chunks1],
    )
    part2_other = swap(part2, "tensor", 2)
    core_mlp = swap(core_mlp, "tensor", 1)
    far_act = swap(behind(pack_act, part2), "dp", 4)
    far_pre = swap(behind(pack_pre, part2), "dp", 1)

    part4, mid_grad, low_back, stacked, back_sums = call(
        order,
        lambda *refs: attention_back_kernel(frames, *refs),
        "attention_back",
        5.0,
        [
            ((half, width), BF),
            ((half, width), F32),
            ((half, width), BF),
            ((half, 2 * pad_lanes(n_qkv)), BF),
            ((8, width), F32),
        ],
        [
            lengths, part3, part3_other, mods, normed2, inv2, branch1, cot,
            *out_ws, *qkv_ws, saved_a, saved_b, probs,
        ],
    )
    part4_other = swap(part4, "tensor", 2)
    s_wide = pad_lanes(n_qkv)
    pack3, chunks3 = call(
        order,
        lambda *refs: pack_back_kernel(n_dp, *refs),
        "pack_back",
        0.02,
        [((half, 2 * s_wide + wide), BF), ((half, wide), BF)],
        [low_back, stacked],
        free=True,
    )
    far3 = swap(pack3, "dp", 2)

    result, gate2_sum = call(
        order,
        lambda *refs: output_kernel(frames, spots, *refs),
        "output",
        0.02,
        [((half, width), BF), ((1, width), F32)],
        [lengths, tok, part2, part2_other, bias_row, mods, branch1, cot],
    )
    both, sums = call(
        order,
        lambda *refs: input_back_kernel(frames, *refs),
        "input_back",
        0.02,
        [((half, 2 * width), BF), ((16, width), F32)],
        [
            lengths, part4, part4_other, mods, normed1, inv1, mid_grad, cot,
            back_sums, gate2_sum, fc2_sum, pre_sums, result,
        ],
    )
    sums_other = swap(sums, "tensor", 1)
    layout, at = {}, 0
    for name, size in (
        ("mod", ada_cols), ("fc2", width), ("proj", width), ("fc1", hidden), ("stack", n_qkv),
        ("cond", width), ("label", 128),
    ):
        layout[name] = (at, size)
        at += pad_lanes(size)
    (vector,) = call(
        order,
        lambda *refs: vector_kernel(layout, *refs),
        "vector",
        0.02,
        [((1, at), F32)],
        [labels, sums, sums_other, cond],
    )

    def stack(name, value, flip):
        n, cols = value.shape
        other = swap(value, "dp", flip)
        return call(order, stack_kernel, name, 0.02, [((2 * n, cols), F32)], [value, other])[0]

    def mlp_grads(name, bit, pack, chunks, far, mixed, at):
        left = ((1, 0), (4, at + hidden), (2, 2 * hidden), (3, hidden))
        right = ((0, 0), (4, at), (2, 0), (3, 0))
        return first_grads(name, bit, [(left, right, hidden)], [pack, chunks, far, mixed, core_mlp])

    vector = stack("stack0", vector, 1)
    mixed_act, mixed_pre = forward(
        "forward_mlp", [[(i, hidden, hidden), (i, 2 * hidden, wide)] for i in range(2)], [far_act, far_pre]
    )
    down_grad = mlp_grads("down_grad", 2, pack_act, chunks_act, far_act, mixed_act, 0)
    up_grad = mlp_grads("up_grad", 0, pack_pre, chunks_pre, far_pre, mixed_pre, n_mix)
    (mixed3,) = forward(
        "forward3",
        [[(0, s_wide, s_wide), (0, 2 * s_wide, wide), (1, s_wide, s_wide), (2, 0, wide)]],
        [far3, pack3, chunks3],
    )
    vector = stack("stack1", vector, 2)
    n_mix3 = s_wide + wide
    left_qkv = ((1, 0), (3, at1 + n_mix1 + att_core), (2, att_far), (3, at1 + att_core))
    right_qkv = ((4, 0), (7, n_mix3), (6, 0), (7, 0))
    left_out = ((5, 0), (7, n_mix3 + s_wide), (6, 2 * s_wide), (7, s_wide))
    right_out = ((0, 0), (3, at1 + n_mix1), (2, 0), (3, at1))
    qkv_grad = first_grads(
        "qkv_grad",
        1,
        [(left_qkv, right_qkv, n_qkv), (left_out, right_out, n_att)],
        [pack1, chunks1, far1, core_mlp, pack3, chunks3, far3, mixed3],
    )
    both_other = swap(behind(both, qkv_grad[0]), "tensor", 1)
    down_grad = second_grads("down_halve", 2, *down_grad)
    up_grad = second_grads("up_halve", 0, *up_grad)
    result, tokens_grad = call(
        order, join_kernel, "join", 0.02, [((rows, width), BF)] * 2, [both, both_other]
    )
    result, tokens_grad = result.reshape(tokens.shape), tokens_grad.reshape(tokens.shape)
    flip = 4
    while flip < n_dp:
        vector = stack("stack%d" % flip, vector, flip)
        flip *= 2
    ada_grad, ada_bias_grad, qv_grad, proj_grad, fc1_grad, fc2_grad, stay, send, cond_cols, labels_all = call(
        order,
        lambda *refs: gathered_kernel(layout, n_dp, chunk, *refs),
        "gathered",
        0.02,
        [((chunk, ada_cols), F32)]
        + [((n,), F32) for n in (ada_cols, qv_bias.shape[0], width, hidden, width)]
        + [((n_dp, 2 * pad_lanes(columns)), F32)] * 2
        + [((n_dp, columns), F32), ((n_dp, 128), F32)],
        [ada_weight.T, vector],
        [pltpu.VMEM((n_dp, at), F32)],
    )
    qkv_grad = second_grads("qkv_halve", 1, *qkv_grad)
    mine, send = call(
        order,
        middle_kernel,
        "middle",
        0.02,
        [((n_dp, columns), F32)] * 2,
        [stay, swap(send, "tensor", 1)],
    )
    (table_grad,) = call(
        order,
        table_kernel,
        "table",
        0.02,
        [((columns, n_classes), F32)],
        [mine, swap(send, "tensor", 2), cond_cols, labels_all],
    )
    (down_grad,) = last_grads("down_add", 2, [hidden], *down_grad)
    (up_grad,) = last_grads("up_add", 0, [hidden], *up_grad)
    qkv_grad, out_grad = last_grads("qkv_add", 1, [n_qkv, n_att], *qkv_grad)
    return (
        result,
        tokens_grad,
        qkv_grad,
        out_grad,
        up_grad,
        down_grad,
        ada_grad,
        table_grad.T,
        qv_grad,
        proj_grad,
        fc1_grad,
        fc2_grad,
        ada_bias_grad,
    )


def solution(mesh):
    placed = (
        P("dp", None, None, None),
        P("dp"),
        P("dp"),
        P("dp"),
        P(None, "tensor"),
        P(None, "tensor"),
        P("tensor"),
        P(None, "tensor"),
        P("tensor"),
        P(None, "tensor"),
        P(),
        P(None, "tensor"),
        P("tensor"),
        P(None, "tensor"),
        P(),
        P("dp", None, None, None),
    )
    return jax.shard_map(
        shards,
        mesh=mesh,
        in_specs=placed,
        out_specs=(
            P("dp", None, None, None),
            P("dp", None, None, None),
            P("dp", "tensor"),
            P("dp", "tensor"),
            P("dp", "tensor"),
            P("dp", "tensor"),
            P("dp", "tensor"),
            P(None, "tensor"),
            P("tensor"),
            P(),
            P("tensor"),
            P(),
            P("tensor"),
        ),
        check_vma=False,
    )
```

```python
import math

import jax
import jax.numpy as jnp
import numpy as np
from jax import lax
from jax.experimental import pallas as pl
from jax.experimental.pallas import tpu as pltpu
from jax.sharding import PartitionSpec as P

HEAD_DIM = 72
BF = jnp.bfloat16
F32 = jnp.float32


def dot(left, right):
    return jnp.dot(left, right, preferred_element_type=F32)


def dot_trans(left, right):
    return lax.dot_general(left, right, (((1,), (1,)), ((), ())), preferred_element_type=F32)


def dot_rows(left, right):
    return lax.dot_general(left, right, (((0,), (0,)), ((), ())), preferred_element_type=F32)


def swap(value, axis, flip):
    size = lax.axis_size(axis)
    return lax.ppermute(value, axis, [(i, i ^ flip) for i in range(size)])


def call(order, body, name, us, outs, args, scratch=(), also=(), limit=24, free=False):
    specs = [
        pl.BlockSpec(
            memory_space=pltpu.SMEM if a.dtype == jnp.int32 else pltpu.VMEM
        )
        for a in args
    ]
    marks = [*(order[:1] if free else order), *also]
    specs += [pl.BlockSpec(memory_space=pl.ANY)] * len(marks)
    n_args, n_outs = len(args), len(outs)
    first_out = n_args + len(marks)

    def whole(*refs):
        body(*refs[:n_args], *refs[first_out : first_out + n_outs], *refs[first_out + n_outs + 1 :])
        refs[first_out + n_outs][...] = jnp.zeros((8, 128), F32)

    *results, mark = pl.pallas_call(
        whole,
        out_shape=[jax.ShapeDtypeStruct(s, d) for s, d in [*outs, ((8, 128), F32)]],
        in_specs=specs,
        out_specs=[pl.BlockSpec(memory_space=pltpu.VMEM)] * (n_outs + 1),
        scratch_shapes=list(scratch),
        compiler_params=pltpu.CompilerParams(vmem_limit_bytes=limit << 20),
        cost_estimate=pl.CostEstimate(
            flops=int(us * 1.1e9), bytes_accessed=1024, transcendentals=0
        ),
        name=name,
    )(*args, *marks)
    if not free:
        order.clear()
    order.append(mark)
    return results


def behind(value, *others):
    return lax.optimization_barrier((value, *others))[0]


def pad_lanes(width):
    return -(-width // 128) * 128


def standardize(value):
    center = value - jnp.mean(value, axis=-1, keepdims=True)
    spread = jnp.mean(center * center, axis=-1, keepdims=True)
    inv = lax.rsqrt(spread + 1e-06)
    return center * inv, inv


def standardize_back(grad, scale, normed, inv):
    g = grad * (1.0 + scale)
    return (
        g
        - jnp.mean(g, axis=-1, keepdims=True)
        - normed * jnp.mean(g * normed, axis=-1, keepdims=True)
    ) * inv


def gelu_pair(value):
    k, c = math.sqrt(2.0 / math.pi), 0.044715
    square = value * value
    h = 0.5 + 0.5 * jnp.tanh(value * (k + (k * c) * square))
    steep = value * (2.0 * k + (6.0 * k * c) * square)
    return value * h, h * (1.0 + (1.0 - h) * steep)


def row_part(ref, spots, name):
    at, size = spots[name]
    return ref[:, at : at + size].astype(F32)


def column_sum(value):
    return jnp.sum(value, axis=0, keepdims=True)


def kept_rows(length_ref, half, frames):
    frame = lax.broadcasted_iota(jnp.int32, (half, 1), 0) % frames
    return frame < length_ref[0]


def split_chunks(value, n_dp, bit):
    r = value.shape[1] // n_dp
    low, high = (
        jnp.concatenate(
            [value[:, i * r : i * r + r] for i in range(n_dp) if (i >> bit) & 1 == side], axis=1
        )
        for side in range(2)
    )
    mine_low = ((lax.axis_index("dp") >> bit) & 1) == 0
    return jnp.where(mine_low, low, high), jnp.where(mine_low, high, low)


def clock_kernel(spots, times, row, clock):
    freqs = row_part(row, spots, "freqs")
    angles = jnp.full(freqs.shape, times[0], jnp.int32).astype(F32) * freqs
    clock[...] = jnp.concatenate([jnp.cos(angles), jnp.sin(angles)], axis=1)


def start_kernel(tokens, cotangent, normed, inv, tok_half, cot_half):
    half = tok_half.shape[0]
    rows = pl.ds(pl.multiple_of((lax.axis_index("tensor") & 1) * half, half), half)
    tok_half[...] = tokens[rows, :]
    cot_half[...] = cotangent[rows, :]
    normed[...], inv[...] = standardize(tok_half[...].astype(F32))


def modulation_kernel(spots, e0, e1, e2, e3, clock, weight, bias, cond_out, part, rows):
    rank = lax.axis_index("tensor")
    for flip, piece in enumerate((e0, e1, e2, e3)):
        rows[pl.ds(rank ^ flip, 1), :] = piece[...].astype(F32)
    cond = clock[...] + jnp.concatenate([rows[i : i + 1, :] for i in range(4)], axis=1)
    cond_out[...] = cond
    act = (cond / (1.0 + jnp.exp(-cond))).astype(BF)
    act = jnp.broadcast_to(act, (16, act.shape[1]))
    part[...] = dot_trans(act, weight[...])[0:1, :] + row_part(bias, spots, "ada")


def attention_kernel(
    frames, spots, length, normed, m0, m1, m2, m3, qkv_a, qkv_b, bias_a, bias_b, out_a, out_b,
    part, mods, normed_low, saved_a, saved_b, probs_out, att_a, att_b, rows,
):
    rank = lax.axis_index("tensor")
    width = normed.shape[1]
    for flip, piece in enumerate((m0, m1, m2, m3)):
        rows[pl.ds(rank ^ flip, 1), :] = piece[...]
    cols = rows.shape[1]
    extra = cols - width
    for side in range(2):
        a, b = rows[2 * side : 2 * side + 1, :], rows[2 * side + 1 : 2 * side + 2, :]
        mods[3 * side : 3 * side + 1, :] = a[:, :width]
        mods[3 * side + 1 : 3 * side + 2, :] = jnp.concatenate([a[:, width:], b[:, :extra]], axis=1)
        mods[3 * side + 2 : 3 * side + 3, :] = b[:, extra:]
    mods[6:8, :] = jnp.zeros((2, width), F32)
    low = (normed[...] * (1.0 + mods[1:2, :]) + mods[0:1, :]).astype(BF)
    normed_low[...] = low
    half = low.shape[0]
    row_id = lax.broadcasted_iota(jnp.int32, (half, half), 0)
    col_id = lax.broadcasted_iota(jnp.int32, (half, half), 1)
    seen = ((row_id // frames) == (col_id // frames)) & ((col_id % frames) < length[0])
    factor = HEAD_DIM ** (-0.5)
    heads = out_a.shape[0] // HEAD_DIM
    total = None
    blocks = ((qkv_a, bias_a, out_a, saved_a, att_a), (qkv_b, bias_b, out_b, saved_b, att_b))
    for block, (w, b, o, saved, att_ref) in enumerate(blocks):
        qv = row_part(b, spots, "qv")
        zero = jnp.zeros((1, HEAD_DIM), F32)
        pieces = [
            piece
            for h in range(heads)
            for piece in (
                qv[:, 2 * h * HEAD_DIM : (2 * h + 1) * HEAD_DIM],
                zero,
                qv[:, (2 * h + 1) * HEAD_DIM : (2 * h + 2) * HEAD_DIM],
            )
        ]
        qkv = dot_trans(low, w[...]) + jnp.concatenate(pieces, axis=1)
        saved[...] = qkv.astype(BF)
        for h in range(heads):
            base = h * 3 * HEAD_DIM
            q, k, v = (
                qkv[:, base + j * HEAD_DIM : base + (j + 1) * HEAD_DIM].astype(BF)
                for j in range(3)
            )
            scores = jnp.where(seen, dot_trans(q, k) * factor, -1e30)
            raised = jnp.exp(scores - jnp.max(scores, axis=-1, keepdims=True))
            probs = raised / jnp.sum(raised, axis=-1, keepdims=True)
            probs_out[block * heads + h] = probs
            att_ref[:, h * HEAD_DIM : (h + 1) * HEAD_DIM] = dot(probs.astype(BF), v).astype(BF)
        term = dot(att_ref[...], o[...])
        total = term if total is None else total + term
    part[...] = total.astype(BF)


def early_back_kernel(
    frames, n_dp, length, mods, cotangent, down_a, down_b, normed_low, att_a, att_b,
    grad_a, grad_b, low_out, pack_far, own_chunks, fc2_sum, pick,
):
    upstream = cotangent[...].astype(F32)
    half, width = upstream.shape
    keep = kept_rows(length, half, frames)
    low = (mods[5:6, :] * jnp.where(keep, upstream, 0.0)).astype(BF)
    low_out[...] = low
    grad_a[...] = dot(low, down_a[...])
    grad_b[...] = dot(low, down_b[...])
    fc2_sum[...] = column_sum(low.astype(F32))
    n_att = att_a.shape[1]
    part = width // 2
    mine, other = split_chunks(normed_low[...].astype(F32), n_dp, 1)
    pack_far[:, 0:n_att] = att_a[...]
    pack_far[:, n_att : 2 * n_att] = att_b[...]
    at = pad_lanes(2 * n_att)
    pack_far[:, at : at + part] = other.astype(BF)
    own_chunks[:, 0:part] = mine.astype(BF)
    r = width // n_dp
    feature = lax.broadcasted_iota(jnp.int32, pick.shape, 1)
    column = lax.broadcasted_iota(jnp.int32, pick.shape, 0)
    target = column + (lax.axis_index("dp") & 5) * r
    ahead = 0
    for k in range(1, n_dp // 4):
        now = ((k & 1) << 1) + ((k >> 1) << 3) - k
        target = target + jnp.where(column >= k * r, (now - ahead) * r, 0)
        ahead = now
    pick[...] = jnp.where(feature == target, 1.0, 0.0).astype(BF)


def mlp_kernel(
    spots, tokens, part1, part1_other, mods, up_a, up_b, fc1_a, fc1_b, grad_a, grad_b,
    part3, act_out, pre_out, low_out, branch_out, normed_out, inv_out, sums,
):
    branch = part1[...].astype(F32) + part1_other[...].astype(F32) + row_part(fc1_a, spots, "proj")
    branch_out[...] = branch
    mid = tokens[...].astype(F32) + mods[2:3, :] * branch
    normed, inv = standardize(mid)
    normed_out[...] = normed
    inv_out[...] = inv
    low = (normed * (1.0 + mods[4:5, :]) + mods[3:4, :]).astype(BF)
    low_out[...] = low
    total = None
    cols = up_a.shape[1]
    for block, (u, b, g) in enumerate(((up_a, fc1_a, grad_a), (up_b, fc1_b, grad_b))):
        act, slope = gelu_pair(dot(low, u[...]) + row_part(b, spots, "fc1"))
        act_out[:, block * cols : (block + 1) * cols] = act.astype(BF)
        pre = (g[...] * slope).astype(BF)
        if block == 0:
            pre_out[...] = pre
        sums[block : block + 1, :] = column_sum(pre.astype(F32))
        term = dot_trans(pre, u[...])
        total = term if total is None else total + term
    part3[...] = total.astype(BF)


def mlp_tail_kernel(act, down_a, down_b, part2):
    cols = down_a.shape[1]
    part2[...] = (
        dot_trans(act[:, 0:cols], down_a[...]) + dot_trans(act[:, cols : 2 * cols], down_b[...])
    ).astype(BF)


def rows_kernel(*refs):
    half = refs[0].shape[0]
    for i, source in enumerate(refs[:-1]):
        refs[-1][i * half : (i + 1) * half, :] = source[...]


def remake_kernel(n_dp, spots, own, before, last, n_blocks, span, pick, up, down, bias, *refs):
    cols = up.shape[1]
    normed, grads, refs = refs[:n_blocks], refs[n_blocks : 2 * n_blocks], refs[2 * n_blocks :]
    if span is not None:
        normed, grads = ([ref.at[span[0] : span[1], :] for ref in v] for v in (normed, grads))
    down_sum, up_sum = 0.0, 0.0
    if own:
        act_own, pre_own, refs = refs[0][:, 0:cols], refs[1][...], refs[2:]
    if before:
        down_sum, up_sum, refs = refs[0][...], refs[1][...], refs[2:]
    joined = lambda parts: parts[0] if len(parts) == 1 else jnp.concatenate(parts, axis=0)
    n_new, g_new = (joined([ref[...] for ref in v[int(own) :]]) for v in (normed, grads))
    act, slope = gelu_pair(dot(n_new, up[...]) + row_part(bias, spots, "fc1"))
    act, pre = act.astype(BF), (dot(g_new, down[...]) * slope).astype(BF)
    if own:
        n_new, g_new = joined([normed[0][...], n_new]), joined([grads[0][...], g_new])
        act, pre = joined([act_own, act]), joined([pre_own, pre])
    down_sum = down_sum + dot(dot_trans(pick[...], g_new).astype(BF), act)
    up_sum = up_sum + dot(dot_trans(pick[...], n_new).astype(BF), pre)
    if last and n_dp == 8:
        stay, send = refs
        r = down_sum.shape[0] // 2
        high = ((lax.axis_index("dp") >> 1) & 1) == 1
        for i, total in enumerate((down_sum, up_sum)):
            one, two = total[:r, :], total[r:, :]
            stay[:, i * cols : (i + 1) * cols] = jnp.where(high, two, one)
            send[:, i * cols : (i + 1) * cols] = jnp.where(high, one, two).astype(BF)
    else:
        refs[0][...] = down_sum
        refs[1][...] = up_sum


def attention_back_kernel(
    frames, length, part3, part3_other, mods, normed, inv, branch, cotangent,
    out_a, out_b, qkv_a, qkv_b, saved_a, saved_b, probs_in,
    part4, mid_grad_out, low_out, stacked, sums,
):
    upstream = cotangent[...].astype(F32)
    half, width = upstream.shape
    keep = kept_rows(length, half, frames)
    grad = part3[...].astype(F32) + part3_other[...].astype(F32)
    norm = normed[...]
    mid_grad = jnp.where(keep, upstream, 0.0) + standardize_back(grad, mods[4:5, :], norm, inv[...])
    mid_grad_out[...] = mid_grad
    low = (mods[2:3, :] * mid_grad).astype(BF)
    low_out[...] = low
    sums[0:1, :] = column_sum(grad)
    sums[1:2, :] = column_sum(grad * norm)
    sums[2:3, :] = column_sum(mid_grad * branch[...])
    sums[3:4, :] = column_sum(low.astype(F32))
    factor = HEAD_DIM ** (-0.5)
    heads = out_a.shape[0] // HEAD_DIM
    cols = heads * 3 * HEAD_DIM
    wide = pad_lanes(cols)
    total = None
    for block, (w, o, saved) in enumerate(((qkv_a, out_a, saved_a), (qkv_b, out_b, saved_b))):
        att_grad = dot_trans(low, o[...])
        qkv = saved[...].astype(F32)
        for h in range(heads):
            base = h * 3 * HEAD_DIM
            q, k, v = (
                qkv[:, base + j * HEAD_DIM : base + (j + 1) * HEAD_DIM].astype(BF)
                for j in range(3)
            )
            ag = att_grad[:, h * HEAD_DIM : (h + 1) * HEAD_DIM].astype(BF)
            probs = probs_in[block * heads + h]
            value_grad = dot_rows(probs.astype(BF), ag)
            probs_grad = dot_trans(ag, v)
            inner = jnp.sum(probs * probs_grad, axis=-1, keepdims=True)
            scores_low = (probs * (probs_grad - inner)).astype(BF)
            query_grad = dot(scores_low, k) * factor
            key_grad = dot_rows(scores_low, q) * factor
            at = block * wide + base
            for j, piece in enumerate((query_grad, key_grad, value_grad)):
                stacked[:, at + j * HEAD_DIM : at + (j + 1) * HEAD_DIM] = piece.astype(BF)
        mine = stacked[:, block * wide : block * wide + cols]
        sums[4 + block : 5 + block, 0:cols] = column_sum(mine.astype(F32))
        term = dot(mine, w[...])
        total = term if total is None else total + term
    part4[...] = total.astype(BF)


def pack_back_kernel(n_dp, low, stacked, pack_far, own_chunks):
    mine, other = split_chunks(low[...].astype(F32), n_dp, 1)
    part, cols = mine.shape[1], stacked.shape[1]
    pack_far[:, 0:cols] = stacked[...]
    pack_far[:, cols : cols + part] = other.astype(BF)
    own_chunks[:, 0:part] = mine.astype(BF)


def output_kernel(
    frames, spots, length, tokens, part2, part2_other, bias, mods, branch1, cotangent,
    result, gate_sum,
):
    inputs, upstream = tokens[...].astype(F32), cotangent[...].astype(F32)
    keep = kept_rows(length, inputs.shape[0], frames)
    branch = part2[...].astype(F32) + part2_other[...].astype(F32) + row_part(bias, spots, "fc2")
    mid = inputs + mods[2:3, :] * branch1[...]
    result[...] = jnp.where(keep, mid + mods[5:6, :] * branch, inputs).astype(BF)
    gate_sum[...] = column_sum(jnp.where(keep, upstream, 0.0) * branch)


def input_back_kernel(
    frames, length, part4, part4_other, mods, normed, inv, mid_grad, cotangent,
    back_sums, gate2_sum, fc2_sum, pre_sums, result, both, sums,
):
    upstream = cotangent[...].astype(F32)
    keep = kept_rows(length, upstream.shape[0], frames)
    grad = part4[...].astype(F32) + part4_other[...].astype(F32)
    norm = normed[...]
    back = standardize_back(grad, mods[1:2, :], norm, inv[...])
    width = norm.shape[1]
    both[:, :width] = result[...]
    both[:, width:] = (mid_grad[...] + back + jnp.where(keep, 0.0, upstream)).astype(BF)
    sums[0:1, :] = column_sum(grad)
    sums[1:2, :] = column_sum(grad * norm)
    sums[2:3, :] = back_sums[2:3, :]
    sums[3:5, :] = back_sums[0:2, :]
    sums[5:6, :] = gate2_sum[...]
    sums[6:7, :] = fc2_sum[...]
    sums[7:8, :] = back_sums[3:4, :]
    sums[8:10, :] = pre_sums[0:2, :]
    sums[10:12, :] = back_sums[4:6, :]
    sums[12:16, :] = jnp.zeros((4, sums.shape[1]), F32)


def vector_kernel(layout, label, mine, other, cond, vector):
    rank = lax.axis_index("tensor")
    width = mine.shape[1]
    both = mine[...] + other[...]
    upper = rank >= 2
    pick = lambda i: jnp.where(upper, both[3 + i : 4 + i, :], both[i : i + 1, :])
    cols = layout["mod"][1]
    extra = cols - width
    shift, scale, gate = pick(0), pick(1), pick(2)
    even = jnp.concatenate([shift, scale[:, :extra]], axis=1)
    odd = jnp.concatenate([scale[:, extra:], gate], axis=1)
    vector[...] = jnp.zeros(vector.shape, F32)

    def put(name, value):
        at, size = layout[name]
        vector[:, at : at + size] = value

    put("mod", jnp.where((rank & 1) == 0, even, odd).astype(BF).astype(F32))
    put("fc2", both[6:7, :])
    put("proj", both[7:8, :])
    put("fc1", (mine[8:9, :] + other[9:10, :])[:, : layout["fc1"][1]])
    put("stack", (mine[10:11, :] + other[11:12, :])[:, : layout["stack"][1]])
    put("cond", cond[...])
    put("label", jnp.full((1, 128), label[0], jnp.int32).astype(F32))


def gathered_kernel(layout, n_dp, rows_out, flips, weight, source, *refs):
    ada_grad, ada_bias, qv, proj, fc1, fc2, stay, send, cond_cols, labels, table = refs
    rank, place = lax.axis_index("tensor"), lax.axis_index("dp")
    for i in range(n_dp):
        flip = sum(f for k, f in enumerate(flips) if (i >> k) & 1)
        table[pl.ds(place ^ flip, 1), :] = source[i : i + 1, :]

    def get(name):
        at, size = layout[name]
        return table[:, at : at + size]

    sums = lambda name: column_sum(get(name))
    for name, out in (("mod", ada_bias), ("proj", proj), ("fc1", fc1), ("fc2", fc2)):
        out[...] = sums(name).reshape(out.shape)
    stack = sums("stack")
    pieces = [
        stack[:, i * HEAD_DIM : (i + 1) * HEAD_DIM]
        for i in range(stack.shape[1] // HEAD_DIM)
        if i % 3 != 1
    ]
    qv[...] = jnp.concatenate(pieces, axis=1).reshape(qv.shape)
    mod = get("mod").astype(BF)
    cond = get("cond")
    act = cond / (1.0 + jnp.exp(-cond))
    width = act.shape[1]
    mine = pltpu.roll(act, (width - place * rows_out) % width, 1)[:, :rows_out].astype(BF)
    ada_grad[...] = dot_rows(mine, mod)
    columns = cond_cols.shape[1]
    cond_part = dot(mod, weight[...])
    wide = pad_lanes(columns)
    for flip in range(4):
        out, at = (stay, send)[flip & 1], (flip >> 1) * wide
        piece = pltpu.roll(cond_part, (width - (rank ^ flip) * columns) % width, 1)[:, :columns]
        out[:, at : at + columns] = piece
    cond_cols[...] = pltpu.roll(cond, (width - rank * columns) % width, 1)[:, :columns]
    labels[...] = get("label")


def middle_kernel(stay, other, mine, send):
    columns = mine.shape[1]
    wide = pad_lanes(columns)
    mine[...] = stay[:, 0:columns] + other[:, 0:columns]
    send[...] = stay[:, wide : wide + columns] + other[:, wide : wide + columns]


def table_kernel(mine, other, cond_cols, labels, out):
    cond = cond_cols[...]
    gate = 1.0 / (1.0 + jnp.exp(-cond))
    grad = (mine[...] + other[...]) * gate * (1.0 + cond * (1.0 - gate))
    classes = lax.broadcasted_iota(jnp.int32, (cond.shape[0], out.shape[1]), 1).astype(F32)
    onehot = jnp.where(labels[:, : out.shape[1]] == classes, 1.0, 0.0)
    out[...] = lax.dot_general(
        grad,
        onehot,
        (((0,), (0,)), ((), ())),
        precision=lax.Precision.HIGHEST,
        preferred_element_type=F32,
    )


def forward_kernel(spans, *refs):
    for parts, out in zip(spans, refs[-len(spans) :]):
        at = 0
        for i, start, size in parts:
            out[:, at : at + size] = refs[i][:, start : start + size]
            at += size


def weight_kernel(n_dp, split_bit, products, n_in, *refs):
    outs, lefts = refs[n_in : -len(products)], refs[-len(products) :]
    half = refs[0].shape[0]
    part = lefts[0].shape[0]
    r = part // (n_dp // 2)
    at = 0
    for left, (left_rows, right_rows, cols) in zip(lefts, products):
        for i, (j, start) in enumerate(left_rows):
            value = refs[j][:, start : start + part]
            left[:, i * half : (i + 1) * half] = value.astype(F32).T.astype(BF)
        right = [refs[j][:, start : start + cols] for j, start in right_rows]
        right = jnp.concatenate(right, axis=0)
        if split_bit is None:
            outs[0][:, at : at + cols] = dot(left[...], right)
        else:
            stay, send = outs
            mine = (lax.axis_index("dp") >> split_bit) & 1
            for k in range(n_dp // 4):
                for out, side in ((stay, mine), (send, 1 - mine)):
                    start = pl.multiple_of((2 * k + side) * r, r)
                    out[k, :, at : at + cols] = dot(left[pl.ds(start, r), :], right).astype(out.dtype)
        at += cols


def halve_kernel(bit, stay, other, out_stay, out_send):
    mine = (lax.axis_index("dp") >> bit) & 1
    out_stay[...] = stay[mine] + other[mine].astype(F32)
    out_send[...] = (stay[1 - mine] + other[1 - mine].astype(F32)).astype(BF)


def add_kernel(widths, stay, other, *outs):
    total = stay[...] + other[...].astype(F32)
    at = 0
    for out, cols in zip(outs, widths):
        out[...] = total[:, at : at + cols]
        at += cols


def join_kernel(mine, other, *outs):
    half, width = mine.shape[0], outs[0].shape[1]
    core = lax.axis_index("tensor") & 1
    for source, side in ((mine, core), (other, 1 - core)):
        rows = pl.ds(pl.multiple_of(side * half, half), half)
        for i, out in enumerate(outs):
            out[rows, :] = source[:, i * width : (i + 1) * width]


def stack_kernel(mine, other, out):
    n = mine.shape[0]
    out[0:n, :] = mine[...]
    out[n : 2 * n, :] = other[...]


def shards(
    tokens,
    lengths,
    timesteps,
    labels,
    class_table,
    ada_weight,
    ada_bias,
    qkv_weight,
    qv_bias,
    out_weight,
    proj_bias,
    up_weight,
    fc1_bias,
    down_weight,
    fc2_bias,
    cotangent,
):
    clips, patches, frames, width = tokens.shape
    assert clips == 1 and lax.axis_size("tensor") == 4
    rows = patches * frames
    half = rows // 2
    n_att = out_weight.shape[1]
    heads = n_att // HEAD_DIM
    n_qkv = qkv_weight.shape[1]
    hidden = up_weight.shape[1]
    columns = class_table.shape[1]
    ada_cols = ada_weight.shape[1]
    n_classes = class_table.shape[0]
    t_rank = lax.axis_index("tensor")
    d_rank = lax.axis_index("dp")
    n_dp = lax.axis_size("dp")
    order = []
    chunk = width // n_dp
    part = width // 2
    wide = pad_lanes(part)

    tokens2 = tokens.reshape(rows, width)
    cot2 = cotangent.reshape(rows, width)
    half_width = width // 2
    freqs = np.exp(-math.log(10000.0) * np.arange(half_width) / half_width)
    small = (
        ("ada", ada_bias), ("qv", qv_bias), ("fc1", fc1_bias), ("proj", proj_bias),
        ("fc2", fc2_bias), ("freqs", jnp.asarray(freqs, F32)),
    )
    spots, n_row = {}, 0
    for name, v in small:
        spots[name] = (n_row, v.shape[0])
        n_row += pad_lanes(v.shape[0])
    bias_row = sum(
        jnp.pad(v.astype(F32), (spots[name][0], n_row - spots[name][0] - v.shape[0]))
        for name, v in small
    ).reshape(1, n_row)

    def gather_tensor(own, *others):
        across = behind(swap(own, "tensor", 2), *others)
        return [own, swap(own, "tensor", 1), across, swap(across, "tensor", 1)]

    def pair(weight, *others):
        return weight, swap(behind(weight, *others), "tensor", 1)

    picked = lax.dynamic_slice_in_dim(class_table, labels[0], 1, 0)
    (clock,) = call(
        order,
        lambda *refs: clock_kernel(spots, *refs),
        "clock",
        5.0,
        [((1, width), F32)],
        [timesteps, bias_row],
    )
    pieces = gather_tensor(picked, clock, bias_row)
    bias_ws = pair(bias_row)
    cond, mod_part = call(
        order,
        lambda *refs: modulation_kernel(spots, *refs),
        "modulation",
        1.0,
        [((1, width), F32), ((1, ada_cols), F32)],
        [*pieces, clock, ada_weight.T, bias_row],
        [pltpu.VMEM((8, columns), F32)],
    )
    normed1, inv1, tok, cot = call(
        order,
        start_kernel,
        "start",
        1.0,
        [((half, width), F32), ((half, 1), F32), ((half, width), BF), ((half, width), BF)],
        [tokens2, cot2],
    )
    qkv_ws = pair(qkv_weight.T, pieces[1], pieces[3])
    out_ws = pair(out_weight.T, pieces[1], pieces[3])
    mod_pieces = gather_tensor(mod_part, bias_ws[1], qkv_ws[1], out_ws[1], normed1)
    up_ws = pair(up_weight, *mod_pieces)
    down_ws = pair(down_weight, *mod_pieces)

    part1, mods, low1, saved_a, saved_b, probs, att_a, att_b = call(
        order,
        lambda *refs: attention_kernel(frames, spots, *refs),
        "attention",
        4.0,
        [
            ((half, width), BF),
            ((8, width), F32),
            ((half, width), BF),
            ((half, n_qkv), BF),
            ((half, n_qkv), BF),
            ((2 * heads, half, half), F32),
            ((half, n_att), BF),
            ((half, n_att), BF),
        ],
        [lengths, normed1, *mod_pieces, *qkv_ws, *bias_ws, *out_ws],
        [pltpu.VMEM((8, ada_cols), F32)],
    )
    part1_other = swap(part1, "tensor", 2)

    att_far, att_core = pad_lanes(2 * n_att), pad_lanes(n_att)
    grad_a, grad_b, low_grad, pack1, chunks1, fc2_sum, pick = call(
        order,
        lambda *refs: early_back_kernel(frames, n_dp, *refs),
        "early_back",
        2.0,
        [
            ((half, hidden), F32),
            ((half, hidden), F32),
            ((half, width), BF),
            ((half, att_far + wide), BF),
            ((half, wide), BF),
            ((1, width), F32),
            ((part // 2, width), BF),
        ],
        [lengths, mods, cot, *down_ws, low1, att_a, att_b],
    )
    far1 = swap(pack1, "dp", 2)
    grad_y = swap(low_grad, "dp", 1)
    grad_f = swap(low_grad, "dp", 4)

    part3, act, pre_own, low2, branch1, normed2, inv2, pre_sums = call(
        order,
        lambda *refs: mlp_kernel(spots, *refs),
        "mlp",
        3.0,
        [
            ((half, width), BF),
            ((half, 2 * hidden), BF),
            ((half, hidden), BF),
            ((half, width), BF),
            ((half, width), F32),
            ((half, width), F32),
            ((half, 1), F32),
            ((2, hidden), F32),
        ],
        [tok, part1, part1_other, mods, *up_ws, *bias_ws, grad_a, grad_b],
    )
    part3_other = swap(part3, "tensor", 2)
    rows_y = swap(behind(low2, grad_y), "dp", 1)
    rows_f = swap(low2, "dp", 4)

    def forward(name, spans, sources, us=0.02):
        outs = [((half, sum(size for _, _, size in parts)), BF) for parts in spans]
        outs = call(
            order, lambda *refs: forward_kernel(spans, *refs), name, us, outs, sources
        )
        return [swap(out, "tensor", 1) for out in outs]

    def first_grads(name, bit, products, args):
        cols = sum(p[2] for p in products)
        scratch = [pltpu.VMEM((part, 4 * half), BF)] * len(products)
        split, outs = None, [((part, cols), F32)]
        if n_dp == 8:
            split = 0 if bit else 1
            outs = [((2, chunk, cols), F32), ((2, chunk, cols), BF)]
        outs = call(
            order,
            lambda *refs: weight_kernel(n_dp, split, products, len(args), *refs),
            name,
            0.02,
            outs,
            args,
            scratch,
        )
        return outs[0], swap(outs[1], "dp", 1 << split) if n_dp == 8 else None

    def second_grads(name, bit, stay, other):
        if n_dp != 8:
            return stay, other
        last = 1 if bit == 2 else 2
        shape = (chunk, stay.shape[2])
        stay, send = call(
            order, lambda *refs: halve_kernel(last, *refs), name, 0.02, [(shape, F32), (shape, BF)], [stay, other]
        )
        return stay, swap(send, "dp", 1 << last)

    def halve_all(grad, done):
        for b in range((n_dp - 1).bit_length()):
            if b not in done:
                my_bit = (d_rank >> b) & 1
                grad = grad.reshape(grad.shape[0] // 2, 2, chunk, grad.shape[2])
                send = lax.dynamic_index_in_dim(grad, 1 - my_bit, 1, keepdims=False).astype(BF)
                stay = lax.dynamic_index_in_dim(grad, my_bit, 1, keepdims=False)
                grad = stay + swap(send, "dp", 1 << b).astype(F32)
        return grad[0]

    def last_grads(name, bit, widths, stay, other):
        if n_dp == 8:
            return call(
                order,
                lambda *refs: add_kernel(widths, *refs),
                name,
                0.02,
                [((chunk, w), F32) for w in widths],
                [stay, other],
            )
        grad = halve_all(stay.reshape(n_dp // 2, chunk, -1), [bit])
        return jnp.split(grad, [sum(widths[:i]) for i in range(1, len(widths))], axis=1)

    (part2,) = call(
        order,
        mlp_tail_kernel,
        "mlp_tail",
        1.0,
        [((half, width), BF)],
        [act, *down_ws],
        also=[far1, grad_f],
    )
    part2_other = swap(part2, "tensor", 2)
    grad_yf = swap(grad_f, "dp", 1)

    part4, mid_grad, low_back, stacked, back_sums = call(
        order,
        lambda *refs: attention_back_kernel(frames, *refs),
        "attention_back",
        5.0,
        [
            ((half, width), BF),
            ((half, width), F32),
            ((half, width), BF),
            ((half, 2 * pad_lanes(n_qkv)), BF),
            ((8, width), F32),
        ],
        [
            lengths, part3, part3_other, mods, normed2, inv2, branch1, cot,
            *out_ws, *qkv_ws, saved_a, saved_b, probs,
        ],
    )
    part4_other = swap(part4, "tensor", 2)
    s_wide = pad_lanes(n_qkv)
    rows_yf = swap(rows_f, "dp", 1)
    pack3, chunks3 = call(
        order,
        lambda *refs: pack_back_kernel(n_dp, *refs),
        "pack_back",
        0.02,
        [((half, 2 * s_wide + wide), BF), ((half, wide), BF)],
        [low_back, stacked],
        free=True,
    )
    far3 = swap(pack3, "dp", 2)

    def remake(name, normed, grads, own, before, last, span=None, us=0.02):
        outs = [((part // 2, hidden), F32)] * 2
        if last and n_dp == 8:
            outs = [((chunk, 2 * hidden), F32), ((chunk, 2 * hidden), BF)]
        return call(
            order,
            lambda *refs: remake_kernel(
                n_dp, spots, bool(own), bool(before), last, len(normed), span, *refs
            ),
            name,
            us,
            outs,
            [pick, up_weight, down_weight, bias_row, *normed, *grads, *own, *before],
            limit=40,
        )

    sums2 = remake(
        "remake_near",
        [low2, rows_y, rows_f],
        [low_grad, grad_y, grad_f],
        [act, pre_own],
        [],
        False,
        us=1.0,
    )
    (grads_core,) = call(
        order,
        rows_kernel,
        "rows_grad",
        0.02,
        [((4 * half, width), BF)],
        [low_grad, grad_y, grad_f, grad_yf],
    )
    grads_other = swap(grads_core, "tensor", 1)
    result, gate2_sum = call(
        order,
        lambda *refs: output_kernel(frames, spots, *refs),
        "output",
        1.0,
        [((half, width), BF), ((1, width), F32)],
        [lengths, tok, part2, part2_other, bias_row, mods, branch1, cot],
    )
    both, sums = call(
        order,
        lambda *refs: input_back_kernel(frames, *refs),
        "input_back",
        0.02,
        [((half, 2 * width), BF), ((16, width), F32)],
        [
            lengths, part4, part4_other, mods, normed1, inv1, mid_grad, cot,
            back_sums, gate2_sum, fc2_sum, pre_sums, result,
        ],
    )
    sums_other = swap(sums, "tensor", 1)
    (rows_core,) = call(
        order,
        rows_kernel,
        "rows_norm",
        0.02,
        [((4 * half, width), BF)],
        [low2, rows_y, rows_f, rows_yf],
    )
    rows_other = swap(rows_core, "tensor", 1)

    layout, at = {}, 0
    for name, size in (
        ("mod", ada_cols), ("fc2", width), ("proj", width), ("fc1", hidden), ("stack", n_qkv),
        ("cond", width), ("label", 128),
    ):
        layout[name] = (at, size)
        at += pad_lanes(size)
    (vector,) = call(
        order,
        lambda *refs: vector_kernel(layout, *refs),
        "vector",
        0.02,
        [((1, at), F32)],
        [labels, sums, sums_other, cond],
    )

    def stack(name, value, flip):
        n, cols = value.shape
        other = swap(value, "dp", flip)
        return call(order, stack_kernel, name, 0.02, [((2 * n, cols), F32)], [value, other])[0]

    def mlp_grads(stay, other):
        if n_dp == 8:
            return call(
                order,
                lambda *refs: add_kernel([hidden] * 2, *refs),
                "mlp_add",
                0.02,
                [((chunk, hidden), F32)] * 2,
                [stay, other],
            )
        return [halve_all(g.reshape(n_dp // 4, chunk, hidden), [0, 2]) for g in (stay, other)]

    sums2 = remake("remake_yf", [rows_yf], [grad_yf], [], sums2, False)
    flips = [4, 1] + [1 << b for b in range(3, (n_dp - 1).bit_length())] + [2]
    mixed3, mixed1 = forward(
        "forward3",
        [
            [(0, s_wide, s_wide), (0, 2 * s_wide, wide), (1, s_wide, s_wide), (2, 0, wide)],
            [(3, n_att, att_core), (3, att_far, wide), (4, n_att, att_core), (5, 0, wide)],
        ],
        [far3, pack3, chunks3, far1, pack1, chunks1],
        us=6.5,
    )
    vector = stack("stack0", vector, flips[0])
    core_args = ([rows_other], [grads_other], [])
    sums2 = remake("remake_core0", *core_args, sums2, False, (0, 2 * half), us=8.0)
    for i, flip in enumerate(flips[1:-1]):
        vector = stack("stack%d" % (i + 1), vector, flip)
    n_mix3 = s_wide + wide
    n_mix1 = att_core + wide
    left_qkv = ((1, 0), (7, n_mix1 + att_core), (2, att_far), (7, att_core))
    right_qkv = ((3, 0), (6, n_mix3), (5, 0), (6, 0))
    left_out = ((4, 0), (6, n_mix3 + s_wide), (5, 2 * s_wide), (6, s_wide))
    right_out = ((0, 0), (7, n_mix1), (2, 0), (7, 0))
    qkv_grad = first_grads(
        "qkv_grad",
        1,
        [(left_qkv, right_qkv, n_qkv), (left_out, right_out, n_att)],
        [pack1, chunks1, far1, pack3, chunks3, far3, mixed3, mixed1],
    )
    mlp_grad = remake("remake_core1", *core_args, sums2, True, (2 * half, 4 * half))
    mlp_grad = (mlp_grad[0], swap(mlp_grad[1], "dp", 2) if n_dp == 8 else mlp_grad[1])
    both_other = swap(behind(both, mlp_grad[0]), "tensor", 1)
    vector = stack("stack_last", vector, flips[-1])
    ada_grad, ada_bias_grad, qv_grad, proj_grad, fc1_grad, fc2_grad, stay, send, cond_cols, labels_all = call(
        order,
        lambda *refs: gathered_kernel(layout, n_dp, chunk, flips, *refs),
        "gathered",
        5.0,
        [((chunk, ada_cols), F32)]
        + [((n,), F32) for n in (ada_cols, qv_bias.shape[0], width, hidden, width)]
        + [((n_dp, 2 * pad_lanes(columns)), F32)] * 2
        + [((n_dp, columns), F32), ((n_dp, 128), F32)],
        [ada_weight.T, vector],
        [pltpu.VMEM((n_dp, at), F32)],
    )
    result, tokens_grad = call(
        order, join_kernel, "join", 0.02, [((rows, width), BF)] * 2, [both, both_other]
    )
    result, tokens_grad = result.reshape(tokens.shape), tokens_grad.reshape(tokens.shape)
    mine, send = call(
        order,
        middle_kernel,
        "middle",
        0.02,
        [((n_dp, columns), F32)] * 2,
        [stay, swap(send, "tensor", 1)],
    )
    (table_grad,) = call(
        order,
        table_kernel,
        "table",
        0.02,
        [((columns, n_classes), F32)],
        [mine, swap(send, "tensor", 2), cond_cols, labels_all],
    )
    qkv_grad = second_grads("qkv_halve", 1, *qkv_grad)
    down_grad, up_grad = mlp_grads(*mlp_grad)
    qkv_grad, out_grad = last_grads("qkv_add", 1, [n_qkv, n_att], *qkv_grad)
    return (
        result,
        tokens_grad,
        qkv_grad,
        out_grad,
        up_grad,
        down_grad,
        ada_grad,
        table_grad.T,
        qv_grad,
        proj_grad,
        fc1_grad,
        fc2_grad,
        ada_bias_grad,
    )


def solution(mesh):
    placed = (
        P("dp", None, None, None),
        P("dp"),
        P("dp"),
        P("dp"),
        P(None, "tensor"),
        P(None, "tensor"),
        P("tensor"),
        P(None, "tensor"),
        P("tensor"),
        P(None, "tensor"),
        P(),
        P(None, "tensor"),
        P("tensor"),
        P(None, "tensor"),
        P(),
        P("dp", None, None, None),
    )
    return jax.shard_map(
        shards,
        mesh=mesh,
        in_specs=placed,
        out_specs=(
            P("dp", None, None, None),
            P("dp", None, None, None),
            P("dp", "tensor"),
            P("dp", "tensor"),
            P("dp", "tensor"),
            P("dp", "tensor"),
            P("dp", "tensor"),
            P(None, "tensor"),
            P("tensor"),
            P(),
            P("tensor"),
            P(),
            P("tensor"),
        ),
        check_vma=False,
    )
```

```python
import math

import jax
import jax.numpy as jnp
import numpy as np
from jax import lax
from jax.experimental import pallas as pl
from jax.experimental.pallas import tpu as pltpu
from jax.sharding import PartitionSpec as P

HEAD_DIM = 72
BF = jnp.bfloat16
F32 = jnp.float32


def dot(left, right):
    return jnp.dot(left, right, preferred_element_type=F32)


def dot_trans(left, right):
    return lax.dot_general(left, right, (((1,), (1,)), ((), ())), preferred_element_type=F32)


def dot_rows(left, right):
    return lax.dot_general(left, right, (((0,), (0,)), ((), ())), preferred_element_type=F32)


def swap(value, axis, flip):
    size = lax.axis_size(axis)
    return lax.ppermute(value, axis, [(i, i ^ flip) for i in range(size)])


def call(order, body, name, us, outs, args, scratch=(), also=(), limit=24, free=False):
    specs = [
        pl.BlockSpec(
            memory_space=pltpu.SMEM if a.dtype == jnp.int32 else pltpu.VMEM
        )
        for a in args
    ]
    marks = [*(order[:1] if free else order), *also]
    specs += [pl.BlockSpec(memory_space=pl.ANY)] * len(marks)
    n_args, n_outs = len(args), len(outs)
    first_out = n_args + len(marks)

    def whole(*refs):
        body(*refs[:n_args], *refs[first_out : first_out + n_outs], *refs[first_out + n_outs + 1 :])
        refs[first_out + n_outs][...] = jnp.zeros((8, 128), F32)

    *results, mark = pl.pallas_call(
        whole,
        out_shape=[jax.ShapeDtypeStruct(s, d) for s, d in [*outs, ((8, 128), F32)]],
        in_specs=specs,
        out_specs=[pl.BlockSpec(memory_space=pltpu.VMEM)] * (n_outs + 1),
        scratch_shapes=list(scratch),
        compiler_params=pltpu.CompilerParams(vmem_limit_bytes=limit << 20),
        cost_estimate=pl.CostEstimate(
            flops=int(us * 1.1e9), bytes_accessed=1024, transcendentals=0
        ),
        name=name,
    )(*args, *marks)
    if not free:
        order.clear()
    order.append(mark)
    return results


def behind(value, *others):
    return lax.optimization_barrier((value, *others))[0]


def pad_lanes(width):
    return -(-width // 128) * 128


def standardize(value):
    center = value - jnp.mean(value, axis=-1, keepdims=True)
    spread = jnp.mean(center * center, axis=-1, keepdims=True)
    inv = lax.rsqrt(spread + 1e-06)
    return center * inv, inv


def standardize_back(grad, scale, normed, inv):
    g = grad * (1.0 + scale)
    return (
        g
        - jnp.mean(g, axis=-1, keepdims=True)
        - normed * jnp.mean(g * normed, axis=-1, keepdims=True)
    ) * inv


def gelu_pair(value):
    k, c = math.sqrt(2.0 / math.pi), 0.044715
    square = value * value
    h = 0.5 + 0.5 * jnp.tanh(value * (k + (k * c) * square))
    steep = value * (2.0 * k + (6.0 * k * c) * square)
    return value * h, h * (1.0 + (1.0 - h) * steep)


def row_part(ref, spots, name):
    at, size = spots[name]
    return ref[:, at : at + size].astype(F32)


def column_sum(value):
    return jnp.sum(value, axis=0, keepdims=True)


def kept_rows(length_ref, half, frames):
    frame = lax.broadcasted_iota(jnp.int32, (half, 1), 0) % frames
    return frame < length_ref[0]


def split_chunks(value, n_dp, bit):
    r = value.shape[1] // n_dp
    low, high = (
        jnp.concatenate(
            [value[:, i * r : i * r + r] for i in range(n_dp) if (i >> bit) & 1 == side], axis=1
        )
        for side in range(2)
    )
    mine_low = ((lax.axis_index("dp") >> bit) & 1) == 0
    return jnp.where(mine_low, low, high), jnp.where(mine_low, high, low)


def clock_kernel(spots, times, row, clock):
    freqs = row_part(row, spots, "freqs")
    angles = jnp.full(freqs.shape, times[0], jnp.int32).astype(F32) * freqs
    clock[...] = jnp.concatenate([jnp.cos(angles), jnp.sin(angles)], axis=1)


def start_kernel(tokens, cotangent, normed, inv, tok_half, cot_half):
    half = tok_half.shape[0]
    rows = pl.ds(pl.multiple_of((lax.axis_index("tensor") & 1) * half, half), half)
    tok_half[...] = tokens[rows, :]
    cot_half[...] = cotangent[rows, :]
    normed[...], inv[...] = standardize(tok_half[...].astype(F32))


def modulation_kernel(spots, e0, e1, e2, e3, clock, weight, bias, cond_out, part, rows):
    rank = lax.axis_index("tensor")
    for flip, piece in enumerate((e0, e1, e2, e3)):
        rows[pl.ds(rank ^ flip, 1), :] = piece[...].astype(F32)
    cond = clock[...] + jnp.concatenate([rows[i : i + 1, :] for i in range(4)], axis=1)
    cond_out[...] = cond
    act = (cond / (1.0 + jnp.exp(-cond))).astype(BF)
    act = jnp.broadcast_to(act, (16, act.shape[1]))
    part[...] = dot_trans(act, weight[...])[0:1, :] + row_part(bias, spots, "ada")


def attention_kernel(
    frames, spots, length, normed, m0, m1, m2, m3, qkv_a, qkv_b, bias_a, bias_b, out_a, out_b,
    part, mods, normed_low, saved_a, saved_b, probs_out, att_a, att_b, rows,
):
    rank = lax.axis_index("tensor")
    width = normed.shape[1]
    for flip, piece in enumerate((m0, m1, m2, m3)):
        rows[pl.ds(rank ^ flip, 1), :] = piece[...]
    cols = rows.shape[1]
    extra = cols - width
    for side in range(2):
        a, b = rows[2 * side : 2 * side + 1, :], rows[2 * side + 1 : 2 * side + 2, :]
        mods[3 * side : 3 * side + 1, :] = a[:, :width]
        mods[3 * side + 1 : 3 * side + 2, :] = jnp.concatenate([a[:, width:], b[:, :extra]], axis=1)
        mods[3 * side + 2 : 3 * side + 3, :] = b[:, extra:]
    mods[6:8, :] = jnp.zeros((2, width), F32)
    low = (normed[...] * (1.0 + mods[1:2, :]) + mods[0:1, :]).astype(BF)
    normed_low[...] = low
    half = low.shape[0]
    row_id = lax.broadcasted_iota(jnp.int32, (half, half), 0)
    col_id = lax.broadcasted_iota(jnp.int32, (half, half), 1)
    seen = ((row_id // frames) == (col_id // frames)) & ((col_id % frames) < length[0])
    factor = HEAD_DIM ** (-0.5)
    heads = out_a.shape[0] // HEAD_DIM
    total = None
    blocks = ((qkv_a, bias_a, out_a, saved_a, att_a), (qkv_b, bias_b, out_b, saved_b, att_b))
    for block, (w, b, o, saved, att_ref) in enumerate(blocks):
        qv = row_part(b, spots, "qv")
        zero = jnp.zeros((1, HEAD_DIM), F32)
        pieces = [
            piece
            for h in range(heads)
            for piece in (
                qv[:, 2 * h * HEAD_DIM : (2 * h + 1) * HEAD_DIM],
                zero,
                qv[:, (2 * h + 1) * HEAD_DIM : (2 * h + 2) * HEAD_DIM],
            )
        ]
        qkv = dot_trans(low, w[...]) + jnp.concatenate(pieces, axis=1)
        saved[...] = qkv.astype(BF)
        for h in range(heads):
            base = h * 3 * HEAD_DIM
            q, k, v = (
                qkv[:, base + j * HEAD_DIM : base + (j + 1) * HEAD_DIM].astype(BF)
                for j in range(3)
            )
            scores = jnp.where(seen, dot_trans(q, k) * factor, -1e30)
            raised = jnp.exp(scores - jnp.max(scores, axis=-1, keepdims=True))
            probs = raised / jnp.sum(raised, axis=-1, keepdims=True)
            probs_out[block * heads + h] = probs
            att_ref[:, h * HEAD_DIM : (h + 1) * HEAD_DIM] = dot(probs.astype(BF), v).astype(BF)
        term = dot(att_ref[...], o[...])
        total = term if total is None else total + term
    part[...] = total.astype(BF)


def early_back_kernel(
    frames, n_dp, length, mods, cotangent, down_a, down_b, normed_low, att_a, att_b,
    grad_a, grad_b, low_out, pack_far, own_chunks, fc2_sum, pick,
):
    upstream = cotangent[...].astype(F32)
    half, width = upstream.shape
    keep = kept_rows(length, half, frames)
    low = (mods[5:6, :] * jnp.where(keep, upstream, 0.0)).astype(BF)
    low_out[...] = low
    grad_a[...] = dot(low, down_a[...])
    grad_b[...] = dot(low, down_b[...])
    fc2_sum[...] = column_sum(low.astype(F32))
    n_att = att_a.shape[1]
    part = width // 2
    mine, other = split_chunks(normed_low[...].astype(F32), n_dp, 1)
    pack_far[:, 0:n_att] = att_a[...]
    pack_far[:, n_att : 2 * n_att] = att_b[...]
    at = pad_lanes(2 * n_att)
    pack_far[:, at : at + part] = other.astype(BF)
    own_chunks[:, 0:part] = mine.astype(BF)
    r = width // n_dp
    feature = lax.broadcasted_iota(jnp.int32, pick.shape, 1)
    column = lax.broadcasted_iota(jnp.int32, pick.shape, 0)
    target = column + (lax.axis_index("dp") & 5) * r
    ahead = 0
    for k in range(1, n_dp // 4):
        now = ((k & 1) << 1) + ((k >> 1) << 3) - k
        target = target + jnp.where(column >= k * r, (now - ahead) * r, 0)
        ahead = now
    pick[...] = jnp.where(feature == target, 1.0, 0.0).astype(BF)


def mlp_kernel(
    spots, tokens, part1, part1_other, mods, up_a, up_b, fc1_a, fc1_b, grad_a, grad_b,
    part3, act_out, pre_out, low_out, branch_out, normed_out, inv_out, sums,
):
    branch = part1[...].astype(F32) + part1_other[...].astype(F32) + row_part(fc1_a, spots, "proj")
    branch_out[...] = branch
    mid = tokens[...].astype(F32) + mods[2:3, :] * branch
    normed, inv = standardize(mid)
    normed_out[...] = normed
    inv_out[...] = inv
    low = (normed * (1.0 + mods[4:5, :]) + mods[3:4, :]).astype(BF)
    low_out[...] = low
    total = None
    cols = up_a.shape[1]
    for block, (u, b, g) in enumerate(((up_a, fc1_a, grad_a), (up_b, fc1_b, grad_b))):
        act, slope = gelu_pair(dot(low, u[...]) + row_part(b, spots, "fc1"))
        act_out[:, block * cols : (block + 1) * cols] = act.astype(BF)
        pre = (g[...] * slope).astype(BF)
        if block == 0:
            pre_out[...] = pre
        sums[block : block + 1, :] = column_sum(pre.astype(F32))
        term = dot_trans(pre, u[...])
        total = term if total is None else total + term
    part3[...] = total.astype(BF)


def mlp_tail_kernel(act, down_a, down_b, part2):
    cols = down_a.shape[1]
    part2[...] = (
        dot_trans(act[:, 0:cols], down_a[...]) + dot_trans(act[:, cols : 2 * cols], down_b[...])
    ).astype(BF)


def rows_kernel(*refs):
    half = refs[0].shape[0]
    for i, source in enumerate(refs[:-1]):
        refs[-1][i * half : (i + 1) * half, :] = source[...]


def remake_kernel(n_dp, spots, own, before, last, n_blocks, span, pick, up, down, bias, *refs):
    cols = up.shape[1]
    normed, grads, refs = refs[:n_blocks], refs[n_blocks : 2 * n_blocks], refs[2 * n_blocks :]
    if span is not None:
        normed, grads = ([ref.at[span[0] : span[1], :] for ref in v] for v in (normed, grads))
    down_sum, up_sum = 0.0, 0.0
    if own:
        act_own, pre_own, refs = refs[0][:, 0:cols], refs[1][...], refs[2:]
    if before:
        down_sum, up_sum, refs = refs[0][...], refs[1][...], refs[2:]
    joined = lambda parts: parts[0] if len(parts) == 1 else jnp.concatenate(parts, axis=0)
    n_new, g_new = (joined([ref[...] for ref in v[int(own) :]]) for v in (normed, grads))
    act, slope = gelu_pair(dot(n_new, up[...]) + row_part(bias, spots, "fc1"))
    act, pre = act.astype(BF), (dot(g_new, down[...]) * slope).astype(BF)
    if own:
        n_new, g_new = joined([normed[0][...], n_new]), joined([grads[0][...], g_new])
        act, pre = joined([act_own, act]), joined([pre_own, pre])
    down_sum = down_sum + dot(dot_trans(pick[...], g_new).astype(BF), act)
    up_sum = up_sum + dot(dot_trans(pick[...], n_new).astype(BF), pre)
    if last and n_dp == 8:
        stay, send = refs
        r = down_sum.shape[0] // 2
        high = ((lax.axis_index("dp") >> 1) & 1) == 1
        for i, total in enumerate((down_sum, up_sum)):
            one, two = total[:r, :], total[r:, :]
            stay[:, i * cols : (i + 1) * cols] = jnp.where(high, two, one)
            send[:, i * cols : (i + 1) * cols] = jnp.where(high, one, two).astype(BF)
    else:
        refs[0][...] = down_sum
        refs[1][...] = up_sum


def attention_back_kernel(
    frames, length, part3, part3_other, mods, normed, inv, branch, cotangent,
    out_a, out_b, qkv_a, qkv_b, saved_a, saved_b, probs_in,
    part4, mid_grad_out, low_out, stacked, sums,
):
    upstream = cotangent[...].astype(F32)
    half, width = upstream.shape
    keep = kept_rows(length, half, frames)
    grad = part3[...].astype(F32) + part3_other[...].astype(F32)
    norm = normed[...]
    mid_grad = jnp.where(keep, upstream, 0.0) + standardize_back(grad, mods[4:5, :], norm, inv[...])
    mid_grad_out[...] = mid_grad
    low = (mods[2:3, :] * mid_grad).astype(BF)
    low_out[...] = low
    sums[0:1, :] = column_sum(grad)
    sums[1:2, :] = column_sum(grad * norm)
    sums[2:3, :] = column_sum(mid_grad * branch[...])
    sums[3:4, :] = column_sum(low.astype(F32))
    factor = HEAD_DIM ** (-0.5)
    heads = out_a.shape[0] // HEAD_DIM
    cols = heads * 3 * HEAD_DIM
    wide = pad_lanes(cols)
    total = None
    for block, (w, o, saved) in enumerate(((qkv_a, out_a, saved_a), (qkv_b, out_b, saved_b))):
        att_grad = dot_trans(low, o[...])
        qkv = saved[...].astype(F32)
        for h in range(heads):
            base = h * 3 * HEAD_DIM
            q, k, v = (
                qkv[:, base + j * HEAD_DIM : base + (j + 1) * HEAD_DIM].astype(BF)
                for j in range(3)
            )
            ag = att_grad[:, h * HEAD_DIM : (h + 1) * HEAD_DIM].astype(BF)
            probs = probs_in[block * heads + h]
            value_grad = dot_rows(probs.astype(BF), ag)
            probs_grad = dot_trans(ag, v)
            inner = jnp.sum(probs * probs_grad, axis=-1, keepdims=True)
            scores_low = (probs * (probs_grad - inner)).astype(BF)
            query_grad = dot(scores_low, k) * factor
            key_grad = dot_rows(scores_low, q) * factor
            at = block * wide + base
            for j, piece in enumerate((query_grad, key_grad, value_grad)):
                stacked[:, at + j * HEAD_DIM : at + (j + 1) * HEAD_DIM] = piece.astype(BF)
        mine = stacked[:, block * wide : block * wide + cols]
        sums[4 + block : 5 + block, 0:cols] = column_sum(mine.astype(F32))
        term = dot(mine, w[...])
        total = term if total is None else total + term
    part4[...] = total.astype(BF)


def pack_back_kernel(n_dp, low, stacked, pack_far, own_chunks):
    mine, other = split_chunks(low[...].astype(F32), n_dp, 1)
    part, cols = mine.shape[1], stacked.shape[1]
    pack_far[:, 0:cols] = stacked[...]
    pack_far[:, cols : cols + part] = other.astype(BF)
    own_chunks[:, 0:part] = mine.astype(BF)


def output_kernel(
    frames, spots, length, tokens, part2, part2_other, bias, mods, branch1, cotangent,
    result, gate_sum,
):
    inputs, upstream = tokens[...].astype(F32), cotangent[...].astype(F32)
    keep = kept_rows(length, inputs.shape[0], frames)
    branch = part2[...].astype(F32) + part2_other[...].astype(F32) + row_part(bias, spots, "fc2")
    mid = inputs + mods[2:3, :] * branch1[...]
    result[...] = jnp.where(keep, mid + mods[5:6, :] * branch, inputs).astype(BF)
    gate_sum[...] = column_sum(jnp.where(keep, upstream, 0.0) * branch)


def input_back_kernel(
    frames, length, part4, part4_other, mods, normed, inv, mid_grad, cotangent,
    back_sums, gate2_sum, fc2_sum, pre_sums, result, both, sums,
):
    upstream = cotangent[...].astype(F32)
    keep = kept_rows(length, upstream.shape[0], frames)
    grad = part4[...].astype(F32) + part4_other[...].astype(F32)
    norm = normed[...]
    back = standardize_back(grad, mods[1:2, :], norm, inv[...])
    width = norm.shape[1]
    both[:, :width] = result[...]
    both[:, width:] = (mid_grad[...] + back + jnp.where(keep, 0.0, upstream)).astype(BF)
    sums[0:1, :] = column_sum(grad)
    sums[1:2, :] = column_sum(grad * norm)
    sums[2:3, :] = back_sums[2:3, :]
    sums[3:5, :] = back_sums[0:2, :]
    sums[5:6, :] = gate2_sum[...]
    sums[6:7, :] = fc2_sum[...]
    sums[7:8, :] = back_sums[3:4, :]
    sums[8:10, :] = pre_sums[0:2, :]
    sums[10:12, :] = back_sums[4:6, :]
    sums[12:16, :] = jnp.zeros((4, sums.shape[1]), F32)


def vector_kernel(layout, label, mine, other, cond, vector):
    rank = lax.axis_index("tensor")
    width = mine.shape[1]
    both = mine[...] + other[...]
    upper = rank >= 2
    pick = lambda i: jnp.where(upper, both[3 + i : 4 + i, :], both[i : i + 1, :])
    cols = layout["mod"][1]
    extra = cols - width
    shift, scale, gate = pick(0), pick(1), pick(2)
    even = jnp.concatenate([shift, scale[:, :extra]], axis=1)
    odd = jnp.concatenate([scale[:, extra:], gate], axis=1)
    vector[...] = jnp.zeros(vector.shape, F32)

    def put(name, value):
        at, size = layout[name]
        vector[:, at : at + size] = value

    put("mod", jnp.where((rank & 1) == 0, even, odd).astype(BF).astype(F32))
    put("fc2", both[6:7, :])
    put("proj", both[7:8, :])
    put("fc1", (mine[8:9, :] + other[9:10, :])[:, : layout["fc1"][1]])
    put("stack", (mine[10:11, :] + other[11:12, :])[:, : layout["stack"][1]])
    put("cond", cond[...])
    put("label", jnp.full((1, 128), label[0], jnp.int32).astype(F32))


def gathered_kernel(layout, n_dp, rows_out, flips, weight, source, *refs):
    ada_grad, ada_bias, qv, proj, fc1, fc2, stay, send, cond_cols, labels, table = refs
    rank, place = lax.axis_index("tensor"), lax.axis_index("dp")
    for i in range(n_dp):
        flip = sum(f for k, f in enumerate(flips) if (i >> k) & 1)
        table[pl.ds(place ^ flip, 1), :] = source[i : i + 1, :]

    def get(name):
        at, size = layout[name]
        return table[:, at : at + size]

    sums = lambda name: column_sum(get(name))
    for name, out in (("mod", ada_bias), ("proj", proj), ("fc1", fc1), ("fc2", fc2)):
        out[...] = sums(name).reshape(out.shape)
    stack = sums("stack")
    pieces = [
        stack[:, i * HEAD_DIM : (i + 1) * HEAD_DIM]
        for i in range(stack.shape[1] // HEAD_DIM)
        if i % 3 != 1
    ]
    qv[...] = jnp.concatenate(pieces, axis=1).reshape(qv.shape)
    mod = get("mod").astype(BF)
    cond = get("cond")
    act = cond / (1.0 + jnp.exp(-cond))
    width = act.shape[1]
    mine = pltpu.roll(act, (width - place * rows_out) % width, 1)[:, :rows_out].astype(BF)
    ada_grad[...] = dot_rows(mine, mod)
    columns = cond_cols.shape[1]
    cond_part = dot(mod, weight[...])
    wide = pad_lanes(columns)
    for flip in range(4):
        out, at = (stay, send)[flip & 1], (flip >> 1) * wide
        piece = pltpu.roll(cond_part, (width - (rank ^ flip) * columns) % width, 1)[:, :columns]
        out[:, at : at + columns] = piece
    cond_cols[...] = pltpu.roll(cond, (width - rank * columns) % width, 1)[:, :columns]
    labels[...] = get("label")


def middle_kernel(stay, other, mine, send):
    columns = mine.shape[1]
    wide = pad_lanes(columns)
    mine[...] = stay[:, 0:columns] + other[:, 0:columns]
    send[...] = stay[:, wide : wide + columns] + other[:, wide : wide + columns]


def table_kernel(mine, other, cond_cols, labels, out):
    cond = cond_cols[...]
    gate = 1.0 / (1.0 + jnp.exp(-cond))
    grad = (mine[...] + other[...]) * gate * (1.0 + cond * (1.0 - gate))
    classes = lax.broadcasted_iota(jnp.int32, (cond.shape[0], out.shape[1]), 1).astype(F32)
    onehot = jnp.where(labels[:, : out.shape[1]] == classes, 1.0, 0.0)
    out[...] = lax.dot_general(
        grad,
        onehot,
        (((0,), (0,)), ((), ())),
        precision=lax.Precision.HIGHEST,
        preferred_element_type=F32,
    )


def forward_kernel(spans, *refs):
    for parts, out in zip(spans, refs[-len(spans) :]):
        at = 0
        for i, start, size in parts:
            out[:, at : at + size] = refs[i][:, start : start + size]
            at += size


def weight_kernel(n_dp, split, products, n_in, *refs):
    outs, lefts = refs[n_in : -len(products)], refs[-len(products) :]
    half = refs[0].shape[0]
    part = lefts[0].shape[0]
    r = part // (n_dp // 2)
    at = 0
    for left, (left_rows, right_rows, cols) in zip(lefts, products):
        for i, (j, start) in enumerate(left_rows):
            value = refs[j][:, start : start + part]
            left[:, i * half : (i + 1) * half] = value.astype(F32).T.astype(BF)
        right = [refs[j][:, start : start + cols] for j, start in right_rows]
        right = jnp.concatenate(right, axis=0)
        if split is None:
            outs[0][:, at : at + cols] = dot(left[...], right)
        else:
            near, far = ((lax.axis_index("dp") >> bit) & 1 for bit in split)
            for (stay, send), k in ((outs[0:2], 1 - far), (outs[2:4], far)):
                for out, side in ((stay, near), (send, 1 - near)):
                    start = pl.multiple_of((2 * k + side) * r, r)
                    out[:, at : at + cols] = dot(left[pl.ds(start, r), :], right).astype(out.dtype)
        at += cols


def halve_kernel(stay, other, send):
    send[...] = (stay[...] + other[...].astype(F32)).astype(BF)


def add_kernel(widths, n_others, stay, *refs):
    total = stay[...]
    for other in refs[:n_others]:
        total = total + other[...].astype(F32)
    at = 0
    for out, cols in zip(refs[n_others:], widths):
        out[...] = total[:, at : at + cols]
        at += cols


def join_kernel(mine, other, *outs):
    half, width = mine.shape[0], outs[0].shape[1]
    core = lax.axis_index("tensor") & 1
    for source, side in ((mine, core), (other, 1 - core)):
        rows = pl.ds(pl.multiple_of(side * half, half), half)
        for i, out in enumerate(outs):
            out[rows, :] = source[:, i * width : (i + 1) * width]


def stack_kernel(mine, other, out):
    n = mine.shape[0]
    out[0:n, :] = mine[...]
    out[n : 2 * n, :] = other[...]


def shards(
    tokens,
    lengths,
    timesteps,
    labels,
    class_table,
    ada_weight,
    ada_bias,
    qkv_weight,
    qv_bias,
    out_weight,
    proj_bias,
    up_weight,
    fc1_bias,
    down_weight,
    fc2_bias,
    cotangent,
):
    clips, patches, frames, width = tokens.shape
    assert clips == 1 and lax.axis_size("tensor") == 4
    rows = patches * frames
    half = rows // 2
    n_att = out_weight.shape[1]
    heads = n_att // HEAD_DIM
    n_qkv = qkv_weight.shape[1]
    hidden = up_weight.shape[1]
    columns = class_table.shape[1]
    ada_cols = ada_weight.shape[1]
    n_classes = class_table.shape[0]
    t_rank = lax.axis_index("tensor")
    d_rank = lax.axis_index("dp")
    n_dp = lax.axis_size("dp")
    order = []
    chunk = width // n_dp
    part = width // 2
    wide = pad_lanes(part)

    tokens2 = tokens.reshape(rows, width)
    cot2 = cotangent.reshape(rows, width)
    half_width = width // 2
    freqs = np.exp(-math.log(10000.0) * np.arange(half_width) / half_width)
    small = (
        ("ada", ada_bias), ("qv", qv_bias), ("fc1", fc1_bias), ("proj", proj_bias),
        ("fc2", fc2_bias), ("freqs", jnp.asarray(freqs, F32)),
    )
    spots, n_row = {}, 0
    for name, v in small:
        spots[name] = (n_row, v.shape[0])
        n_row += pad_lanes(v.shape[0])
    bias_row = sum(
        jnp.pad(v.astype(F32), (spots[name][0], n_row - spots[name][0] - v.shape[0]))
        for name, v in small
    ).reshape(1, n_row)

    def gather_tensor(own, *others):
        across = behind(swap(own, "tensor", 2), *others)
        return [own, swap(own, "tensor", 1), across, swap(across, "tensor", 1)]

    def pair(weight, *others):
        return weight, swap(behind(weight, *others), "tensor", 1)

    picked = lax.dynamic_slice_in_dim(class_table, labels[0], 1, 0)
    (clock,) = call(
        order,
        lambda *refs: clock_kernel(spots, *refs),
        "clock",
        5.0,
        [((1, width), F32)],
        [timesteps, bias_row],
    )
    pieces = gather_tensor(picked, clock, bias_row)
    bias_ws = pair(bias_row)
    cond, mod_part = call(
        order,
        lambda *refs: modulation_kernel(spots, *refs),
        "modulation",
        1.0,
        [((1, width), F32), ((1, ada_cols), F32)],
        [*pieces, clock, ada_weight.T, bias_row],
        [pltpu.VMEM((8, columns), F32)],
    )
    normed1, inv1, tok, cot = call(
        order,
        start_kernel,
        "start",
        1.0,
        [((half, width), F32), ((half, 1), F32), ((half, width), BF), ((half, width), BF)],
        [tokens2, cot2],
    )
    qkv_ws = pair(qkv_weight.T, pieces[1], pieces[3])
    out_ws = pair(out_weight.T, pieces[1], pieces[3])
    mod_pieces = gather_tensor(mod_part, bias_ws[1], qkv_ws[1], out_ws[1], normed1)
    up_ws = pair(up_weight, *mod_pieces)
    down_ws = pair(down_weight, *mod_pieces)

    part1, mods, low1, saved_a, saved_b, probs, att_a, att_b = call(
        order,
        lambda *refs: attention_kernel(frames, spots, *refs),
        "attention",
        4.0,
        [
            ((half, width), BF),
            ((8, width), F32),
            ((half, width), BF),
            ((half, n_qkv), BF),
            ((half, n_qkv), BF),
            ((2 * heads, half, half), F32),
            ((half, n_att), BF),
            ((half, n_att), BF),
        ],
        [lengths, normed1, *mod_pieces, *qkv_ws, *bias_ws, *out_ws],
        [pltpu.VMEM((8, ada_cols), F32)],
    )
    part1_other = swap(part1, "tensor", 2)

    att_far, att_core = pad_lanes(2 * n_att), pad_lanes(n_att)
    grad_a, grad_b, low_grad, pack1, chunks1, fc2_sum, pick = call(
        order,
        lambda *refs: early_back_kernel(frames, n_dp, *refs),
        "early_back",
        2.0,
        [
            ((half, hidden), F32),
            ((half, hidden), F32),
            ((half, width), BF),
            ((half, att_far + wide), BF),
            ((half, wide), BF),
            ((1, width), F32),
            ((part // 2, width), BF),
        ],
        [lengths, mods, cot, *down_ws, low1, att_a, att_b],
    )
    far1 = swap(pack1, "dp", 2)
    grad_y = swap(low_grad, "dp", 1)
    grad_f = swap(low_grad, "dp", 4)

    part3, act, pre_own, low2, branch1, normed2, inv2, pre_sums = call(
        order,
        lambda *refs: mlp_kernel(spots, *refs),
        "mlp",
        3.0,
        [
            ((half, width), BF),
            ((half, 2 * hidden), BF),
            ((half, hidden), BF),
            ((half, width), BF),
            ((half, width), F32),
            ((half, width), F32),
            ((half, 1), F32),
            ((2, hidden), F32),
        ],
        [tok, part1, part1_other, mods, *up_ws, *bias_ws, grad_a, grad_b],
    )
    part3_other = swap(part3, "tensor", 2)
    rows_y = swap(behind(low2, grad_y), "dp", 1)
    rows_f = swap(low2, "dp", 4)

    def forward(name, spans, sources, us=0.02):
        outs = [((half, sum(size for _, _, size in parts)), BF) for parts in spans]
        outs = call(
            order, lambda *refs: forward_kernel(spans, *refs), name, us, outs, sources
        )
        return [swap(out, "tensor", 1) for out in outs]

    def first_grads(name, products, args):
        cols = sum(p[2] for p in products)
        scratch = [pltpu.VMEM((part, 4 * half), BF)] * len(products)
        split, outs = None, [((part, cols), F32)]
        if n_dp == 8:
            split, outs = (0, 2), [((chunk, cols), F32), ((chunk, cols), BF)] * 2
        return call(
            order,
            lambda *refs: weight_kernel(n_dp, split, products, len(args), *refs),
            name,
            0.02,
            outs,
            args,
            scratch,
        )

    def add(name, widths, stay, *others):
        return call(
            order,
            lambda *refs: add_kernel(widths, len(others), *refs),
            name,
            0.02,
            [((chunk, w), F32) for w in widths],
            [stay, *others],
        )

    def halve_all(grad, done):
        for b in range((n_dp - 1).bit_length()):
            if b not in done:
                my_bit = (d_rank >> b) & 1
                grad = grad.reshape(grad.shape[0] // 2, 2, chunk, grad.shape[2])
                send = lax.dynamic_index_in_dim(grad, 1 - my_bit, 1, keepdims=False).astype(BF)
                stay = lax.dynamic_index_in_dim(grad, my_bit, 1, keepdims=False)
                grad = stay + swap(send, "dp", 1 << b).astype(F32)
        return grad[0]

    (part2,) = call(
        order,
        mlp_tail_kernel,
        "mlp_tail",
        1.0,
        [((half, width), BF)],
        [act, *down_ws],
    )
    part2_other = swap(behind(part2, far1), "tensor", 2)
    grad_yf = swap(behind(grad_f, part2), "dp", 1)

    part4, mid_grad, low_back, stacked, back_sums = call(
        order,
        lambda *refs: attention_back_kernel(frames, *refs),
        "attention_back",
        5.0,
        [
            ((half, width), BF),
            ((half, width), F32),
            ((half, width), BF),
            ((half, 2 * pad_lanes(n_qkv)), BF),
            ((8, width), F32),
        ],
        [
            lengths, part3, part3_other, mods, normed2, inv2, branch1, cot,
            *out_ws, *qkv_ws, saved_a, saved_b, probs,
        ],
        also=[grad_f],
    )
    part4_other = swap(part4, "tensor", 2)
    s_wide = pad_lanes(n_qkv)
    pack3, chunks3 = call(
        order,
        lambda *refs: pack_back_kernel(n_dp, *refs),
        "pack_back",
        0.02,
        [((half, 2 * s_wide + wide), BF), ((half, wide), BF)],
        [low_back, stacked],
        free=True,
    )
    far3 = swap(pack3, "dp", 2)

    def remake(name, normed, grads, own, before, last, span=None, us=0.02):
        outs = [((part // 2, hidden), F32)] * 2
        if last and n_dp == 8:
            outs = [((chunk, 2 * hidden), F32), ((chunk, 2 * hidden), BF)]
        return call(
            order,
            lambda *refs: remake_kernel(
                n_dp, spots, bool(own), bool(before), last, len(normed), span, *refs
            ),
            name,
            us,
            outs,
            [pick, up_weight, down_weight, bias_row, *normed, *grads, *own, *before],
            limit=40,
        )

    result, gate2_sum = call(
        order,
        lambda *refs: output_kernel(frames, spots, *refs),
        "output",
        2.0,
        [((half, width), BF), ((1, width), F32)],
        [lengths, tok, part2, part2_other, bias_row, mods, branch1, cot],
    )
    rows_yf = swap(behind(rows_f, gate2_sum), "dp", 1)
    sums2 = remake(
        "remake_near",
        [low2, rows_y, rows_f],
        [low_grad, grad_y, grad_f],
        [act, pre_own],
        [],
        False,
        us=1.0,
    )
    (grads_core,) = call(
        order,
        rows_kernel,
        "rows_grad",
        0.02,
        [((4 * half, width), BF)],
        [low_grad, grad_y, grad_f, grad_yf],
    )
    grads_other = swap(grads_core, "tensor", 1)
    both, sums = call(
        order,
        lambda *refs: input_back_kernel(frames, *refs),
        "input_back",
        0.02,
        [((half, 2 * width), BF), ((16, width), F32)],
        [
            lengths, part4, part4_other, mods, normed1, inv1, mid_grad, cot,
            back_sums, gate2_sum, fc2_sum, pre_sums, result,
        ],
    )
    sums_other = swap(sums, "tensor", 1)
    (rows_core,) = call(
        order,
        rows_kernel,
        "rows_norm",
        3.0,
        [((4 * half, width), BF)],
        [low2, rows_y, rows_f, rows_yf],
        also=[sums_other],
    )
    rows_other = swap(rows_core, "tensor", 1)

    layout, at = {}, 0
    for name, size in (
        ("mod", ada_cols), ("fc2", width), ("proj", width), ("fc1", hidden), ("stack", n_qkv),
        ("cond", width), ("label", 128),
    ):
        layout[name] = (at, size)
        at += pad_lanes(size)
    (vector,) = call(
        order,
        lambda *refs: vector_kernel(layout, *refs),
        "vector",
        0.02,
        [((1, at), F32)],
        [labels, sums, sums_other, cond],
    )

    def stack(name, value, flip, us=0.02):
        n, cols = value.shape
        other = swap(value, "dp", flip)
        return call(order, stack_kernel, name, us, [((2 * n, cols), F32)], [value, other])[0]

    def mlp_grads(stay, other):
        if n_dp == 8:
            return add("mlp_add", [hidden] * 2, stay, other)
        return [halve_all(g.reshape(n_dp // 4, chunk, hidden), [0, 2]) for g in (stay, other)]

    sums2 = remake("remake_yf", [rows_yf], [grad_yf], [], sums2, False)
    flips = [4, 1] + [1 << b for b in range(3, (n_dp - 1).bit_length())] + [2]
    mixed3, mixed1 = forward(
        "forward3",
        [
            [(0, s_wide, s_wide), (0, 2 * s_wide, wide), (1, s_wide, s_wide), (2, 0, wide)],
            [(3, n_att, att_core), (3, att_far, wide), (4, n_att, att_core), (5, 0, wide)],
        ],
        [far3, pack3, chunks3, far1, pack1, chunks1],
        us=3.0,
    )
    vector = stack("stack0", vector, flips[0], us=8.0)
    n_mix3 = s_wide + wide
    n_mix1 = att_core + wide
    left_qkv = ((1, 0), (7, n_mix1 + att_core), (2, att_far), (7, att_core))
    right_qkv = ((3, 0), (6, n_mix3), (5, 0), (6, 0))
    left_out = ((4, 0), (6, n_mix3 + s_wide), (5, 2 * s_wide), (6, s_wide))
    right_out = ((0, 0), (7, n_mix1), (2, 0), (7, 0))
    qkv_grad = first_grads(
        "qkv_grad",
        [(left_qkv, right_qkv, n_qkv), (left_out, right_out, n_att)],
        [pack1, chunks1, far1, pack3, chunks3, far3, mixed3, mixed1],
    )
    if n_dp == 8:
        far_other = swap(qkv_grad[1], "dp", 1)
    for i, flip in enumerate(flips[1:-1]):
        vector = stack("stack%d" % (i + 1), vector, flip)
    core_args = ([rows_other], [grads_other], [])
    sums2 = remake("remake_core0", *core_args, sums2, False, (0, 2 * half), us=2.0)
    mlp_grad = remake("remake_core1", *core_args, sums2, True, (2 * half, 4 * half))
    mlp_grad = (mlp_grad[0], swap(mlp_grad[1], "dp", 2) if n_dp == 8 else mlp_grad[1])
    both_other = swap(behind(both, mlp_grad[0]), "tensor", 1)
    if n_dp == 8:
        stay_far, send_far, stay_near, send_near = qkv_grad
        near_other = swap(send_near, "dp", 1)
        (send_far,) = call(
            order,
            halve_kernel,
            "qkv_halve",
            0.02,
            [(send_far.shape, BF)],
            [stay_far, far_other],
        )
        qkv_grad = stay_near, near_other, swap(send_far, "dp", 4)
    vector = stack("stack_last", vector, flips[-1])
    ada_grad, ada_bias_grad, qv_grad, proj_grad, fc1_grad, fc2_grad, stay, send, cond_cols, labels_all = call(
        order,
        lambda *refs: gathered_kernel(layout, n_dp, chunk, flips, *refs),
        "gathered",
        5.0,
        [((chunk, ada_cols), F32)]
        + [((n,), F32) for n in (ada_cols, qv_bias.shape[0], width, hidden, width)]
        + [((n_dp, 2 * pad_lanes(columns)), F32)] * 2
        + [((n_dp, columns), F32), ((n_dp, 128), F32)],
        [ada_weight.T, vector],
        [pltpu.VMEM((n_dp, at), F32)],
    )
    result, tokens_grad = call(
        order, join_kernel, "join", 0.02, [((rows, width), BF)] * 2, [both, both_other]
    )
    result, tokens_grad = result.reshape(tokens.shape), tokens_grad.reshape(tokens.shape)
    mine, send = call(
        order,
        middle_kernel,
        "middle",
        0.02,
        [((n_dp, columns), F32)] * 2,
        [stay, swap(send, "tensor", 1)],
    )
    (table_grad,) = call(
        order,
        table_kernel,
        "table",
        0.02,
        [((columns, n_classes), F32)],
        [mine, swap(send, "tensor", 2), cond_cols, labels_all],
    )
    down_grad, up_grad = mlp_grads(*mlp_grad)
    if n_dp == 8:
        qkv_grad, out_grad = add("qkv_add", [n_qkv, n_att], *qkv_grad)
    else:
        grad = halve_all(qkv_grad[0].reshape(n_dp // 2, chunk, -1), [1])
        qkv_grad, out_grad = grad[:, :n_qkv], grad[:, n_qkv:]
    return (
        result,
        tokens_grad,
        qkv_grad,
        out_grad,
        up_grad,
        down_grad,
        ada_grad,
        table_grad.T,
        qv_grad,
        proj_grad,
        fc1_grad,
        fc2_grad,
        ada_bias_grad,
    )


def solution(mesh):
    placed = (
        P("dp", None, None, None),
        P("dp"),
        P("dp"),
        P("dp"),
        P(None, "tensor"),
        P(None, "tensor"),
        P("tensor"),
        P(None, "tensor"),
        P("tensor"),
        P(None, "tensor"),
        P(),
        P(None, "tensor"),
        P("tensor"),
        P(None, "tensor"),
        P(),
        P("dp", None, None, None),
    )
    return jax.shard_map(
        shards,
        mesh=mesh,
        in_specs=placed,
        out_specs=(
            P("dp", None, None, None),
            P("dp", None, None, None),
            P("dp", "tensor"),
            P("dp", "tensor"),
            P("dp", "tensor"),
            P("dp", "tensor"),
            P("dp", "tensor"),
            P(None, "tensor"),
            P("tensor"),
            P(),
            P("tensor"),
            P(),
            P("tensor"),
        ),
        check_vma=False,
    )
```

```python
import math

import jax
import jax.numpy as jnp
import numpy as np
from jax import lax
from jax.experimental import pallas as pl
from jax.experimental.pallas import tpu as pltpu
from jax.sharding import PartitionSpec as P

HEAD_DIM = 72
BF = jnp.bfloat16
F32 = jnp.float32


def dot(left, right):
    return jnp.dot(left, right, preferred_element_type=F32)


def dot_trans(left, right):
    return lax.dot_general(left, right, (((1,), (1,)), ((), ())), preferred_element_type=F32)


def dot_rows(left, right):
    return lax.dot_general(left, right, (((0,), (0,)), ((), ())), preferred_element_type=F32)


def swap(value, axis, flip):
    size = lax.axis_size(axis)
    return lax.ppermute(value, axis, [(i, i ^ flip) for i in range(size)])


def call(order, body, name, us, outs, args, scratch=(), also=(), limit=24, free=False):
    specs = [
        pl.BlockSpec(
            memory_space=pltpu.SMEM if a.dtype == jnp.int32 else pltpu.VMEM
        )
        for a in args
    ]
    marks = [*(order[:1] if free else order), *also]
    specs += [pl.BlockSpec(memory_space=pl.ANY)] * len(marks)
    n_args, n_outs = len(args), len(outs)
    first_out = n_args + len(marks)

    def whole(*refs):
        body(*refs[:n_args], *refs[first_out : first_out + n_outs], *refs[first_out + n_outs + 1 :])
        refs[first_out + n_outs][...] = jnp.zeros((8, 128), F32)

    *results, mark = pl.pallas_call(
        whole,
        out_shape=[jax.ShapeDtypeStruct(s, d) for s, d in [*outs, ((8, 128), F32)]],
        in_specs=specs,
        out_specs=[pl.BlockSpec(memory_space=pltpu.VMEM)] * (n_outs + 1),
        scratch_shapes=list(scratch),
        compiler_params=pltpu.CompilerParams(vmem_limit_bytes=limit << 20),
        cost_estimate=pl.CostEstimate(
            flops=int(us * 1.1e9), bytes_accessed=1024, transcendentals=0
        ),
        name=name,
    )(*args, *marks)
    if not free:
        order.clear()
    order.append(mark)
    return results


def behind(value, *others):
    return lax.optimization_barrier((value, *others))[0]


def pad_lanes(width):
    return -(-width // 128) * 128


def standardize(value):
    center = value - jnp.mean(value, axis=-1, keepdims=True)
    spread = jnp.mean(center * center, axis=-1, keepdims=True)
    inv = lax.rsqrt(spread + 1e-06)
    return center * inv, inv


def standardize_back(grad, scale, normed, inv):
    g = grad * (1.0 + scale)
    return (
        g
        - jnp.mean(g, axis=-1, keepdims=True)
        - normed * jnp.mean(g * normed, axis=-1, keepdims=True)
    ) * inv


def gelu_pair(value):
    k, c = math.sqrt(2.0 / math.pi), 0.044715
    square = value * value
    h = 0.5 + 0.5 * jnp.tanh(value * (k + (k * c) * square))
    steep = value * (2.0 * k + (6.0 * k * c) * square)
    return value * h, h * (1.0 + (1.0 - h) * steep)


def row_part(ref, spots, name):
    at, size = spots[name]
    return ref[:, at : at + size].astype(F32)


def column_sum(value):
    return jnp.sum(value, axis=0, keepdims=True)


def kept_rows(length_ref, half, frames):
    frame = lax.broadcasted_iota(jnp.int32, (half, 1), 0) % frames
    return frame < length_ref[0]


def split_chunks(value, n_dp, bit):
    r = value.shape[1] // n_dp
    low, high = (
        jnp.concatenate(
            [value[:, i * r : i * r + r] for i in range(n_dp) if (i >> bit) & 1 == side], axis=1
        )
        for side in range(2)
    )
    mine_low = ((lax.axis_index("dp") >> bit) & 1) == 0
    return jnp.where(mine_low, low, high), jnp.where(mine_low, high, low)


def clock_kernel(spots, times, row, clock):
    freqs = row_part(row, spots, "freqs")
    angles = jnp.full(freqs.shape, times[0], jnp.int32).astype(F32) * freqs
    clock[...] = jnp.concatenate([jnp.cos(angles), jnp.sin(angles)], axis=1)


def start_kernel(tokens, cotangent, normed, inv, tok_half, cot_half):
    half = tok_half.shape[0]
    rows = pl.ds(pl.multiple_of((lax.axis_index("tensor") & 1) * half, half), half)
    tok_half[...] = tokens[rows, :]
    cot_half[...] = cotangent[rows, :]
    normed[...], inv[...] = standardize(tok_half[...].astype(F32))


def modulation_kernel(spots, e0, e1, e2, e3, clock, weight, bias, cond_out, part, rows):
    rank = lax.axis_index("tensor")
    for flip, piece in enumerate((e0, e1, e2, e3)):
        rows[pl.ds(rank ^ flip, 1), :] = piece[...].astype(F32)
    cond = clock[...] + jnp.concatenate([rows[i : i + 1, :] for i in range(4)], axis=1)
    cond_out[...] = cond
    act = (cond / (1.0 + jnp.exp(-cond))).astype(BF)
    act = jnp.broadcast_to(act, (16, act.shape[1]))
    part[...] = dot_trans(act, weight[...])[0:1, :] + row_part(bias, spots, "ada")


def split_heads(qkv, heads):
    at = lambda h, j: (3 * h + j) * HEAD_DIM
    return [
        tuple(qkv[:, at(h, j) : at(h, j) + HEAD_DIM].astype(BF) for j in range(3))
        for h in range(heads)
    ]


def attention_kernel(
    frames, spots, length, normed, m0, m1, m2, m3, qkv_a, qkv_b, bias_a, bias_b, out_a, out_b,
    part, mods, normed_low, saved_a, saved_b, probs_out, att_a, att_b, rows,
):
    rank = lax.axis_index("tensor")
    width = normed.shape[1]
    for flip, piece in enumerate((m0, m1, m2, m3)):
        rows[pl.ds(rank ^ flip, 1), :] = piece[...]
    cols = rows.shape[1]
    extra = cols - width
    for side in range(2):
        a, b = rows[2 * side : 2 * side + 1, :], rows[2 * side + 1 : 2 * side + 2, :]
        mods[3 * side : 3 * side + 1, :] = a[:, :width]
        mods[3 * side + 1 : 3 * side + 2, :] = jnp.concatenate([a[:, width:], b[:, :extra]], axis=1)
        mods[3 * side + 2 : 3 * side + 3, :] = b[:, extra:]
    mods[6:8, :] = jnp.zeros((2, width), F32)
    low = (normed[...] * (1.0 + mods[1:2, :]) + mods[0:1, :]).astype(BF)
    normed_low[...] = low
    half = low.shape[0]
    row_id = lax.broadcasted_iota(jnp.int32, (half, half), 0)
    col_id = lax.broadcasted_iota(jnp.int32, (half, half), 1)
    seen = ((row_id // frames) == (col_id // frames)) & ((col_id % frames) < length[0])
    factor = HEAD_DIM ** (-0.5)
    heads = out_a.shape[0] // HEAD_DIM
    heads_in = []
    for w, b, saved in ((qkv_a, bias_a, saved_a), (qkv_b, bias_b, saved_b)):
        qv = row_part(b, spots, "qv")
        zero = jnp.zeros((1, HEAD_DIM), F32)
        pieces = [
            piece
            for h in range(heads)
            for piece in (
                qv[:, 2 * h * HEAD_DIM : (2 * h + 1) * HEAD_DIM],
                zero,
                qv[:, (2 * h + 1) * HEAD_DIM : (2 * h + 2) * HEAD_DIM],
            )
        ]
        qkv = dot_trans(low, w[...]) + jnp.concatenate(pieces, axis=1)
        saved[...] = qkv.astype(BF)
        heads_in += split_heads(qkv, heads)
    all_scores = [dot_trans(q, k) for q, k, _ in heads_in]
    all_probs = []
    for i, scores in enumerate(all_scores):
        scores = jnp.where(seen, scores * factor, -1e30)
        raised = jnp.exp(scores - jnp.max(scores, axis=-1, keepdims=True))
        probs = raised / jnp.sum(raised, axis=-1, keepdims=True)
        probs_out[i] = probs
        all_probs.append(probs.astype(BF))
    outs = [dot(probs, v) for probs, (_, _, v) in zip(all_probs, heads_in)]
    total = None
    for block, (o, att_ref) in enumerate(((out_a, att_a), (out_b, att_b))):
        for h in range(heads):
            att_ref[:, h * HEAD_DIM : (h + 1) * HEAD_DIM] = outs[block * heads + h].astype(BF)
        term = dot(att_ref[...], o[...])
        total = term if total is None else total + term
    part[...] = total.astype(BF)


def early_back_kernel(
    frames, n_dp, length, mods, cotangent, down_a, down_b, normed_low, att_a, att_b,
    grad_a, grad_b, low_out, pack_far, own_chunks, fc2_sum, pick,
):
    upstream = cotangent[...].astype(F32)
    half, width = upstream.shape
    keep = kept_rows(length, half, frames)
    low = (mods[5:6, :] * jnp.where(keep, upstream, 0.0)).astype(BF)
    low_out[...] = low
    grad_a[...] = dot(low, down_a[...])
    grad_b[...] = dot(low, down_b[...])
    fc2_sum[...] = column_sum(low.astype(F32))
    n_att = att_a.shape[1]
    part = width // 2
    mine, other = split_chunks(normed_low[...].astype(F32), n_dp, 1)
    pack_far[:, 0:n_att] = att_a[...]
    pack_far[:, n_att : 2 * n_att] = att_b[...]
    at = pad_lanes(2 * n_att)
    pack_far[:, at : at + part] = other.astype(BF)
    own_chunks[:, 0:part] = mine.astype(BF)
    r = width // n_dp
    feature = lax.broadcasted_iota(jnp.int32, pick.shape, 1)
    column = lax.broadcasted_iota(jnp.int32, pick.shape, 0)
    target = column + (lax.axis_index("dp") & 5) * r
    ahead = 0
    for k in range(1, n_dp // 4):
        now = ((k & 1) << 1) + ((k >> 1) << 3) - k
        target = target + jnp.where(column >= k * r, (now - ahead) * r, 0)
        ahead = now
    pick[...] = jnp.where(feature == target, 1.0, 0.0).astype(BF)


def mlp_kernel(
    spots, tokens, part1, part1_other, mods, up_a, up_b, fc1_a, fc1_b, grad_a, grad_b,
    part3, act_out, pre_out, low_out, branch_out, normed_out, inv_out, sums,
):
    branch = part1[...].astype(F32) + part1_other[...].astype(F32) + row_part(fc1_a, spots, "proj")
    branch_out[...] = branch
    mid = tokens[...].astype(F32) + mods[2:3, :] * branch
    normed, inv = standardize(mid)
    normed_out[...] = normed
    inv_out[...] = inv
    low = (normed * (1.0 + mods[4:5, :]) + mods[3:4, :]).astype(BF)
    low_out[...] = low
    cols = up_a.shape[1]
    blocks = ((up_a, fc1_a, grad_a), (up_b, fc1_b, grad_b))
    hidden = [dot(low, u[...]) + row_part(b, spots, "fc1") for u, b, _ in blocks]
    pres = []
    for block, (value, (_, _, g)) in enumerate(zip(hidden, blocks)):
        act, slope = gelu_pair(value)
        act_out[:, block * cols : (block + 1) * cols] = act.astype(BF)
        pre = (g[...] * slope).astype(BF)
        if block == 0:
            pre_out[...] = pre
        sums[block : block + 1, :] = column_sum(pre.astype(F32))
        pres.append(pre)
    part3[...] = (dot_trans(pres[0], up_a[...]) + dot_trans(pres[1], up_b[...])).astype(BF)


def mlp_tail_kernel(act, down_a, down_b, part2):
    cols = down_a.shape[1]
    part2[...] = (
        dot_trans(act[:, 0:cols], down_a[...]) + dot_trans(act[:, cols : 2 * cols], down_b[...])
    ).astype(BF)


def rows_kernel(*refs):
    half = refs[0].shape[0]
    for i, source in enumerate(refs[:-1]):
        refs[-1][i * half : (i + 1) * half, :] = source[...]


def remake_kernel(n_dp, spots, own, before, last, n_blocks, grads_rows, pick, up, down, bias, *refs):
    cols = up.shape[1]
    normed, grads, refs = refs[:n_blocks], refs[n_blocks : 2 * n_blocks], refs[2 * n_blocks :]
    if n_blocks == 1 and normed[0].shape[0] > grads_rows:
        normed, grads = [normed[0].at[0:grads_rows, :]], [grads[0].at[grads_rows : 2 * grads_rows, :]]
    down_sum, up_sum = 0.0, 0.0
    if own:
        act_own, pre_own, refs = refs[0][:, 0:cols], refs[1][...], refs[2:]
    if before:
        down_sum, up_sum, refs = refs[0][...], refs[1][...], refs[2:]
    joined = lambda parts: parts[0] if len(parts) == 1 else jnp.concatenate(parts, axis=0)
    n_new, g_new = (joined([ref[...] for ref in v[int(own) :]]) for v in (normed, grads))
    act, slope = gelu_pair(dot(n_new, up[...]) + row_part(bias, spots, "fc1"))
    act, pre = act.astype(BF), (dot(g_new, down[...]) * slope).astype(BF)
    if own:
        n_new, g_new = joined([normed[0][...], n_new]), joined([grads[0][...], g_new])
        act, pre = joined([act_own, act]), joined([pre_own, pre])
    down_sum = down_sum + dot(dot_trans(pick[...], g_new).astype(BF), act)
    up_sum = up_sum + dot(dot_trans(pick[...], n_new).astype(BF), pre)
    if last and n_dp == 8:
        stay, send = refs
        r = down_sum.shape[0] // 2
        high = ((lax.axis_index("dp") >> 1) & 1) == 1
        for i, total in enumerate((down_sum, up_sum)):
            one, two = total[:r, :], total[r:, :]
            stay[:, i * cols : (i + 1) * cols] = jnp.where(high, two, one)
            send[:, i * cols : (i + 1) * cols] = jnp.where(high, one, two).astype(BF)
    else:
        refs[0][...] = down_sum
        refs[1][...] = up_sum


def attention_back_kernel(
    frames, length, part3, part3_other, mods, normed, inv, branch, cotangent,
    out_a, out_b, qkv_a, qkv_b, saved_a, saved_b, probs_in,
    part4, mid_grad_out, low_out, stacked, sums,
):
    upstream = cotangent[...].astype(F32)
    half, width = upstream.shape
    keep = kept_rows(length, half, frames)
    grad = part3[...].astype(F32) + part3_other[...].astype(F32)
    norm = normed[...]
    mid_grad = jnp.where(keep, upstream, 0.0) + standardize_back(grad, mods[4:5, :], norm, inv[...])
    mid_grad_out[...] = mid_grad
    low = (mods[2:3, :] * mid_grad).astype(BF)
    low_out[...] = low
    sums[0:1, :] = column_sum(grad)
    sums[1:2, :] = column_sum(grad * norm)
    sums[2:3, :] = column_sum(mid_grad * branch[...])
    sums[3:4, :] = column_sum(low.astype(F32))
    factor = HEAD_DIM ** (-0.5)
    heads = out_a.shape[0] // HEAD_DIM
    cols = heads * 3 * HEAD_DIM
    wide = pad_lanes(cols)
    heads_in, att_grads = [], []
    for o, saved in ((out_a, saved_a), (out_b, saved_b)):
        att_grad = dot_trans(low, o[...])
        heads_in += split_heads(saved[...].astype(F32), heads)
        att_grads += [
            att_grad[:, h * HEAD_DIM : (h + 1) * HEAD_DIM].astype(BF) for h in range(heads)
        ]
    all_probs_grad = [dot_trans(ag, v) for ag, (_, _, v) in zip(att_grads, heads_in)]
    value_grads = [dot_rows(probs_in[i].astype(BF), ag) for i, ag in enumerate(att_grads)]
    all_low = []
    for i, probs_grad in enumerate(all_probs_grad):
        probs = probs_in[i]
        inner = jnp.sum(probs * probs_grad, axis=-1, keepdims=True)
        all_low.append((probs * (probs_grad - inner)).astype(BF))
    query_grads = [dot(scores_low, k) * factor for scores_low, (_, k, _) in zip(all_low, heads_in)]
    key_grads = [dot_rows(scores_low, q) * factor for scores_low, (q, _, _) in zip(all_low, heads_in)]
    total = None
    for block, w in enumerate((qkv_a, qkv_b)):
        for h in range(heads):
            i = block * heads + h
            at = block * wide + h * 3 * HEAD_DIM
            for j, piece in enumerate((query_grads[i], key_grads[i], value_grads[i])):
                stacked[:, at + j * HEAD_DIM : at + (j + 1) * HEAD_DIM] = piece.astype(BF)
        mine = stacked[:, block * wide : block * wide + cols]
        sums[4 + block : 5 + block, 0:cols] = column_sum(mine.astype(F32))
        term = dot(mine, w[...])
        total = term if total is None else total + term
    part4[...] = total.astype(BF)


def pack_back_kernel(n_dp, low, stacked, pack_far, own_chunks):
    mine, other = split_chunks(low[...].astype(F32), n_dp, 1)
    part, cols = mine.shape[1], stacked.shape[1]
    pack_far[:, 0:cols] = stacked[...]
    pack_far[:, cols : cols + part] = other.astype(BF)
    own_chunks[:, 0:part] = mine.astype(BF)


def output_kernel(
    frames, spots, length, tokens, part2, part2_other, bias, mods, branch1, cotangent,
    result, gate_sum,
):
    inputs, upstream = tokens[...].astype(F32), cotangent[...].astype(F32)
    keep = kept_rows(length, inputs.shape[0], frames)
    branch = part2[...].astype(F32) + part2_other[...].astype(F32) + row_part(bias, spots, "fc2")
    mid = inputs + mods[2:3, :] * branch1[...]
    result[...] = jnp.where(keep, mid + mods[5:6, :] * branch, inputs).astype(BF)
    gate_sum[...] = column_sum(jnp.where(keep, upstream, 0.0) * branch)


def input_back_kernel(
    frames, length, part4, part4_other, mods, normed, inv, mid_grad, cotangent,
    back_sums, gate2_sum, fc2_sum, pre_sums, result, both, sums,
):
    upstream = cotangent[...].astype(F32)
    keep = kept_rows(length, upstream.shape[0], frames)
    grad = part4[...].astype(F32) + part4_other[...].astype(F32)
    norm = normed[...]
    back = standardize_back(grad, mods[1:2, :], norm, inv[...])
    width = norm.shape[1]
    both[:, :width] = result[...]
    both[:, width:] = (mid_grad[...] + back + jnp.where(keep, 0.0, upstream)).astype(BF)
    sums[0:1, :] = column_sum(grad)
    sums[1:2, :] = column_sum(grad * norm)
    sums[2:3, :] = back_sums[2:3, :]
    sums[3:5, :] = back_sums[0:2, :]
    sums[5:6, :] = gate2_sum[...]
    sums[6:7, :] = fc2_sum[...]
    sums[7:8, :] = back_sums[3:4, :]
    sums[8:10, :] = pre_sums[0:2, :]
    sums[10:12, :] = back_sums[4:6, :]
    sums[12:16, :] = jnp.zeros((4, sums.shape[1]), F32)


def vector_kernel(layout, label, mine, other, cond, vector):
    rank = lax.axis_index("tensor")
    width = mine.shape[1]
    both = mine[...] + other[...]
    upper = rank >= 2
    pick = lambda i: jnp.where(upper, both[3 + i : 4 + i, :], both[i : i + 1, :])
    cols = layout["mod"][1]
    extra = cols - width
    shift, scale, gate = pick(0), pick(1), pick(2)
    even = jnp.concatenate([shift, scale[:, :extra]], axis=1)
    odd = jnp.concatenate([scale[:, extra:], gate], axis=1)
    vector[...] = jnp.zeros(vector.shape, F32)

    def put(name, value):
        at, size = layout[name]
        vector[:, at : at + size] = value

    put("mod", jnp.where((rank & 1) == 0, even, odd).astype(BF).astype(F32))
    put("fc2", both[6:7, :])
    put("proj", both[7:8, :])
    put("fc1", (mine[8:9, :] + other[9:10, :])[:, : layout["fc1"][1]])
    put("stack", (mine[10:11, :] + other[11:12, :])[:, : layout["stack"][1]])
    put("cond", cond[...])
    put("label", jnp.full((1, 128), label[0], jnp.int32).astype(F32))


def gathered_kernel(layout, n_dp, rows_out, flips, weight, source, *refs):
    ada_grad, ada_bias, qv, proj, fc1, fc2, stay, send, cond_cols, labels, table = refs
    rank, place = lax.axis_index("tensor"), lax.axis_index("dp")
    for i in range(n_dp):
        flip = sum(f for k, f in enumerate(flips) if (i >> k) & 1)
        table[pl.ds(place ^ flip, 1), :] = source[i : i + 1, :]

    def get(name):
        at, size = layout[name]
        return table[:, at : at + size]

    sums = lambda name: column_sum(get(name))
    for name, out in (("mod", ada_bias), ("proj", proj), ("fc1", fc1), ("fc2", fc2)):
        out[...] = sums(name).reshape(out.shape)
    stack = sums("stack")
    pieces = [
        stack[:, i * HEAD_DIM : (i + 1) * HEAD_DIM]
        for i in range(stack.shape[1] // HEAD_DIM)
        if i % 3 != 1
    ]
    qv[...] = jnp.concatenate(pieces, axis=1).reshape(qv.shape)
    mod = get("mod").astype(BF)
    cond = get("cond")
    act = cond / (1.0 + jnp.exp(-cond))
    width = act.shape[1]
    mine = pltpu.roll(act, (width - place * rows_out) % width, 1)[:, :rows_out].astype(BF)
    ada_grad[...] = dot_rows(mine, mod)
    columns = cond_cols.shape[1]
    cond_part = dot(mod, weight[...])
    wide = pad_lanes(columns)
    for flip in range(4):
        out, at = (stay, send)[flip & 1], (flip >> 1) * wide
        piece = pltpu.roll(cond_part, (width - (rank ^ flip) * columns) % width, 1)[:, :columns]
        out[:, at : at + columns] = piece
    cond_cols[...] = pltpu.roll(cond, (width - rank * columns) % width, 1)[:, :columns]
    labels[...] = get("label")


def middle_kernel(stay, other, mine, send):
    columns = mine.shape[1]
    wide = pad_lanes(columns)
    mine[...] = stay[:, 0:columns] + other[:, 0:columns]
    send[...] = stay[:, wide : wide + columns] + other[:, wide : wide + columns]


def table_kernel(mine, other, cond_cols, labels, out):
    cond = cond_cols[...]
    gate = 1.0 / (1.0 + jnp.exp(-cond))
    grad = (mine[...] + other[...]) * gate * (1.0 + cond * (1.0 - gate))
    classes = lax.broadcasted_iota(jnp.int32, (cond.shape[0], out.shape[1]), 1).astype(F32)
    onehot = jnp.where(labels[:, : out.shape[1]] == classes, 1.0, 0.0)
    out[...] = lax.dot_general(
        grad,
        onehot,
        (((0,), (0,)), ((), ())),
        precision=lax.Precision.HIGHEST,
        preferred_element_type=F32,
    )


def forward_kernel(spans, *refs):
    for parts, out in zip(spans, refs[-len(spans) :]):
        at = 0
        for i, start, size in parts:
            out[:, at : at + size] = refs[i][:, start : start + size]
            at += size


def weight_kernel(n_dp, split, products, n_in, *refs):
    outs, lefts = refs[n_in : -len(products)], refs[-len(products) :]
    half = refs[0].shape[0]
    part = lefts[0].shape[0]
    r = part // (n_dp // 2)
    at = 0
    for left, (left_rows, right_rows, cols) in zip(lefts, products):
        for i, (j, start) in enumerate(left_rows):
            value = refs[j][:, start : start + part]
            left[:, i * half : (i + 1) * half] = value.astype(F32).T.astype(BF)
        right = [refs[j][:, start : start + cols] for j, start in right_rows]
        right = jnp.concatenate(right, axis=0)
        if split is None:
            outs[0][:, at : at + cols] = dot(left[...], right)
        else:
            near, far = ((lax.axis_index("dp") >> bit) & 1 for bit in split)
            for (stay, send), k in ((outs[0:2], 1 - far), (outs[2:4], far)):
                for out, side in ((stay, near), (send, 1 - near)):
                    start = pl.multiple_of((2 * k + side) * r, r)
                    out[:, at : at + cols] = dot(left[pl.ds(start, r), :], right).astype(out.dtype)
        at += cols


def halve_kernel(stay, other, send):
    send[...] = (stay[...] + other[...].astype(F32)).astype(BF)


def add_kernel(widths, n_others, stay, *refs):
    total = stay[...]
    for other in refs[:n_others]:
        total = total + other[...].astype(F32)
    at = 0
    for out, cols in zip(refs[n_others:], widths):
        out[...] = total[:, at : at + cols]
        at += cols


def join_kernel(mine, other, *outs):
    half, width = mine.shape[0], outs[0].shape[1]
    core = lax.axis_index("tensor") & 1
    for source, side in ((mine, core), (other, 1 - core)):
        rows = pl.ds(pl.multiple_of(side * half, half), half)
        for i, out in enumerate(outs):
            out[rows, :] = source[:, i * width : (i + 1) * width]


def stack_kernel(mine, other, out):
    n = mine.shape[0]
    out[0:n, :] = mine[...]
    out[n : 2 * n, :] = other[...]


def shards(
    tokens,
    lengths,
    timesteps,
    labels,
    class_table,
    ada_weight,
    ada_bias,
    qkv_weight,
    qv_bias,
    out_weight,
    proj_bias,
    up_weight,
    fc1_bias,
    down_weight,
    fc2_bias,
    cotangent,
):
    clips, patches, frames, width = tokens.shape
    assert clips == 1 and lax.axis_size("tensor") == 4
    rows = patches * frames
    half = rows // 2
    n_att = out_weight.shape[1]
    heads = n_att // HEAD_DIM
    n_qkv = qkv_weight.shape[1]
    hidden = up_weight.shape[1]
    columns = class_table.shape[1]
    ada_cols = ada_weight.shape[1]
    n_classes = class_table.shape[0]
    t_rank = lax.axis_index("tensor")
    d_rank = lax.axis_index("dp")
    n_dp = lax.axis_size("dp")
    order = []
    chunk = width // n_dp
    part = width // 2
    wide = pad_lanes(part)

    tokens2 = tokens.reshape(rows, width)
    cot2 = cotangent.reshape(rows, width)
    half_width = width // 2
    freqs = np.exp(-math.log(10000.0) * np.arange(half_width) / half_width)
    small = (
        ("ada", ada_bias), ("qv", qv_bias), ("fc1", fc1_bias), ("proj", proj_bias),
        ("fc2", fc2_bias), ("freqs", jnp.asarray(freqs, F32)),
    )
    spots, n_row = {}, 0
    for name, v in small:
        spots[name] = (n_row, v.shape[0])
        n_row += pad_lanes(v.shape[0])
    bias_row = sum(
        jnp.pad(v.astype(F32), (spots[name][0], n_row - spots[name][0] - v.shape[0]))
        for name, v in small
    ).reshape(1, n_row)

    def gather_tensor(own, *others):
        across = behind(swap(own, "tensor", 2), *others)
        return [own, swap(own, "tensor", 1), across, swap(across, "tensor", 1)]

    def pair(weight, *others):
        return weight, swap(behind(weight, *others), "tensor", 1)

    picked = lax.dynamic_slice_in_dim(class_table, labels[0], 1, 0)
    (clock,) = call(
        order,
        lambda *refs: clock_kernel(spots, *refs),
        "clock",
        5.0,
        [((1, width), F32)],
        [timesteps, bias_row],
    )
    pieces = gather_tensor(picked, clock, bias_row)
    bias_ws = pair(bias_row)
    cond, mod_part = call(
        order,
        lambda *refs: modulation_kernel(spots, *refs),
        "modulation",
        1.0,
        [((1, width), F32), ((1, ada_cols), F32)],
        [*pieces, clock, ada_weight.T, bias_row],
        [pltpu.VMEM((8, columns), F32)],
    )
    normed1, inv1, tok, cot = call(
        order,
        start_kernel,
        "start",
        1.0,
        [((half, width), F32), ((half, 1), F32), ((half, width), BF), ((half, width), BF)],
        [tokens2, cot2],
    )
    qkv_ws = pair(qkv_weight.T, pieces[1], pieces[3])
    out_ws = pair(out_weight.T, pieces[1], pieces[3])
    mod_pieces = gather_tensor(mod_part, bias_ws[1], qkv_ws[1], out_ws[1], normed1)
    up_ws = pair(up_weight, *mod_pieces)
    down_ws = pair(down_weight, *mod_pieces)

    part1, mods, low1, saved_a, saved_b, probs, att_a, att_b = call(
        order,
        lambda *refs: attention_kernel(frames, spots, *refs),
        "attention",
        4.0,
        [
            ((half, width), BF),
            ((8, width), F32),
            ((half, width), BF),
            ((half, n_qkv), BF),
            ((half, n_qkv), BF),
            ((2 * heads, half, half), F32),
            ((half, n_att), BF),
            ((half, n_att), BF),
        ],
        [lengths, normed1, *mod_pieces, *qkv_ws, *bias_ws, *out_ws],
        [pltpu.VMEM((8, ada_cols), F32)],
    )
    part1_other = swap(part1, "tensor", 2)

    att_far, att_core = pad_lanes(2 * n_att), pad_lanes(n_att)
    grad_a, grad_b, low_grad, pack1, chunks1, fc2_sum, pick = call(
        order,
        lambda *refs: early_back_kernel(frames, n_dp, *refs),
        "early_back",
        2.0,
        [
            ((half, hidden), F32),
            ((half, hidden), F32),
            ((half, width), BF),
            ((half, att_far + wide), BF),
            ((half, wide), BF),
            ((1, width), F32),
            ((part // 2, width), BF),
        ],
        [lengths, mods, cot, *down_ws, low1, att_a, att_b],
    )
    far1 = swap(pack1, "dp", 2)
    grad_y = swap(low_grad, "dp", 1)
    grad_f = swap(low_grad, "dp", 4)

    part3, act, pre_own, low2, branch1, normed2, inv2, pre_sums = call(
        order,
        lambda *refs: mlp_kernel(spots, *refs),
        "mlp",
        3.0,
        [
            ((half, width), BF),
            ((half, 2 * hidden), BF),
            ((half, hidden), BF),
            ((half, width), BF),
            ((half, width), F32),
            ((half, width), F32),
            ((half, 1), F32),
            ((2, hidden), F32),
        ],
        [tok, part1, part1_other, mods, *up_ws, *bias_ws, grad_a, grad_b],
    )
    part3_other = swap(part3, "tensor", 2)
    rows_y = swap(behind(low2, grad_y), "dp", 1)
    rows_f = swap(low2, "dp", 4)

    def forward(name, spans, sources, us=0.02):
        outs = [((half, sum(size for _, _, size in parts)), BF) for parts in spans]
        outs = call(
            order, lambda *refs: forward_kernel(spans, *refs), name, us, outs, sources
        )
        return [swap(out, "tensor", 1) for out in outs]

    def first_grads(name, products, args):
        cols = sum(p[2] for p in products)
        scratch = [pltpu.VMEM((part, 4 * half), BF)] * len(products)
        split, outs = None, [((part, cols), F32)]
        if n_dp == 8:
            split, outs = (0, 2), [((chunk, cols), F32), ((chunk, cols), BF)] * 2
        return call(
            order,
            lambda *refs: weight_kernel(n_dp, split, products, len(args), *refs),
            name,
            0.02,
            outs,
            args,
            scratch,
        )

    def add(name, widths, stay, *others):
        return call(
            order,
            lambda *refs: add_kernel(widths, len(others), *refs),
            name,
            0.02,
            [((chunk, w), F32) for w in widths],
            [stay, *others],
        )

    def halve_all(grad, done):
        for b in range((n_dp - 1).bit_length()):
            if b not in done:
                my_bit = (d_rank >> b) & 1
                grad = grad.reshape(grad.shape[0] // 2, 2, chunk, grad.shape[2])
                send = lax.dynamic_index_in_dim(grad, 1 - my_bit, 1, keepdims=False).astype(BF)
                stay = lax.dynamic_index_in_dim(grad, my_bit, 1, keepdims=False)
                grad = stay + swap(send, "dp", 1 << b).astype(F32)
        return grad[0]

    (part2,) = call(
        order,
        mlp_tail_kernel,
        "mlp_tail",
        1.0,
        [((half, width), BF)],
        [act, *down_ws],
    )
    part2_other = swap(behind(part2, far1), "tensor", 2)
    grad_yf = swap(behind(grad_f, part2), "dp", 1)

    part4, mid_grad, low_back, stacked, back_sums = call(
        order,
        lambda *refs: attention_back_kernel(frames, *refs),
        "attention_back",
        5.0,
        [
            ((half, width), BF),
            ((half, width), F32),
            ((half, width), BF),
            ((half, 2 * pad_lanes(n_qkv)), BF),
            ((8, width), F32),
        ],
        [
            lengths, part3, part3_other, mods, normed2, inv2, branch1, cot,
            *out_ws, *qkv_ws, saved_a, saved_b, probs,
        ],
        also=[grad_f],
    )
    part4_other = swap(part4, "tensor", 2)
    (near_rows,) = call(
        order,
        rows_kernel,
        "rows_near",
        0.02,
        [((4 * half, width), BF)],
        [low2, rows_y, low_grad, grad_y],
    )
    near_other = swap(near_rows, "tensor", 1)
    s_wide = pad_lanes(n_qkv)
    pack3, chunks3 = call(
        order,
        lambda *refs: pack_back_kernel(n_dp, *refs),
        "pack_back",
        0.02,
        [((half, 2 * s_wide + wide), BF), ((half, wide), BF)],
        [low_back, stacked],
        free=True,
    )
    far3 = swap(pack3, "dp", 2)

    def remake(name, normed, grads, own, before, last, us=0.02):
        outs = [((part // 2, hidden), F32)] * 2
        if last and n_dp == 8:
            outs = [((chunk, 2 * hidden), F32), ((chunk, 2 * hidden), BF)]
        return call(
            order,
            lambda *refs: remake_kernel(
                n_dp, spots, bool(own), bool(before), last, len(normed), 2 * half, *refs
            ),
            name,
            us,
            outs,
            [pick, up_weight, down_weight, bias_row, *normed, *grads, *own, *before],
            limit=40,
        )

    result, gate2_sum = call(
        order,
        lambda *refs: output_kernel(frames, spots, *refs),
        "output",
        2.0,
        [((half, width), BF), ((1, width), F32)],
        [lengths, tok, part2, part2_other, bias_row, mods, branch1, cot],
    )
    rows_yf = swap(behind(rows_f, gate2_sum), "dp", 1)
    sums2 = remake(
        "remake_near",
        [low2, rows_y, rows_f],
        [low_grad, grad_y, grad_f],
        [act, pre_own],
        [],
        False,
        us=1.0,
    )
    both, sums = call(
        order,
        lambda *refs: input_back_kernel(frames, *refs),
        "input_back",
        10.0,
        [((half, 2 * width), BF), ((16, width), F32)],
        [
            lengths, part4, part4_other, mods, normed1, inv1, mid_grad, cot,
            back_sums, gate2_sum, fc2_sum, pre_sums, result,
        ],
    )
    sums_other = swap(sums, "tensor", 1)
    sums2 = remake("remake_core0", [near_other], [near_other], [], sums2, False, us=2.0)
    (far_rows,) = call(
        order,
        rows_kernel,
        "rows_far",
        3.0,
        [((4 * half, width), BF)],
        [rows_f, rows_yf, grad_f, grad_yf],
        also=[sums_other],
    )
    far_rows_other = swap(far_rows, "tensor", 1)

    layout, at = {}, 0
    for name, size in (
        ("mod", ada_cols), ("fc2", width), ("proj", width), ("fc1", hidden), ("stack", n_qkv),
        ("cond", width), ("label", 128),
    ):
        layout[name] = (at, size)
        at += pad_lanes(size)
    (vector,) = call(
        order,
        lambda *refs: vector_kernel(layout, *refs),
        "vector",
        0.02,
        [((1, at), F32)],
        [labels, sums, sums_other, cond],
    )

    def stack(name, value, flip, us=0.02):
        n, cols = value.shape
        other = swap(value, "dp", flip)
        return call(order, stack_kernel, name, us, [((2 * n, cols), F32)], [value, other])[0]

    def mlp_grads(stay, other):
        if n_dp == 8:
            return add("mlp_add", [hidden] * 2, stay, other)
        return [halve_all(g.reshape(n_dp // 4, chunk, hidden), [0, 2]) for g in (stay, other)]

    sums2 = remake("remake_yf", [rows_yf], [grad_yf], [], sums2, False)
    flips = [4, 1] + [1 << b for b in range(3, (n_dp - 1).bit_length())] + [2]
    mixed3, mixed1 = forward(
        "forward3",
        [
            [(0, s_wide, s_wide), (0, 2 * s_wide, wide), (1, s_wide, s_wide), (2, 0, wide)],
            [(3, n_att, att_core), (3, att_far, wide), (4, n_att, att_core), (5, 0, wide)],
        ],
        [far3, pack3, chunks3, far1, pack1, chunks1],
        us=3.0,
    )
    vector = stack("stack0", vector, flips[0], us=8.0)
    n_mix3 = s_wide + wide
    n_mix1 = att_core + wide
    left_qkv = ((1, 0), (7, n_mix1 + att_core), (2, att_far), (7, att_core))
    right_qkv = ((3, 0), (6, n_mix3), (5, 0), (6, 0))
    left_out = ((4, 0), (6, n_mix3 + s_wide), (5, 2 * s_wide), (6, s_wide))
    right_out = ((0, 0), (7, n_mix1), (2, 0), (7, 0))
    qkv_grad = first_grads(
        "qkv_grad",
        [(left_qkv, right_qkv, n_qkv), (left_out, right_out, n_att)],
        [pack1, chunks1, far1, pack3, chunks3, far3, mixed3, mixed1],
    )
    if n_dp == 8:
        far_other = swap(qkv_grad[1], "dp", 1)
    for i, flip in enumerate(flips[1:-1]):
        vector = stack("stack%d" % (i + 1), vector, flip, us=2.0)
    mlp_grad = remake("remake_core1", [far_rows_other], [far_rows_other], [], sums2, True)
    mlp_grad = (mlp_grad[0], swap(mlp_grad[1], "dp", 2) if n_dp == 8 else mlp_grad[1])
    both_other = swap(behind(both, mlp_grad[0]), "tensor", 1)
    if n_dp == 8:
        stay_far, send_far, stay_near, send_near = qkv_grad
        near_other = swap(send_near, "dp", 1)
        (send_far,) = call(
            order,
            halve_kernel,
            "qkv_halve",
            0.02,
            [(send_far.shape, BF)],
            [stay_far, far_other],
        )
        qkv_grad = stay_near, near_other, swap(send_far, "dp", 4)
    vector = stack("stack_last", vector, flips[-1])
    ada_grad, ada_bias_grad, qv_grad, proj_grad, fc1_grad, fc2_grad, stay, send, cond_cols, labels_all = call(
        order,
        lambda *refs: gathered_kernel(layout, n_dp, chunk, flips, *refs),
        "gathered",
        5.0,
        [((chunk, ada_cols), F32)]
        + [((n,), F32) for n in (ada_cols, qv_bias.shape[0], width, hidden, width)]
        + [((n_dp, 2 * pad_lanes(columns)), F32)] * 2
        + [((n_dp, columns), F32), ((n_dp, 128), F32)],
        [ada_weight.T, vector],
        [pltpu.VMEM((n_dp, at), F32)],
    )
    result, tokens_grad = call(
        order, join_kernel, "join", 0.02, [((rows, width), BF)] * 2, [both, both_other]
    )
    result, tokens_grad = result.reshape(tokens.shape), tokens_grad.reshape(tokens.shape)
    mine, send = call(
        order,
        middle_kernel,
        "middle",
        0.02,
        [((n_dp, columns), F32)] * 2,
        [stay, swap(send, "tensor", 1)],
    )
    (table_grad,) = call(
        order,
        table_kernel,
        "table",
        0.02,
        [((columns, n_classes), F32)],
        [mine, swap(send, "tensor", 2), cond_cols, labels_all],
    )
    if n_dp == 8:
        qkv_grad, out_grad = add("qkv_add", [n_qkv, n_att], *qkv_grad)
    else:
        grad = halve_all(qkv_grad[0].reshape(n_dp // 2, chunk, -1), [1])
        qkv_grad, out_grad = grad[:, :n_qkv], grad[:, n_qkv:]
    down_grad, up_grad = mlp_grads(*mlp_grad)
    return (
        result,
        tokens_grad,
        qkv_grad,
        out_grad,
        up_grad,
        down_grad,
        ada_grad,
        table_grad.T,
        qv_grad,
        proj_grad,
        fc1_grad,
        fc2_grad,
        ada_bias_grad,
    )


def solution(mesh):
    placed = (
        P("dp", None, None, None),
        P("dp"),
        P("dp"),
        P("dp"),
        P(None, "tensor"),
        P(None, "tensor"),
        P("tensor"),
        P(None, "tensor"),
        P("tensor"),
        P(None, "tensor"),
        P(),
        P(None, "tensor"),
        P("tensor"),
        P(None, "tensor"),
        P(),
        P("dp", None, None, None),
    )
    return jax.shard_map(
        shards,
        mesh=mesh,
        in_specs=placed,
        out_specs=(
            P("dp", None, None, None),
            P("dp", None, None, None),
            P("dp", "tensor"),
            P("dp", "tensor"),
            P("dp", "tensor"),
            P("dp", "tensor"),
            P("dp", "tensor"),
            P(None, "tensor"),
            P("tensor"),
            P(),
            P("tensor"),
            P(),
            P("tensor"),
        ),
        check_vma=False,
    )
```

```python
import math

import jax
import jax.numpy as jnp
import numpy as np
from jax import lax
from jax.experimental import pallas as pl
from jax.experimental.pallas import tpu as pltpu
from jax.sharding import PartitionSpec as P

HEAD_DIM = 72
BF = jnp.bfloat16
F32 = jnp.float32


def dot(left, right):
    return jnp.dot(left, right, preferred_element_type=F32)


def dot_trans(left, right):
    return lax.dot_general(left, right, (((1,), (1,)), ((), ())), preferred_element_type=F32)


def dot_rows(left, right):
    return lax.dot_general(left, right, (((0,), (0,)), ((), ())), preferred_element_type=F32)


def swap(value, axis, flip):
    size = lax.axis_size(axis)
    return lax.ppermute(value, axis, [(i, i ^ flip) for i in range(size)])


def call(order, body, name, us, outs, args, scratch=(), also=(), limit=24, free=False):
    specs = [
        pl.BlockSpec(
            memory_space=pltpu.SMEM if a.dtype == jnp.int32 else pltpu.VMEM
        )
        for a in args
    ]
    marks = [*(order[:1] if free else order), *also]
    specs += [pl.BlockSpec(memory_space=pl.ANY)] * len(marks)
    n_args, n_outs = len(args), len(outs)
    first_out = n_args + len(marks)

    def whole(*refs):
        body(*refs[:n_args], *refs[first_out : first_out + n_outs], *refs[first_out + n_outs + 1 :])
        refs[first_out + n_outs][...] = jnp.zeros((8, 128), F32)

    *results, mark = pl.pallas_call(
        whole,
        out_shape=[jax.ShapeDtypeStruct(s, d) for s, d in [*outs, ((8, 128), F32)]],
        in_specs=specs,
        out_specs=[pl.BlockSpec(memory_space=pltpu.VMEM)] * (n_outs + 1),
        scratch_shapes=list(scratch),
        compiler_params=pltpu.CompilerParams(vmem_limit_bytes=limit << 20),
        cost_estimate=pl.CostEstimate(
            flops=int(us * 1.1e9), bytes_accessed=1024, transcendentals=0
        ),
        name=name,
    )(*args, *marks)
    if not free:
        order.clear()
    order.append(mark)
    return results


def behind(value, *others):
    return lax.optimization_barrier((value, *others))[0]


def pad_lanes(width):
    return -(-width // 128) * 128


def standardize(value):
    center = value - jnp.mean(value, axis=-1, keepdims=True)
    spread = jnp.mean(center * center, axis=-1, keepdims=True)
    inv = lax.rsqrt(spread + 1e-06)
    return center * inv, inv


def standardize_back(grad, scale, normed, inv):
    g = grad * (1.0 + scale)
    return (
        g
        - jnp.mean(g, axis=-1, keepdims=True)
        - normed * jnp.mean(g * normed, axis=-1, keepdims=True)
    ) * inv


def gelu_pair(value):
    k, c = math.sqrt(2.0 / math.pi), 0.044715
    square = value * value
    h = 0.5 + 0.5 * jnp.tanh(value * (k + (k * c) * square))
    steep = value * (2.0 * k + (6.0 * k * c) * square)
    return value * h, h * (1.0 + (1.0 - h) * steep)


def row_part(ref, spots, name):
    at, size = spots[name]
    return ref[:, at : at + size].astype(F32)


def column_sum(value):
    return jnp.sum(value, axis=0, keepdims=True)


def kept_rows(length_ref, half, frames):
    frame = lax.broadcasted_iota(jnp.int32, (half, 1), 0) % frames
    return frame < length_ref[0]


def split_chunks(value, n_dp, bit):
    r = value.shape[1] // n_dp
    low, high = (
        jnp.concatenate(
            [value[:, i * r : i * r + r] for i in range(n_dp) if (i >> bit) & 1 == side], axis=1
        )
        for side in range(2)
    )
    mine_low = ((lax.axis_index("dp") >> bit) & 1) == 0
    return jnp.where(mine_low, low, high), jnp.where(mine_low, high, low)


def clock_kernel(spots, times, row, clock):
    freqs = row_part(row, spots, "freqs")
    angles = jnp.full(freqs.shape, times[0], jnp.int32).astype(F32) * freqs
    clock[...] = jnp.concatenate([jnp.cos(angles), jnp.sin(angles)], axis=1)


def start_kernel(tokens, cotangent, normed, inv, tok_half, cot_half):
    half = tok_half.shape[0]
    rows = pl.ds(pl.multiple_of((lax.axis_index("tensor") & 1) * half, half), half)
    tok_half[...] = tokens[rows, :]
    cot_half[...] = cotangent[rows, :]
    normed[...], inv[...] = standardize(tok_half[...].astype(F32))


def modulation_kernel(spots, e0, e1, e2, e3, clock, weight, bias, cond_out, part, rows):
    rank = lax.axis_index("tensor")
    for flip, piece in enumerate((e0, e1, e2, e3)):
        rows[pl.ds(rank ^ flip, 1), :] = piece[...].astype(F32)
    cond = clock[...] + jnp.concatenate([rows[i : i + 1, :] for i in range(4)], axis=1)
    cond_out[...] = cond
    act = (cond / (1.0 + jnp.exp(-cond))).astype(BF)
    act = jnp.broadcast_to(act, (16, act.shape[1]))
    part[...] = dot_trans(act, weight[...])[0:1, :] + row_part(bias, spots, "ada")


def split_heads(qkv, heads):
    at = lambda h, j: (3 * h + j) * HEAD_DIM
    return [
        tuple(qkv[:, at(h, j) : at(h, j) + HEAD_DIM].astype(BF) for j in range(3))
        for h in range(heads)
    ]


def attention_kernel(
    frames, spots, length, normed, cotangent, m0, m1, m2, m3,
    qkv_a, qkv_b, bias_a, bias_b, out_a, out_b,
    part, mods, normed_low, saved_a, saved_b, probs_out, att_a, att_b, low_grad, rows,
):
    rank = lax.axis_index("tensor")
    width = normed.shape[1]
    for flip, piece in enumerate((m0, m1, m2, m3)):
        rows[pl.ds(rank ^ flip, 1), :] = piece[...]
    cols = rows.shape[1]
    extra = cols - width
    for side in range(2):
        a, b = rows[2 * side : 2 * side + 1, :], rows[2 * side + 1 : 2 * side + 2, :]
        mods[3 * side : 3 * side + 1, :] = a[:, :width]
        mods[3 * side + 1 : 3 * side + 2, :] = jnp.concatenate([a[:, width:], b[:, :extra]], axis=1)
        mods[3 * side + 2 : 3 * side + 3, :] = b[:, extra:]
    mods[6:8, :] = jnp.zeros((2, width), F32)
    low = (normed[...] * (1.0 + mods[1:2, :]) + mods[0:1, :]).astype(BF)
    normed_low[...] = low
    half = low.shape[0]
    row_id = lax.broadcasted_iota(jnp.int32, (half, half), 0)
    col_id = lax.broadcasted_iota(jnp.int32, (half, half), 1)
    seen = ((row_id // frames) == (col_id // frames)) & ((col_id % frames) < length[0])
    factor = HEAD_DIM ** (-0.5)
    heads = out_a.shape[0] // HEAD_DIM
    heads_in = []
    for w, b, saved in ((qkv_a, bias_a, saved_a), (qkv_b, bias_b, saved_b)):
        qv = row_part(b, spots, "qv")
        zero = jnp.zeros((1, HEAD_DIM), F32)
        pieces = [
            piece
            for h in range(heads)
            for piece in (
                qv[:, 2 * h * HEAD_DIM : (2 * h + 1) * HEAD_DIM],
                zero,
                qv[:, (2 * h + 1) * HEAD_DIM : (2 * h + 2) * HEAD_DIM],
            )
        ]
        qkv = dot_trans(low, w[...]) + jnp.concatenate(pieces, axis=1)
        saved[...] = qkv.astype(BF)
        heads_in += split_heads(qkv, heads)
    all_scores = [dot_trans(q, k) for q, k, _ in heads_in]
    all_probs = []
    for i, scores in enumerate(all_scores):
        scores = jnp.where(seen, scores * factor, -1e30)
        raised = jnp.exp(scores - jnp.max(scores, axis=-1, keepdims=True))
        probs = raised / jnp.sum(raised, axis=-1, keepdims=True)
        probs_out[i] = probs
        all_probs.append(probs.astype(BF))
    outs = [dot(probs, v) for probs, (_, _, v) in zip(all_probs, heads_in)]
    total = None
    for block, (o, att_ref) in enumerate(((out_a, att_a), (out_b, att_b))):
        for h in range(heads):
            att_ref[:, h * HEAD_DIM : (h + 1) * HEAD_DIM] = outs[block * heads + h].astype(BF)
        term = dot(att_ref[...], o[...])
        total = term if total is None else total + term
    part[...] = total.astype(BF)
    keep = kept_rows(length, half, frames)
    low_grad[...] = (mods[5:6, :] * jnp.where(keep, cotangent[...].astype(F32), 0.0)).astype(BF)


def early_back_kernel(
    n_dp, low_ref, down_a, down_b, normed_low, att_a, att_b,
    grad_a, grad_b, pack_far, own_chunks, fc2_sum, pick,
):
    low = low_ref[...]
    width = low.shape[1]
    grad_a[...] = dot(low, down_a[...])
    grad_b[...] = dot(low, down_b[...])
    fc2_sum[...] = column_sum(low.astype(F32))
    n_att = att_a.shape[1]
    part = width // 2
    mine, other = split_chunks(normed_low[...].astype(F32), n_dp, 1)
    pack_far[:, 0:n_att] = att_a[...]
    pack_far[:, n_att : 2 * n_att] = att_b[...]
    at = pad_lanes(2 * n_att)
    pack_far[:, at : at + part] = other.astype(BF)
    own_chunks[:, 0:part] = mine.astype(BF)
    r = width // n_dp
    feature = lax.broadcasted_iota(jnp.int32, pick.shape, 1)
    column = lax.broadcasted_iota(jnp.int32, pick.shape, 0)
    target = column + (lax.axis_index("dp") & 5) * r
    ahead = 0
    for k in range(1, n_dp // 4):
        now = ((k & 1) << 1) + ((k >> 1) << 3) - k
        target = target + jnp.where(column >= k * r, (now - ahead) * r, 0)
        ahead = now
    pick[...] = jnp.where(feature == target, 1.0, 0.0).astype(BF)


def mlp_kernel(
    spots, tokens, part1, part1_other, mods, up_a, up_b, fc1_a, fc1_b, grad_a, grad_b,
    part3, act_out, pre_out, low_out, branch_out, normed_out, inv_out, sums,
):
    branch = part1[...].astype(F32) + part1_other[...].astype(F32) + row_part(fc1_a, spots, "proj")
    branch_out[...] = branch
    mid = tokens[...].astype(F32) + mods[2:3, :] * branch
    normed, inv = standardize(mid)
    normed_out[...] = normed
    inv_out[...] = inv
    low = (normed * (1.0 + mods[4:5, :]) + mods[3:4, :]).astype(BF)
    low_out[...] = low
    cols = up_a.shape[1]
    blocks = ((up_a, fc1_a, grad_a), (up_b, fc1_b, grad_b))
    hidden = [dot(low, u[...]) + row_part(b, spots, "fc1") for u, b, _ in blocks]
    pres = []
    for block, (value, (_, _, g)) in enumerate(zip(hidden, blocks)):
        act, slope = gelu_pair(value)
        act_out[:, block * cols : (block + 1) * cols] = act.astype(BF)
        pre = (g[...] * slope).astype(BF)
        if block == 0:
            pre_out[...] = pre
        sums[block : block + 1, :] = column_sum(pre.astype(F32))
        pres.append(pre)
    part3[...] = (dot_trans(pres[0], up_a[...]) + dot_trans(pres[1], up_b[...])).astype(BF)


def mlp_tail_kernel(act, down_a, down_b, part2):
    cols = down_a.shape[1]
    part2[...] = (
        dot_trans(act[:, 0:cols], down_a[...]) + dot_trans(act[:, cols : 2 * cols], down_b[...])
    ).astype(BF)


def rows_kernel(*refs):
    half = refs[0].shape[0]
    for i, source in enumerate(refs[:-1]):
        refs[-1][i * half : (i + 1) * half, :] = source[...]


def remake_kernel(n_dp, spots, own, before, last, n_blocks, grads_rows, pick, up, down, bias, *refs):
    cols = up.shape[1]
    normed, grads, refs = refs[:n_blocks], refs[n_blocks : 2 * n_blocks], refs[2 * n_blocks :]
    if n_blocks == 1 and normed[0].shape[0] > grads_rows:
        normed, grads = [normed[0].at[0:grads_rows, :]], [grads[0].at[grads_rows : 2 * grads_rows, :]]
    down_sum, up_sum = 0.0, 0.0
    if own:
        act_own, pre_own, refs = refs[0][:, 0:cols], refs[1][...], refs[2:]
    if before:
        down_sum, up_sum, refs = refs[0][...], refs[1][...], refs[2:]
    joined = lambda parts: parts[0] if len(parts) == 1 else jnp.concatenate(parts, axis=0)
    n_new, g_new = (joined([ref[...] for ref in v[int(own) :]]) for v in (normed, grads))
    act, slope = gelu_pair(dot(n_new, up[...]) + row_part(bias, spots, "fc1"))
    act, pre = act.astype(BF), (dot(g_new, down[...]) * slope).astype(BF)
    if own:
        n_new, g_new = joined([normed[0][...], n_new]), joined([grads[0][...], g_new])
        act, pre = joined([act_own, act]), joined([pre_own, pre])
    down_sum = down_sum + dot(dot_trans(pick[...], g_new).astype(BF), act)
    up_sum = up_sum + dot(dot_trans(pick[...], n_new).astype(BF), pre)
    if last and n_dp == 8:
        stay, send = refs
        r = down_sum.shape[0] // 2
        high = ((lax.axis_index("dp") >> 1) & 1) == 1
        for i, total in enumerate((down_sum, up_sum)):
            one, two = total[:r, :], total[r:, :]
            stay[:, i * cols : (i + 1) * cols] = jnp.where(high, two, one)
            send[:, i * cols : (i + 1) * cols] = jnp.where(high, one, two).astype(BF)
    else:
        refs[0][...] = down_sum
        refs[1][...] = up_sum


def attention_back_kernel(
    frames, length, part3, part3_other, mods, normed, inv, branch, cotangent,
    out_a, out_b, qkv_a, qkv_b, saved_a, saved_b, probs_in,
    part4, mid_grad_out, low_out, stacked, sums,
):
    upstream = cotangent[...].astype(F32)
    half, width = upstream.shape
    keep = kept_rows(length, half, frames)
    grad = part3[...].astype(F32) + part3_other[...].astype(F32)
    norm = normed[...]
    mid_grad = jnp.where(keep, upstream, 0.0) + standardize_back(grad, mods[4:5, :], norm, inv[...])
    mid_grad_out[...] = mid_grad
    low = (mods[2:3, :] * mid_grad).astype(BF)
    low_out[...] = low
    sums[0:1, :] = column_sum(grad)
    sums[1:2, :] = column_sum(grad * norm)
    sums[2:3, :] = column_sum(mid_grad * branch[...])
    sums[3:4, :] = column_sum(low.astype(F32))
    factor = HEAD_DIM ** (-0.5)
    heads = out_a.shape[0] // HEAD_DIM
    cols = heads * 3 * HEAD_DIM
    wide = pad_lanes(cols)
    heads_in, att_grads = [], []
    for o, saved in ((out_a, saved_a), (out_b, saved_b)):
        att_grad = dot_trans(low, o[...])
        heads_in += split_heads(saved[...].astype(F32), heads)
        att_grads += [
            att_grad[:, h * HEAD_DIM : (h + 1) * HEAD_DIM].astype(BF) for h in range(heads)
        ]
    all_probs_grad = [dot_trans(ag, v) for ag, (_, _, v) in zip(att_grads, heads_in)]
    value_grads = [dot_rows(probs_in[i].astype(BF), ag) for i, ag in enumerate(att_grads)]
    all_low = []
    for i, probs_grad in enumerate(all_probs_grad):
        probs = probs_in[i]
        inner = jnp.sum(probs * probs_grad, axis=-1, keepdims=True)
        all_low.append((probs * (probs_grad - inner)).astype(BF))
    query_grads = [dot(scores_low, k) * factor for scores_low, (_, k, _) in zip(all_low, heads_in)]
    key_grads = [dot_rows(scores_low, q) * factor for scores_low, (q, _, _) in zip(all_low, heads_in)]
    total = None
    for block, w in enumerate((qkv_a, qkv_b)):
        for h in range(heads):
            i = block * heads + h
            at = block * wide + h * 3 * HEAD_DIM
            for j, piece in enumerate((query_grads[i], key_grads[i], value_grads[i])):
                stacked[:, at + j * HEAD_DIM : at + (j + 1) * HEAD_DIM] = piece.astype(BF)
        mine = stacked[:, block * wide : block * wide + cols]
        sums[4 + block : 5 + block, 0:cols] = column_sum(mine.astype(F32))
        term = dot(mine, w[...])
        total = term if total is None else total + term
    part4[...] = total.astype(BF)


def pack_back_kernel(n_dp, low, stacked, pack_far, own_chunks):
    mine, other = split_chunks(low[...].astype(F32), n_dp, 1)
    part, cols = mine.shape[1], stacked.shape[1]
    pack_far[:, 0:cols] = stacked[...]
    pack_far[:, cols : cols + part] = other.astype(BF)
    own_chunks[:, 0:part] = mine.astype(BF)


def output_kernel(
    frames, spots, length, tokens, part2, part2_other, bias, mods, branch1, cotangent,
    result, gate_sum,
):
    inputs, upstream = tokens[...].astype(F32), cotangent[...].astype(F32)
    keep = kept_rows(length, inputs.shape[0], frames)
    branch = part2[...].astype(F32) + part2_other[...].astype(F32) + row_part(bias, spots, "fc2")
    mid = inputs + mods[2:3, :] * branch1[...]
    result[...] = jnp.where(keep, mid + mods[5:6, :] * branch, inputs).astype(BF)
    gate_sum[...] = column_sum(jnp.where(keep, upstream, 0.0) * branch)


def input_back_kernel(
    frames, length, part4, part4_other, mods, normed, inv, mid_grad, cotangent,
    back_sums, gate2_sum, fc2_sum, pre_sums, result, both, sums,
):
    upstream = cotangent[...].astype(F32)
    keep = kept_rows(length, upstream.shape[0], frames)
    grad = part4[...].astype(F32) + part4_other[...].astype(F32)
    norm = normed[...]
    back = standardize_back(grad, mods[1:2, :], norm, inv[...])
    width = norm.shape[1]
    both[:, :width] = result[...]
    both[:, width:] = (mid_grad[...] + back + jnp.where(keep, 0.0, upstream)).astype(BF)
    sums[0:1, :] = column_sum(grad)
    sums[1:2, :] = column_sum(grad * norm)
    sums[2:3, :] = back_sums[2:3, :]
    sums[3:5, :] = back_sums[0:2, :]
    sums[5:6, :] = gate2_sum[...]
    sums[6:7, :] = fc2_sum[...]
    sums[7:8, :] = back_sums[3:4, :]
    sums[8:10, :] = pre_sums[0:2, :]
    sums[10:12, :] = back_sums[4:6, :]
    sums[12:16, :] = jnp.zeros((4, sums.shape[1]), F32)


def vector_kernel(layout, label, mine, other, cond, vector):
    rank = lax.axis_index("tensor")
    width = mine.shape[1]
    both = mine[...] + other[...]
    upper = rank >= 2
    pick = lambda i: jnp.where(upper, both[3 + i : 4 + i, :], both[i : i + 1, :])
    cols = layout["mod"][1]
    extra = cols - width
    shift, scale, gate = pick(0), pick(1), pick(2)
    even = jnp.concatenate([shift, scale[:, :extra]], axis=1)
    odd = jnp.concatenate([scale[:, extra:], gate], axis=1)
    vector[...] = jnp.zeros(vector.shape, F32)

    def put(name, value):
        at, size = layout[name]
        vector[:, at : at + size] = value

    put("mod", jnp.where((rank & 1) == 0, even, odd).astype(BF).astype(F32))
    put("fc2", both[6:7, :])
    put("proj", both[7:8, :])
    put("fc1", (mine[8:9, :] + other[9:10, :])[:, : layout["fc1"][1]])
    put("stack", (mine[10:11, :] + other[11:12, :])[:, : layout["stack"][1]])
    put("cond", cond[...])
    put("label", jnp.full((1, 128), label[0], jnp.int32).astype(F32))


def gathered_kernel(layout, n_dp, rows_out, flips, weight, source, *refs):
    ada_grad, ada_bias, qv, proj, fc1, fc2, stay, send, cond_cols, labels, table = refs
    rank, place = lax.axis_index("tensor"), lax.axis_index("dp")
    for i in range(n_dp):
        flip = sum(f for k, f in enumerate(flips) if (i >> k) & 1)
        table[pl.ds(place ^ flip, 1), :] = source[i : i + 1, :]

    def get(name):
        at, size = layout[name]
        return table[:, at : at + size]

    sums = lambda name: column_sum(get(name))
    for name, out in (("mod", ada_bias), ("proj", proj), ("fc1", fc1), ("fc2", fc2)):
        out[...] = sums(name).reshape(out.shape)
    stack = sums("stack")
    pieces = [
        stack[:, i * HEAD_DIM : (i + 1) * HEAD_DIM]
        for i in range(stack.shape[1] // HEAD_DIM)
        if i % 3 != 1
    ]
    qv[...] = jnp.concatenate(pieces, axis=1).reshape(qv.shape)
    mod = get("mod").astype(BF)
    cond = get("cond")
    act = cond / (1.0 + jnp.exp(-cond))
    width = act.shape[1]
    mine = pltpu.roll(act, (width - place * rows_out) % width, 1)[:, :rows_out].astype(BF)
    ada_grad[...] = dot_rows(mine, mod)
    columns = cond_cols.shape[1]
    cond_part = dot(mod, weight[...])
    wide = pad_lanes(columns)
    for flip in range(4):
        out, at = (stay, send)[flip & 1], (flip >> 1) * wide
        piece = pltpu.roll(cond_part, (width - (rank ^ flip) * columns) % width, 1)[:, :columns]
        out[:, at : at + columns] = piece
    cond_cols[...] = pltpu.roll(cond, (width - rank * columns) % width, 1)[:, :columns]
    labels[...] = get("label")


def middle_kernel(stay, other, mine, send):
    columns = mine.shape[1]
    wide = pad_lanes(columns)
    mine[...] = stay[:, 0:columns] + other[:, 0:columns]
    send[...] = stay[:, wide : wide + columns] + other[:, wide : wide + columns]


def table_kernel(mine, other, cond_cols, labels, out):
    cond = cond_cols[...]
    gate = 1.0 / (1.0 + jnp.exp(-cond))
    grad = (mine[...] + other[...]) * gate * (1.0 + cond * (1.0 - gate))
    classes = lax.broadcasted_iota(jnp.int32, (cond.shape[0], out.shape[1]), 1).astype(F32)
    onehot = jnp.where(labels[:, : out.shape[1]] == classes, 1.0, 0.0)
    out[...] = lax.dot_general(
        grad,
        onehot,
        (((0,), (0,)), ((), ())),
        precision=lax.Precision.HIGHEST,
        preferred_element_type=F32,
    )


def forward_kernel(spans, *refs):
    for parts, out in zip(spans, refs[-len(spans) :]):
        at = 0
        for i, start, size in parts:
            out[:, at : at + size] = refs[i][:, start : start + size]
            at += size


def weight_kernel(n_dp, split, products, n_in, *refs):
    outs, lefts = refs[n_in : -len(products)], refs[-len(products) :]
    half = refs[0].shape[0]
    part = lefts[0].shape[0]
    r = part // (n_dp // 2)
    at = 0
    for left, (left_rows, right_rows, cols) in zip(lefts, products):
        for i, (j, start) in enumerate(left_rows):
            value = refs[j][:, start : start + part]
            left[:, i * half : (i + 1) * half] = value.astype(F32).T.astype(BF)
        right = [refs[j][:, start : start + cols] for j, start in right_rows]
        right = jnp.concatenate(right, axis=0)
        if split is None:
            outs[0][:, at : at + cols] = dot(left[...], right)
        else:
            near, far = ((lax.axis_index("dp") >> bit) & 1 for bit in split)
            for (stay, send), k in ((outs[0:2], 1 - far), (outs[2:4], far)):
                for out, side in ((stay, near), (send, 1 - near)):
                    start = pl.multiple_of((2 * k + side) * r, r)
                    out[:, at : at + cols] = dot(left[pl.ds(start, r), :], right).astype(out.dtype)
        at += cols


def halve_kernel(stay, other, send):
    send[...] = (stay[...] + other[...].astype(F32)).astype(BF)


def last_kernel(near, near_other, far_other, mlp, mlp_other, qkv, out, down, up):
    cols = qkv.shape[1]
    for source, target, start in ((mlp, down, 0), (mlp, up, down.shape[1])):
        at = slice(start, start + target.shape[1])
        target[...] = source[:, at] + mlp_other[:, at].astype(F32)
    total = near[...] + near_other[...].astype(F32) + far_other[...].astype(F32)
    qkv[...] = total[:, :cols]
    out[...] = total[:, cols:]


def join_kernel(mine, other, *outs):
    half, width = mine.shape[0], outs[0].shape[1]
    core = lax.axis_index("tensor") & 1
    for source, side in ((mine, core), (other, 1 - core)):
        rows = pl.ds(pl.multiple_of(side * half, half), half)
        for i, out in enumerate(outs):
            out[rows, :] = source[:, i * width : (i + 1) * width]


def stack_kernel(mine, other, out):
    n = mine.shape[0]
    out[0:n, :] = mine[...]
    out[n : 2 * n, :] = other[...]


def shards(
    tokens,
    lengths,
    timesteps,
    labels,
    class_table,
    ada_weight,
    ada_bias,
    qkv_weight,
    qv_bias,
    out_weight,
    proj_bias,
    up_weight,
    fc1_bias,
    down_weight,
    fc2_bias,
    cotangent,
):
    clips, patches, frames, width = tokens.shape
    assert clips == 1 and lax.axis_size("tensor") == 4
    rows = patches * frames
    half = rows // 2
    n_att = out_weight.shape[1]
    heads = n_att // HEAD_DIM
    n_qkv = qkv_weight.shape[1]
    hidden = up_weight.shape[1]
    columns = class_table.shape[1]
    ada_cols = ada_weight.shape[1]
    n_classes = class_table.shape[0]
    t_rank = lax.axis_index("tensor")
    d_rank = lax.axis_index("dp")
    n_dp = lax.axis_size("dp")
    order = []
    chunk = width // n_dp
    part = width // 2
    wide = pad_lanes(part)

    tokens2 = tokens.reshape(rows, width)
    cot2 = cotangent.reshape(rows, width)
    half_width = width // 2
    freqs = np.exp(-math.log(10000.0) * np.arange(half_width) / half_width)
    small = (
        ("ada", ada_bias), ("qv", qv_bias), ("fc1", fc1_bias), ("proj", proj_bias),
        ("fc2", fc2_bias), ("freqs", jnp.asarray(freqs, F32)),
    )
    spots, n_row = {}, 0
    for name, v in small:
        spots[name] = (n_row, v.shape[0])
        n_row += pad_lanes(v.shape[0])
    bias_row = sum(
        jnp.pad(v.astype(F32), (spots[name][0], n_row - spots[name][0] - v.shape[0]))
        for name, v in small
    ).reshape(1, n_row)

    def gather_tensor(own, *others):
        across = behind(swap(own, "tensor", 2), *others)
        return [own, swap(own, "tensor", 1), across, swap(across, "tensor", 1)]

    def pair(weight, *others):
        return weight, swap(behind(weight, *others), "tensor", 1)

    picked = lax.dynamic_slice_in_dim(class_table, labels[0], 1, 0)
    (clock,) = call(
        order,
        lambda *refs: clock_kernel(spots, *refs),
        "clock",
        5.0,
        [((1, width), F32)],
        [timesteps, bias_row],
    )
    pieces = gather_tensor(picked, clock, bias_row)
    bias_ws = pair(bias_row)
    cond, mod_part = call(
        order,
        lambda *refs: modulation_kernel(spots, *refs),
        "modulation",
        1.0,
        [((1, width), F32), ((1, ada_cols), F32)],
        [*pieces, clock, ada_weight.T, bias_row],
        [pltpu.VMEM((8, columns), F32)],
    )
    normed1, inv1, tok, cot = call(
        order,
        start_kernel,
        "start",
        1.0,
        [((half, width), F32), ((half, 1), F32), ((half, width), BF), ((half, width), BF)],
        [tokens2, cot2],
    )
    qkv_ws = pair(qkv_weight.T, pieces[1], pieces[3])
    out_ws = pair(out_weight.T, pieces[1], pieces[3])
    mod_pieces = gather_tensor(mod_part, bias_ws[1], qkv_ws[1], out_ws[1], normed1)
    up_ws = pair(up_weight, *mod_pieces)
    down_ws = pair(down_weight, *mod_pieces)

    part1, mods, low1, saved_a, saved_b, probs, att_a, att_b, low_grad = call(
        order,
        lambda *refs: attention_kernel(frames, spots, *refs),
        "attention",
        4.0,
        [
            ((half, width), BF),
            ((8, width), F32),
            ((half, width), BF),
            ((half, n_qkv), BF),
            ((half, n_qkv), BF),
            ((2 * heads, half, half), F32),
            ((half, n_att), BF),
            ((half, n_att), BF),
            ((half, width), BF),
        ],
        [lengths, normed1, cot, *mod_pieces, *qkv_ws, *bias_ws, *out_ws],
        [pltpu.VMEM((8, ada_cols), F32)],
    )
    part1_other = swap(part1, "tensor", 2)

    att_far, att_core = pad_lanes(2 * n_att), pad_lanes(n_att)
    grad_a, grad_b, pack1, chunks1, fc2_sum, pick = call(
        order,
        lambda *refs: early_back_kernel(n_dp, *refs),
        "early_back",
        2.0,
        [
            ((half, hidden), F32),
            ((half, hidden), F32),
            ((half, att_far + wide), BF),
            ((half, wide), BF),
            ((1, width), F32),
            ((part // 2, width), BF),
        ],
        [low_grad, *down_ws, low1, att_a, att_b],
    )
    far1 = swap(pack1, "dp", 2)
    grad_y = swap(low_grad, "dp", 1)
    grad_f = swap(low_grad, "dp", 4)

    part3, act, pre_own, low2, branch1, normed2, inv2, pre_sums = call(
        order,
        lambda *refs: mlp_kernel(spots, *refs),
        "mlp",
        3.0,
        [
            ((half, width), BF),
            ((half, 2 * hidden), BF),
            ((half, hidden), BF),
            ((half, width), BF),
            ((half, width), F32),
            ((half, width), F32),
            ((half, 1), F32),
            ((2, hidden), F32),
        ],
        [tok, part1, part1_other, mods, *up_ws, *bias_ws, grad_a, grad_b],
    )
    part3_other = swap(part3, "tensor", 2)
    rows_y = swap(behind(low2, grad_y), "dp", 1)
    rows_f = swap(low2, "dp", 4)

    def forward(name, spans, sources, us=0.02):
        outs = [((half, sum(size for _, _, size in parts)), BF) for parts in spans]
        outs = call(
            order, lambda *refs: forward_kernel(spans, *refs), name, us, outs, sources
        )
        return [swap(out, "tensor", 1) for out in outs]

    def first_grads(name, products, args):
        cols = sum(p[2] for p in products)
        scratch = [pltpu.VMEM((part, 4 * half), BF)] * len(products)
        split, outs = None, [((part, cols), F32)]
        if n_dp == 8:
            split, outs = (0, 2), [((chunk, cols), F32), ((chunk, cols), BF)] * 2
        return call(
            order,
            lambda *refs: weight_kernel(n_dp, split, products, len(args), *refs),
            name,
            0.02,
            outs,
            args,
            scratch,
        )

    def halve_all(grad, done):
        for b in range((n_dp - 1).bit_length()):
            if b not in done:
                my_bit = (d_rank >> b) & 1
                grad = grad.reshape(grad.shape[0] // 2, 2, chunk, grad.shape[2])
                send = lax.dynamic_index_in_dim(grad, 1 - my_bit, 1, keepdims=False).astype(BF)
                stay = lax.dynamic_index_in_dim(grad, my_bit, 1, keepdims=False)
                grad = stay + swap(send, "dp", 1 << b).astype(F32)
        return grad[0]

    (part2,) = call(
        order,
        mlp_tail_kernel,
        "mlp_tail",
        1.0,
        [((half, width), BF)],
        [act, *down_ws],
    )
    part2_other = swap(behind(part2, far1), "tensor", 2)
    grad_yf = swap(behind(grad_f, part2), "dp", 1)

    part4, mid_grad, low_back, stacked, back_sums = call(
        order,
        lambda *refs: attention_back_kernel(frames, *refs),
        "attention_back",
        5.0,
        [
            ((half, width), BF),
            ((half, width), F32),
            ((half, width), BF),
            ((half, 2 * pad_lanes(n_qkv)), BF),
            ((8, width), F32),
        ],
        [
            lengths, part3, part3_other, mods, normed2, inv2, branch1, cot,
            *out_ws, *qkv_ws, saved_a, saved_b, probs,
        ],
        also=[grad_f],
    )
    part4_other = swap(part4, "tensor", 2)
    (near_rows,) = call(
        order,
        rows_kernel,
        "rows_near",
        0.02,
        [((4 * half, width), BF)],
        [low2, rows_y, low_grad, grad_y],
    )
    near_other = swap(near_rows, "tensor", 1)
    s_wide = pad_lanes(n_qkv)
    pack3, chunks3 = call(
        order,
        lambda *refs: pack_back_kernel(n_dp, *refs),
        "pack_back",
        0.02,
        [((half, 2 * s_wide + wide), BF), ((half, wide), BF)],
        [low_back, stacked],
        free=True,
    )
    far3 = swap(pack3, "dp", 2)

    def remake(name, normed, grads, own, before, last, us=0.02):
        outs = [((part // 2, hidden), F32)] * 2
        if last and n_dp == 8:
            outs = [((chunk, 2 * hidden), F32), ((chunk, 2 * hidden), BF)]
        return call(
            order,
            lambda *refs: remake_kernel(
                n_dp, spots, bool(own), bool(before), last, len(normed), 2 * half, *refs
            ),
            name,
            us,
            outs,
            [pick, up_weight, down_weight, bias_row, *normed, *grads, *own, *before],
            limit=40,
        )

    result, gate2_sum = call(
        order,
        lambda *refs: output_kernel(frames, spots, *refs),
        "output",
        2.0,
        [((half, width), BF), ((1, width), F32)],
        [lengths, tok, part2, part2_other, bias_row, mods, branch1, cot],
    )
    rows_yf = swap(behind(rows_f, gate2_sum), "dp", 1)
    sums2 = remake(
        "remake_near",
        [low2, rows_y, rows_f],
        [low_grad, grad_y, grad_f],
        [act, pre_own],
        [],
        False,
        us=1.0,
    )
    both, sums = call(
        order,
        lambda *refs: input_back_kernel(frames, *refs),
        "input_back",
        10.0,
        [((half, 2 * width), BF), ((16, width), F32)],
        [
            lengths, part4, part4_other, mods, normed1, inv1, mid_grad, cot,
            back_sums, gate2_sum, fc2_sum, pre_sums, result,
        ],
    )
    sums_other = swap(sums, "tensor", 1)
    sums2 = remake("remake_core0", [near_other], [near_other], [], sums2, False, us=2.0)
    (far_rows,) = call(
        order,
        rows_kernel,
        "rows_far",
        3.0,
        [((4 * half, width), BF)],
        [rows_f, rows_yf, grad_f, grad_yf],
        also=[sums_other],
    )
    far_rows_other = swap(far_rows, "tensor", 1)

    layout, at = {}, 0
    for name, size in (
        ("mod", ada_cols), ("fc2", width), ("proj", width), ("fc1", hidden), ("stack", n_qkv),
        ("cond", width), ("label", 128),
    ):
        layout[name] = (at, size)
        at += pad_lanes(size)
    (vector,) = call(
        order,
        lambda *refs: vector_kernel(layout, *refs),
        "vector",
        0.02,
        [((1, at), F32)],
        [labels, sums, sums_other, cond],
    )

    def stack(name, value, flip, us=0.02):
        n, cols = value.shape
        other = swap(value, "dp", flip)
        return call(order, stack_kernel, name, us, [((2 * n, cols), F32)], [value, other])[0]

    sums2 = remake("remake_yf", [rows_yf], [grad_yf], [], sums2, False)
    flips = [4, 1] + [1 << b for b in range(3, (n_dp - 1).bit_length())] + [2]
    mixed3, mixed1 = forward(
        "forward3",
        [
            [(0, s_wide, s_wide), (0, 2 * s_wide, wide), (1, s_wide, s_wide), (2, 0, wide)],
            [(3, n_att, att_core), (3, att_far, wide), (4, n_att, att_core), (5, 0, wide)],
        ],
        [far3, pack3, chunks3, far1, pack1, chunks1],
        us=3.0,
    )
    vector = stack("stack0", vector, flips[0], us=8.0)
    n_mix3 = s_wide + wide
    n_mix1 = att_core + wide
    left_qkv = ((1, 0), (7, n_mix1 + att_core), (2, att_far), (7, att_core))
    right_qkv = ((3, 0), (6, n_mix3), (5, 0), (6, 0))
    left_out = ((4, 0), (6, n_mix3 + s_wide), (5, 2 * s_wide), (6, s_wide))
    right_out = ((0, 0), (7, n_mix1), (2, 0), (7, 0))
    qkv_grad = first_grads(
        "qkv_grad",
        [(left_qkv, right_qkv, n_qkv), (left_out, right_out, n_att)],
        [pack1, chunks1, far1, pack3, chunks3, far3, mixed3, mixed1],
    )
    if n_dp == 8:
        far_other = swap(qkv_grad[1], "dp", 1)
    for i, flip in enumerate(flips[1:-1]):
        vector = stack("stack%d" % (i + 1), vector, flip, us=2.0)
    mlp_grad = remake("remake_core1", [far_rows_other], [far_rows_other], [], sums2, True)
    mlp_grad = (mlp_grad[0], swap(mlp_grad[1], "dp", 2) if n_dp == 8 else mlp_grad[1])
    both_other = swap(behind(both, mlp_grad[0]), "tensor", 1)
    if n_dp == 8:
        stay_far, send_far, stay_near, send_near = qkv_grad
        near_other = swap(send_near, "dp", 1)
        (send_far,) = call(
            order,
            halve_kernel,
            "qkv_halve",
            0.02,
            [(send_far.shape, BF)],
            [stay_far, far_other],
        )
        qkv_grad = stay_near, near_other, swap(send_far, "dp", 4)
    vector = stack("stack_last", vector, flips[-1])
    ada_grad, ada_bias_grad, qv_grad, proj_grad, fc1_grad, fc2_grad, stay, send, cond_cols, labels_all = call(
        order,
        lambda *refs: gathered_kernel(layout, n_dp, chunk, flips, *refs),
        "gathered",
        5.0,
        [((chunk, ada_cols), F32)]
        + [((n,), F32) for n in (ada_cols, qv_bias.shape[0], width, hidden, width)]
        + [((n_dp, 2 * pad_lanes(columns)), F32)] * 2
        + [((n_dp, columns), F32), ((n_dp, 128), F32)],
        [ada_weight.T, vector],
        [pltpu.VMEM((n_dp, at), F32)],
    )
    result, tokens_grad = call(
        order, join_kernel, "join", 0.02, [((rows, width), BF)] * 2, [both, both_other]
    )
    result, tokens_grad = result.reshape(tokens.shape), tokens_grad.reshape(tokens.shape)
    mine, send = call(
        order,
        middle_kernel,
        "middle",
        0.02,
        [((n_dp, columns), F32)] * 2,
        [stay, swap(send, "tensor", 1)],
    )
    (table_grad,) = call(
        order,
        table_kernel,
        "table",
        0.02,
        [((columns, n_classes), F32)],
        [mine, swap(send, "tensor", 2), cond_cols, labels_all],
    )
    if n_dp == 8:
        qkv_grad, out_grad, down_grad, up_grad = call(
            order,
            last_kernel,
            "last_add",
            0.02,
            [((chunk, w), F32) for w in (n_qkv, n_att, hidden, hidden)],
            [*qkv_grad, *mlp_grad],
        )
    else:
        grad = halve_all(qkv_grad[0].reshape(n_dp // 2, chunk, -1), [1])
        qkv_grad, out_grad = grad[:, :n_qkv], grad[:, n_qkv:]
        down_grad, up_grad = (
            halve_all(g.reshape(n_dp // 4, chunk, hidden), [0, 2]) for g in mlp_grad
        )
    return (
        result,
        tokens_grad,
        qkv_grad,
        out_grad,
        up_grad,
        down_grad,
        ada_grad,
        table_grad.T,
        qv_grad,
        proj_grad,
        fc1_grad,
        fc2_grad,
        ada_bias_grad,
    )


def solution(mesh):
    placed = (
        P("dp", None, None, None),
        P("dp"),
        P("dp"),
        P("dp"),
        P(None, "tensor"),
        P(None, "tensor"),
        P("tensor"),
        P(None, "tensor"),
        P("tensor"),
        P(None, "tensor"),
        P(),
        P(None, "tensor"),
        P("tensor"),
        P(None, "tensor"),
        P(),
        P("dp", None, None, None),
    )
    return jax.shard_map(
        shards,
        mesh=mesh,
        in_specs=placed,
        out_specs=(
            P("dp", None, None, None),
            P("dp", None, None, None),
            P("dp", "tensor"),
            P("dp", "tensor"),
            P("dp", "tensor"),
            P("dp", "tensor"),
            P("dp", "tensor"),
            P(None, "tensor"),
            P("tensor"),
            P(),
            P("tensor"),
            P(),
            P("tensor"),
        ),
        check_vma=False,
    )
```

```python
import math

import jax
import jax.numpy as jnp
import numpy as np
from jax import lax
from jax.experimental import pallas as pl
from jax.experimental.pallas import tpu as pltpu
from jax.sharding import PartitionSpec as P

HEAD_DIM = 72
BF = jnp.bfloat16
F32 = jnp.float32


def dot(left, right):
    return jnp.dot(left, right, preferred_element_type=F32)


def dot_trans(left, right):
    return lax.dot_general(left, right, (((1,), (1,)), ((), ())), preferred_element_type=F32)


def dot_rows(left, right):
    return lax.dot_general(left, right, (((0,), (0,)), ((), ())), preferred_element_type=F32)


def swap(value, axis, flip):
    size = lax.axis_size(axis)
    return lax.ppermute(value, axis, [(i, i ^ flip) for i in range(size)])


def call(order, body, name, us, outs, args, scratch=(), also=(), limit=24, free=False):
    specs = [
        pl.BlockSpec(
            memory_space=pltpu.SMEM if a.dtype == jnp.int32 else pltpu.VMEM
        )
        for a in args
    ]
    marks = [*(order[:1] if free else order), *also]
    specs += [pl.BlockSpec(memory_space=pl.ANY)] * len(marks)
    n_args, n_outs = len(args), len(outs)
    first_out = n_args + len(marks)

    def whole(*refs):
        body(*refs[:n_args], *refs[first_out : first_out + n_outs], *refs[first_out + n_outs + 1 :])
        refs[first_out + n_outs][...] = jnp.zeros((8, 128), F32)

    *results, mark = pl.pallas_call(
        whole,
        out_shape=[jax.ShapeDtypeStruct(s, d) for s, d in [*outs, ((8, 128), F32)]],
        in_specs=specs,
        out_specs=[pl.BlockSpec(memory_space=pltpu.VMEM)] * (n_outs + 1),
        scratch_shapes=list(scratch),
        compiler_params=pltpu.CompilerParams(vmem_limit_bytes=limit << 20),
        cost_estimate=pl.CostEstimate(
            flops=int(us * 1.1e9), bytes_accessed=1024, transcendentals=0
        ),
        name=name,
    )(*args, *marks)
    if not free:
        order.clear()
    order.append(mark)
    return results


def behind(value, *others):
    return lax.optimization_barrier((value, *others))[0]


def pad_lanes(width):
    return -(-width // 128) * 128


def standardize(value):
    center = value - jnp.mean(value, axis=-1, keepdims=True)
    spread = jnp.mean(center * center, axis=-1, keepdims=True)
    inv = lax.rsqrt(spread + 1e-06)
    return center * inv, inv


def standardize_back(grad, scale, normed, inv):
    g = grad * (1.0 + scale)
    return (
        g
        - jnp.mean(g, axis=-1, keepdims=True)
        - normed * jnp.mean(g * normed, axis=-1, keepdims=True)
    ) * inv


def gelu_pair(value):
    k, c = math.sqrt(2.0 / math.pi), 0.044715
    square = value * value
    h = 0.5 + 0.5 * jnp.tanh(value * (k + (k * c) * square))
    steep = value * (2.0 * k + (6.0 * k * c) * square)
    return value * h, h * (1.0 + (1.0 - h) * steep)


def row_part(ref, spots, name):
    at, size = spots[name]
    return ref[:, at : at + size].astype(F32)


def column_sum(value):
    return jnp.sum(value, axis=0, keepdims=True)


def kept_rows(length_ref, half, frames):
    frame = lax.broadcasted_iota(jnp.int32, (half, 1), 0) % frames
    return frame < length_ref[0]


def split_chunks(value, n_dp, bit):
    r = value.shape[1] // n_dp
    low, high = (
        jnp.concatenate(
            [value[:, i * r : i * r + r] for i in range(n_dp) if (i >> bit) & 1 == side], axis=1
        )
        for side in range(2)
    )
    mine_low = ((lax.axis_index("dp") >> bit) & 1) == 0
    return jnp.where(mine_low, low, high), jnp.where(mine_low, high, low)


def clock_kernel(spots, times, row, clock):
    freqs = row_part(row, spots, "freqs")
    angles = jnp.full(freqs.shape, times[0], jnp.int32).astype(F32) * freqs
    clock[...] = jnp.concatenate([jnp.cos(angles), jnp.sin(angles)], axis=1)


def start_kernel(tokens, cotangent, normed, inv, tok_half, cot_half):
    half = tok_half.shape[0]
    rows = pl.ds(pl.multiple_of((lax.axis_index("tensor") & 1) * half, half), half)
    tok_half[...] = tokens[rows, :]
    cot_half[...] = cotangent[rows, :]
    normed[...], inv[...] = standardize(tok_half[...].astype(F32))


def modulation_kernel(spots, e0, e1, e2, e3, clock, weight, bias, cond_out, part, rows):
    rank = lax.axis_index("tensor")
    for flip, piece in enumerate((e0, e1, e2, e3)):
        rows[pl.ds(rank ^ flip, 1), :] = piece[...].astype(F32)
    cond = clock[...] + jnp.concatenate([rows[i : i + 1, :] for i in range(4)], axis=1)
    cond_out[...] = cond
    act = (cond / (1.0 + jnp.exp(-cond))).astype(BF)
    act = jnp.broadcast_to(act, (16, act.shape[1]))
    part[...] = dot_trans(act, weight[...])[0:1, :] + row_part(bias, spots, "ada")


def split_heads(qkv, heads):
    at = lambda h, j: (3 * h + j) * HEAD_DIM
    return [
        tuple(qkv[:, at(h, j) : at(h, j) + HEAD_DIM].astype(BF) for j in range(3))
        for h in range(heads)
    ]


def attention_kernel(
    frames, spots, length, normed, cotangent, m0, m1, m2, m3,
    qkv_a, qkv_b, bias_a, bias_b, out_a, out_b,
    part, mods, normed_low, saved_a, saved_b, probs_out, att_a, att_b, low_grad, rows,
):
    rank = lax.axis_index("tensor")
    width = normed.shape[1]
    for flip, piece in enumerate((m0, m1, m2, m3)):
        rows[pl.ds(rank ^ flip, 1), :] = piece[...]
    cols = rows.shape[1]
    extra = cols - width
    for side in range(2):
        a, b = rows[2 * side : 2 * side + 1, :], rows[2 * side + 1 : 2 * side + 2, :]
        mods[3 * side : 3 * side + 1, :] = a[:, :width]
        mods[3 * side + 1 : 3 * side + 2, :] = jnp.concatenate([a[:, width:], b[:, :extra]], axis=1)
        mods[3 * side + 2 : 3 * side + 3, :] = b[:, extra:]
    mods[6:8, :] = jnp.zeros((2, width), F32)
    low = (normed[...] * (1.0 + mods[1:2, :]) + mods[0:1, :]).astype(BF)
    normed_low[...] = low
    half = low.shape[0]
    row_id = lax.broadcasted_iota(jnp.int32, (half, half), 0)
    col_id = lax.broadcasted_iota(jnp.int32, (half, half), 1)
    seen = ((row_id // frames) == (col_id // frames)) & ((col_id % frames) < length[0])
    factor = HEAD_DIM ** (-0.5)
    heads = out_a.shape[0] // HEAD_DIM
    heads_in = []
    for w, b, saved in ((qkv_a, bias_a, saved_a), (qkv_b, bias_b, saved_b)):
        qv = row_part(b, spots, "qv")
        zero = jnp.zeros((1, HEAD_DIM), F32)
        pieces = [
            piece
            for h in range(heads)
            for piece in (
                qv[:, 2 * h * HEAD_DIM : (2 * h + 1) * HEAD_DIM],
                zero,
                qv[:, (2 * h + 1) * HEAD_DIM : (2 * h + 2) * HEAD_DIM],
            )
        ]
        qkv = dot_trans(low, w[...]) + jnp.concatenate(pieces, axis=1)
        saved[...] = qkv.astype(BF)
        heads_in += split_heads(qkv, heads)
    all_scores = [dot_trans(q, k) for q, k, _ in heads_in]
    all_probs = []
    for i, scores in enumerate(all_scores):
        scores = jnp.where(seen, scores * factor, -1e30)
        raised = jnp.exp(scores - jnp.max(scores, axis=-1, keepdims=True))
        probs = raised / jnp.sum(raised, axis=-1, keepdims=True)
        probs_out[i] = probs
        all_probs.append(probs.astype(BF))
    outs = [dot(probs, v) for probs, (_, _, v) in zip(all_probs, heads_in)]
    total = None
    for block, (o, att_ref) in enumerate(((out_a, att_a), (out_b, att_b))):
        for h in range(heads):
            att_ref[:, h * HEAD_DIM : (h + 1) * HEAD_DIM] = outs[block * heads + h].astype(BF)
        term = dot(att_ref[...], o[...])
        total = term if total is None else total + term
    part[...] = total.astype(BF)
    keep = kept_rows(length, half, frames)
    low_grad[...] = (mods[5:6, :] * jnp.where(keep, cotangent[...].astype(F32), 0.0)).astype(BF)


def early_back_kernel(
    n_dp, low_ref, down_a, down_b, normed_low, att_a, att_b,
    grad_a, grad_b, pack_far, own_chunks, fc2_sum, pick,
):
    low = low_ref[...]
    width = low.shape[1]
    grad_a[...] = dot(low, down_a[...])
    grad_b[...] = dot(low, down_b[...])
    fc2_sum[...] = column_sum(low.astype(F32))
    n_att = att_a.shape[1]
    part = width // 2
    mine, other = split_chunks(normed_low[...].astype(F32), n_dp, 1)
    pack_far[:, 0:n_att] = att_a[...]
    pack_far[:, n_att : 2 * n_att] = att_b[...]
    at = pad_lanes(2 * n_att)
    pack_far[:, at : at + part] = other.astype(BF)
    own_chunks[:, 0:part] = mine.astype(BF)
    r = width // n_dp
    feature = lax.broadcasted_iota(jnp.int32, pick.shape, 1)
    column = lax.broadcasted_iota(jnp.int32, pick.shape, 0)
    target = column + (lax.axis_index("dp") & 5) * r
    ahead = 0
    for k in range(1, n_dp // 4):
        now = ((k & 1) << 1) + ((k >> 1) << 3) - k
        target = target + jnp.where(column >= k * r, (now - ahead) * r, 0)
        ahead = now
    pick[...] = jnp.where(feature == target, 1.0, 0.0).astype(BF)


def mlp_kernel(
    spots, tokens, part1, part1_other, mods, up_a, up_b, fc1_a, fc1_b, grad_a, grad_b,
    part3, act_out, pre_out, low_out, branch_out, normed_out, inv_out, sums,
):
    branch = part1[...].astype(F32) + part1_other[...].astype(F32) + row_part(fc1_a, spots, "proj")
    branch_out[...] = branch
    mid = tokens[...].astype(F32) + mods[2:3, :] * branch
    normed, inv = standardize(mid)
    normed_out[...] = normed
    inv_out[...] = inv
    low = (normed * (1.0 + mods[4:5, :]) + mods[3:4, :]).astype(BF)
    low_out[...] = low
    cols = up_a.shape[1]
    blocks = ((up_a, fc1_a, grad_a), (up_b, fc1_b, grad_b))
    hidden = [dot(low, u[...]) + row_part(b, spots, "fc1") for u, b, _ in blocks]
    pres = []
    for block, (value, (_, _, g)) in enumerate(zip(hidden, blocks)):
        act, slope = gelu_pair(value)
        act_out[:, block * cols : (block + 1) * cols] = act.astype(BF)
        pre = (g[...] * slope).astype(BF)
        if block == 0:
            pre_out[...] = pre
        sums[block : block + 1, :] = column_sum(pre.astype(F32))
        pres.append(pre)
    part3[...] = (dot_trans(pres[0], up_a[...]) + dot_trans(pres[1], up_b[...])).astype(BF)


def mlp_tail_kernel(act, down_a, down_b, part2):
    cols = down_a.shape[1]
    part2[...] = (
        dot_trans(act[:, 0:cols], down_a[...]) + dot_trans(act[:, cols : 2 * cols], down_b[...])
    ).astype(BF)


def rows_kernel(*refs):
    half = refs[0].shape[0]
    for i, source in enumerate(refs[:-1]):
        refs[-1][i * half : (i + 1) * half, :] = source[...]


def remake_kernel(n_dp, spots, own, before, last, n_blocks, grads_rows, pick, up, down, bias, *refs):
    cols = up.shape[1]
    normed, grads, refs = refs[:n_blocks], refs[n_blocks : 2 * n_blocks], refs[2 * n_blocks :]
    if n_blocks == 1 and normed[0].shape[0] > grads_rows:
        normed, grads = [normed[0].at[0:grads_rows, :]], [grads[0].at[grads_rows : 2 * grads_rows, :]]
    down_sum, up_sum = 0.0, 0.0
    if own:
        act_own, pre_own, refs = refs[0][:, 0:cols], refs[1][...], refs[2:]
    if before:
        down_sum, up_sum, refs = refs[0][...], refs[1][...], refs[2:]
    joined = lambda parts: parts[0] if len(parts) == 1 else jnp.concatenate(parts, axis=0)
    n_new, g_new = (joined([ref[...] for ref in v[int(own) :]]) for v in (normed, grads))
    act, slope = gelu_pair(dot(n_new, up[...]) + row_part(bias, spots, "fc1"))
    act, pre = act.astype(BF), (dot(g_new, down[...]) * slope).astype(BF)
    if own:
        n_new, g_new = joined([normed[0][...], n_new]), joined([grads[0][...], g_new])
        act, pre = joined([act_own, act]), joined([pre_own, pre])
    down_sum = down_sum + dot(dot_trans(pick[...], g_new).astype(BF), act)
    up_sum = up_sum + dot(dot_trans(pick[...], n_new).astype(BF), pre)
    if last and n_dp == 8:
        stay, send = refs
        r = down_sum.shape[0] // 2
        high = ((lax.axis_index("dp") >> 1) & 1) == 1
        for i, total in enumerate((down_sum, up_sum)):
            one, two = total[:r, :], total[r:, :]
            stay[:, i * cols : (i + 1) * cols] = jnp.where(high, two, one)
            send[:, i * cols : (i + 1) * cols] = jnp.where(high, one, two).astype(BF)
    else:
        refs[0][...] = down_sum
        refs[1][...] = up_sum


def attention_back_kernel(
    frames, length, part3, part3_other, mods, normed, inv, branch, cotangent,
    out_a, out_b, qkv_a, qkv_b, saved_a, saved_b, probs_in,
    part4, mid_grad_out, low_out, stacked, sums,
):
    upstream = cotangent[...].astype(F32)
    half, width = upstream.shape
    keep = kept_rows(length, half, frames)
    grad = part3[...].astype(F32) + part3_other[...].astype(F32)
    norm = normed[...]
    mid_grad = jnp.where(keep, upstream, 0.0) + standardize_back(grad, mods[4:5, :], norm, inv[...])
    mid_grad_out[...] = mid_grad
    low = (mods[2:3, :] * mid_grad).astype(BF)
    low_out[...] = low
    sums[0:1, :] = column_sum(grad)
    sums[1:2, :] = column_sum(grad * norm)
    sums[2:3, :] = column_sum(mid_grad * branch[...])
    sums[3:4, :] = column_sum(low.astype(F32))
    factor = HEAD_DIM ** (-0.5)
    heads = out_a.shape[0] // HEAD_DIM
    cols = heads * 3 * HEAD_DIM
    wide = pad_lanes(cols)
    heads_in, att_grads = [], []
    for o, saved in ((out_a, saved_a), (out_b, saved_b)):
        att_grad = dot_trans(low, o[...])
        heads_in += split_heads(saved[...].astype(F32), heads)
        att_grads += [
            att_grad[:, h * HEAD_DIM : (h + 1) * HEAD_DIM].astype(BF) for h in range(heads)
        ]
    all_probs_grad = [dot_trans(ag, v) for ag, (_, _, v) in zip(att_grads, heads_in)]
    value_grads = [dot_rows(probs_in[i].astype(BF), ag) for i, ag in enumerate(att_grads)]
    all_low = []
    for i, probs_grad in enumerate(all_probs_grad):
        probs = probs_in[i]
        inner = jnp.sum(probs * probs_grad, axis=-1, keepdims=True)
        all_low.append((probs * (probs_grad - inner)).astype(BF))
    query_grads = [dot(scores_low, k) * factor for scores_low, (_, k, _) in zip(all_low, heads_in)]
    key_grads = [dot_rows(scores_low, q) * factor for scores_low, (q, _, _) in zip(all_low, heads_in)]
    total = None
    for block, w in enumerate((qkv_a, qkv_b)):
        for h in range(heads):
            i = block * heads + h
            at = block * wide + h * 3 * HEAD_DIM
            for j, piece in enumerate((query_grads[i], key_grads[i], value_grads[i])):
                stacked[:, at + j * HEAD_DIM : at + (j + 1) * HEAD_DIM] = piece.astype(BF)
        mine = stacked[:, block * wide : block * wide + cols]
        sums[4 + block : 5 + block, 0:cols] = column_sum(mine.astype(F32))
        term = dot(mine, w[...])
        total = term if total is None else total + term
    part4[...] = total.astype(BF)


def pack_back_kernel(n_dp, low, stacked, pack_far, own_chunks):
    mine, other = split_chunks(low[...].astype(F32), n_dp, 1)
    part, cols = mine.shape[1], stacked.shape[1]
    pack_far[:, 0:cols] = stacked[...]
    pack_far[:, cols : cols + part] = other.astype(BF)
    own_chunks[:, 0:part] = mine.astype(BF)


def output_kernel(
    frames, spots, length, tokens, part2, part2_other, bias, mods, branch1, cotangent,
    result, gate_sum,
):
    inputs, upstream = tokens[...].astype(F32), cotangent[...].astype(F32)
    keep = kept_rows(length, inputs.shape[0], frames)
    branch = part2[...].astype(F32) + part2_other[...].astype(F32) + row_part(bias, spots, "fc2")
    mid = inputs + mods[2:3, :] * branch1[...]
    result[...] = jnp.where(keep, mid + mods[5:6, :] * branch, inputs).astype(BF)
    gate_sum[...] = column_sum(jnp.where(keep, upstream, 0.0) * branch)


def input_back_kernel(
    frames, length, part4, part4_other, mods, normed, inv, mid_grad, cotangent,
    back_sums, gate2_sum, fc2_sum, pre_sums, result, both, sums,
):
    upstream = cotangent[...].astype(F32)
    keep = kept_rows(length, upstream.shape[0], frames)
    grad = part4[...].astype(F32) + part4_other[...].astype(F32)
    norm = normed[...]
    back = standardize_back(grad, mods[1:2, :], norm, inv[...])
    width = norm.shape[1]
    both[:, :width] = result[...]
    both[:, width:] = (mid_grad[...] + back + jnp.where(keep, 0.0, upstream)).astype(BF)
    sums[0:1, :] = column_sum(grad)
    sums[1:2, :] = column_sum(grad * norm)
    sums[2:3, :] = back_sums[2:3, :]
    sums[3:5, :] = back_sums[0:2, :]
    sums[5:6, :] = gate2_sum[...]
    sums[6:7, :] = fc2_sum[...]
    sums[7:8, :] = back_sums[3:4, :]
    sums[8:10, :] = pre_sums[0:2, :]
    sums[10:12, :] = back_sums[4:6, :]
    sums[12:16, :] = jnp.zeros((4, sums.shape[1]), F32)


def vector_kernel(layout, label, mine, other, cond, vector):
    rank = lax.axis_index("tensor")
    width = mine.shape[1]
    both = mine[...] + other[...]
    upper = rank >= 2
    pick = lambda i: jnp.where(upper, both[3 + i : 4 + i, :], both[i : i + 1, :])
    cols = layout["mod"][1]
    extra = cols - width
    shift, scale, gate = pick(0), pick(1), pick(2)
    even = jnp.concatenate([shift, scale[:, :extra]], axis=1)
    odd = jnp.concatenate([scale[:, extra:], gate], axis=1)
    vector[...] = jnp.zeros(vector.shape, F32)

    def put(name, value):
        at, size = layout[name]
        vector[:, at : at + size] = value

    put("mod", jnp.where((rank & 1) == 0, even, odd).astype(BF).astype(F32))
    put("fc2", both[6:7, :])
    put("proj", both[7:8, :])
    put("fc1", (mine[8:9, :] + other[9:10, :])[:, : layout["fc1"][1]])
    put("stack", (mine[10:11, :] + other[11:12, :])[:, : layout["stack"][1]])
    put("cond", cond[...])
    put("label", jnp.full((1, 128), label[0], jnp.int32).astype(F32))


def gathered_kernel(layout, n_dp, rows_out, flips, weight, source, *refs):
    ada_grad, ada_bias, qv, proj, fc1, fc2, stay, send, cond_cols, labels, table = refs
    rank, place = lax.axis_index("tensor"), lax.axis_index("dp")
    for i in range(n_dp):
        flip = sum(f for k, f in enumerate(flips) if (i >> k) & 1)
        table[pl.ds(place ^ flip, 1), :] = source[i : i + 1, :]

    def get(name):
        at, size = layout[name]
        return table[:, at : at + size]

    sums = lambda name: column_sum(get(name))
    for name, out in (("mod", ada_bias), ("proj", proj), ("fc1", fc1), ("fc2", fc2)):
        out[...] = sums(name).reshape(out.shape)
    stack = sums("stack")
    pieces = [
        stack[:, i * HEAD_DIM : (i + 1) * HEAD_DIM]
        for i in range(stack.shape[1] // HEAD_DIM)
        if i % 3 != 1
    ]
    qv[...] = jnp.concatenate(pieces, axis=1).reshape(qv.shape)
    mod = get("mod").astype(BF)
    cond = get("cond")
    act = cond / (1.0 + jnp.exp(-cond))
    width = act.shape[1]
    mine = pltpu.roll(act, (width - place * rows_out) % width, 1)[:, :rows_out].astype(BF)
    ada_grad[...] = dot_rows(mine, mod)
    columns = cond_cols.shape[1]
    cond_part = dot(mod, weight[...])
    wide = pad_lanes(columns)
    for flip in range(4):
        out, at = (stay, send)[flip & 1], (flip >> 1) * wide
        piece = pltpu.roll(cond_part, (width - (rank ^ flip) * columns) % width, 1)[:, :columns]
        out[:, at : at + columns] = piece
    cond_cols[...] = pltpu.roll(cond, (width - rank * columns) % width, 1)[:, :columns]
    labels[...] = get("label")


def middle_kernel(stay, other, mine, send):
    columns = mine.shape[1]
    wide = pad_lanes(columns)
    mine[...] = stay[:, 0:columns] + other[:, 0:columns]
    send[...] = stay[:, wide : wide + columns] + other[:, wide : wide + columns]


def table_kernel(mine, other, cond_cols, labels, out):
    cond = cond_cols[...]
    gate = 1.0 / (1.0 + jnp.exp(-cond))
    grad = (mine[...] + other[...]) * gate * (1.0 + cond * (1.0 - gate))
    classes = lax.broadcasted_iota(jnp.int32, (cond.shape[0], out.shape[1]), 1).astype(F32)
    onehot = jnp.where(labels[:, : out.shape[1]] == classes, 1.0, 0.0)
    out[...] = lax.dot_general(
        grad,
        onehot,
        (((0,), (0,)), ((), ())),
        precision=lax.Precision.HIGHEST,
        preferred_element_type=F32,
    )


def forward_kernel(spans, *refs):
    for parts, out in zip(spans, refs[-len(spans) :]):
        at = 0
        for i, start, size in parts:
            out[:, at : at + size] = refs[i][:, start : start + size]
            at += size


def weight_kernel(n_dp, split, products, n_in, *refs):
    outs, lefts = refs[n_in : -len(products)], refs[-len(products) :]
    half = refs[0].shape[0]
    part = lefts[0].shape[0]
    r = part // (n_dp // 2)
    at = 0
    for left, (left_rows, right_rows, cols) in zip(lefts, products):
        for i, (j, start) in enumerate(left_rows):
            value = refs[j][:, start : start + part]
            left[:, i * half : (i + 1) * half] = value.astype(F32).T.astype(BF)
        right = [refs[j][:, start : start + cols] for j, start in right_rows]
        right = jnp.concatenate(right, axis=0)
        if split is None:
            outs[0][:, at : at + cols] = dot(left[...], right)
        else:
            near, far = ((lax.axis_index("dp") >> bit) & 1 for bit in split)
            for (stay, send), k in ((outs[0:2], 1 - far), (outs[2:4], far)):
                for out, side in ((stay, near), (send, 1 - near)):
                    start = pl.multiple_of((2 * k + side) * r, r)
                    out[:, at : at + cols] = dot(left[pl.ds(start, r), :], right).astype(out.dtype)
        at += cols


def halve_kernel(stay, other, send):
    send[...] = (stay[...] + other[...].astype(F32)).astype(BF)


def last_mlp_kernel(mlp, mlp_other, down, up):
    for target, start in ((down, 0), (up, down.shape[1])):
        at = slice(start, start + target.shape[1])
        target[...] = mlp[:, at] + mlp_other[:, at].astype(F32)


def last_qkv_kernel(near, near_other, far_other, qkv, out):
    cols = qkv.shape[1]
    total = near[...] + near_other[...].astype(F32) + far_other[...].astype(F32)
    qkv[...] = total[:, :cols]
    out[...] = total[:, cols:]


def join_kernel(mine, other, *outs):
    half, width = mine.shape[0], outs[0].shape[1]
    core = lax.axis_index("tensor") & 1
    for source, side in ((mine, core), (other, 1 - core)):
        rows = pl.ds(pl.multiple_of(side * half, half), half)
        for i, out in enumerate(outs):
            out[rows, :] = source[:, i * width : (i + 1) * width]


def stack_kernel(mine, other, out):
    n = mine.shape[0]
    out[0:n, :] = mine[...]
    out[n : 2 * n, :] = other[...]


def shards(
    tokens,
    lengths,
    timesteps,
    labels,
    class_table,
    ada_weight,
    ada_bias,
    qkv_weight,
    qv_bias,
    out_weight,
    proj_bias,
    up_weight,
    fc1_bias,
    down_weight,
    fc2_bias,
    cotangent,
):
    clips, patches, frames, width = tokens.shape
    assert clips == 1 and lax.axis_size("tensor") == 4
    rows = patches * frames
    half = rows // 2
    n_att = out_weight.shape[1]
    heads = n_att // HEAD_DIM
    n_qkv = qkv_weight.shape[1]
    hidden = up_weight.shape[1]
    columns = class_table.shape[1]
    ada_cols = ada_weight.shape[1]
    n_classes = class_table.shape[0]
    t_rank = lax.axis_index("tensor")
    d_rank = lax.axis_index("dp")
    n_dp = lax.axis_size("dp")
    order = []
    chunk = width // n_dp
    part = width // 2
    wide = pad_lanes(part)

    tokens2 = tokens.reshape(rows, width)
    cot2 = cotangent.reshape(rows, width)
    half_width = width // 2
    freqs = np.exp(-math.log(10000.0) * np.arange(half_width) / half_width)
    small = (
        ("ada", ada_bias), ("qv", qv_bias), ("fc1", fc1_bias), ("proj", proj_bias),
        ("fc2", fc2_bias), ("freqs", jnp.asarray(freqs, F32)),
    )
    spots, n_row = {}, 0
    for name, v in small:
        spots[name] = (n_row, v.shape[0])
        n_row += pad_lanes(v.shape[0])
    bias_row = sum(
        jnp.pad(v.astype(F32), (spots[name][0], n_row - spots[name][0] - v.shape[0]))
        for name, v in small
    ).reshape(1, n_row)

    def gather_tensor(own, *others):
        across = behind(swap(own, "tensor", 2), *others)
        return [own, swap(own, "tensor", 1), across, swap(across, "tensor", 1)]

    def pair(weight, *others):
        return weight, swap(behind(weight, *others), "tensor", 1)

    picked = lax.dynamic_slice_in_dim(class_table, labels[0], 1, 0)
    (clock,) = call(
        order,
        lambda *refs: clock_kernel(spots, *refs),
        "clock",
        5.0,
        [((1, width), F32)],
        [timesteps, bias_row],
    )
    pieces = gather_tensor(picked, clock, bias_row)
    bias_ws = pair(bias_row)
    cond, mod_part = call(
        order,
        lambda *refs: modulation_kernel(spots, *refs),
        "modulation",
        1.0,
        [((1, width), F32), ((1, ada_cols), F32)],
        [*pieces, clock, ada_weight.T, bias_row],
        [pltpu.VMEM((8, columns), F32)],
    )
    normed1, inv1, tok, cot = call(
        order,
        start_kernel,
        "start",
        1.0,
        [((half, width), F32), ((half, 1), F32), ((half, width), BF), ((half, width), BF)],
        [tokens2, cot2],
    )
    qkv_ws = pair(qkv_weight.T, pieces[1], pieces[3])
    out_ws = pair(out_weight.T, pieces[1], pieces[3])
    mod_pieces = gather_tensor(mod_part, bias_ws[1], qkv_ws[1], out_ws[1], normed1)
    up_ws = pair(up_weight, *mod_pieces)
    down_ws = pair(down_weight, *mod_pieces)

    part1, mods, low1, saved_a, saved_b, probs, att_a, att_b, low_grad = call(
        order,
        lambda *refs: attention_kernel(frames, spots, *refs),
        "attention",
        4.0,
        [
            ((half, width), BF),
            ((8, width), F32),
            ((half, width), BF),
            ((half, n_qkv), BF),
            ((half, n_qkv), BF),
            ((2 * heads, half, half), F32),
            ((half, n_att), BF),
            ((half, n_att), BF),
            ((half, width), BF),
        ],
        [lengths, normed1, cot, *mod_pieces, *qkv_ws, *bias_ws, *out_ws],
        [pltpu.VMEM((8, ada_cols), F32)],
    )
    part1_other = swap(part1, "tensor", 2)

    att_far, att_core = pad_lanes(2 * n_att), pad_lanes(n_att)
    grad_a, grad_b, pack1, chunks1, fc2_sum, pick = call(
        order,
        lambda *refs: early_back_kernel(n_dp, *refs),
        "early_back",
        2.0,
        [
            ((half, hidden), F32),
            ((half, hidden), F32),
            ((half, att_far + wide), BF),
            ((half, wide), BF),
            ((1, width), F32),
            ((part // 2, width), BF),
        ],
        [low_grad, *down_ws, low1, att_a, att_b],
    )
    far1 = swap(pack1, "dp", 2)
    grad_y = swap(low_grad, "dp", 1)
    grad_f = swap(low_grad, "dp", 4)

    part3, act, pre_own, low2, branch1, normed2, inv2, pre_sums = call(
        order,
        lambda *refs: mlp_kernel(spots, *refs),
        "mlp",
        3.0,
        [
            ((half, width), BF),
            ((half, 2 * hidden), BF),
            ((half, hidden), BF),
            ((half, width), BF),
            ((half, width), F32),
            ((half, width), F32),
            ((half, 1), F32),
            ((2, hidden), F32),
        ],
        [tok, part1, part1_other, mods, *up_ws, *bias_ws, grad_a, grad_b],
    )
    part3_other = swap(part3, "tensor", 2)
    rows_y = swap(behind(low2, grad_y), "dp", 1)
    rows_f = swap(low2, "dp", 4)

    def forward(name, spans, sources, us=0.02):
        outs = [((half, sum(size for _, _, size in parts)), BF) for parts in spans]
        outs = call(
            order, lambda *refs: forward_kernel(spans, *refs), name, us, outs, sources
        )
        return [swap(out, "tensor", 1) for out in outs]

    def first_grads(name, products, args):
        cols = sum(p[2] for p in products)
        scratch = [pltpu.VMEM((part, 4 * half), BF)] * len(products)
        split, outs = None, [((part, cols), F32)]
        if n_dp == 8:
            split, outs = (0, 2), [((chunk, cols), F32), ((chunk, cols), BF)] * 2
        return call(
            order,
            lambda *refs: weight_kernel(n_dp, split, products, len(args), *refs),
            name,
            0.02,
            outs,
            args,
            scratch,
        )

    def halve_all(grad, done):
        for b in range((n_dp - 1).bit_length()):
            if b not in done:
                my_bit = (d_rank >> b) & 1
                grad = grad.reshape(grad.shape[0] // 2, 2, chunk, grad.shape[2])
                send = lax.dynamic_index_in_dim(grad, 1 - my_bit, 1, keepdims=False).astype(BF)
                stay = lax.dynamic_index_in_dim(grad, my_bit, 1, keepdims=False)
                grad = stay + swap(send, "dp", 1 << b).astype(F32)
        return grad[0]

    (part2,) = call(
        order,
        mlp_tail_kernel,
        "mlp_tail",
        1.0,
        [((half, width), BF)],
        [act, *down_ws],
    )
    part2_other = swap(behind(part2, far1), "tensor", 2)
    grad_yf = swap(behind(grad_f, part2), "dp", 1)

    part4, mid_grad, low_back, stacked, back_sums = call(
        order,
        lambda *refs: attention_back_kernel(frames, *refs),
        "attention_back",
        5.0,
        [
            ((half, width), BF),
            ((half, width), F32),
            ((half, width), BF),
            ((half, 2 * pad_lanes(n_qkv)), BF),
            ((8, width), F32),
        ],
        [
            lengths, part3, part3_other, mods, normed2, inv2, branch1, cot,
            *out_ws, *qkv_ws, saved_a, saved_b, probs,
        ],
        also=[grad_f],
    )
    part4_other = swap(part4, "tensor", 2)
    (near_rows,) = call(
        order,
        rows_kernel,
        "rows_near",
        0.02,
        [((4 * half, width), BF)],
        [low2, rows_y, low_grad, grad_y],
    )
    near_other = swap(near_rows, "tensor", 1)
    s_wide = pad_lanes(n_qkv)
    pack3, chunks3 = call(
        order,
        lambda *refs: pack_back_kernel(n_dp, *refs),
        "pack_back",
        0.02,
        [((half, 2 * s_wide + wide), BF), ((half, wide), BF)],
        [low_back, stacked],
        free=True,
    )
    far3 = swap(pack3, "dp", 2)

    def remake(name, normed, grads, own, before, last, us=0.02):
        outs = [((part // 2, hidden), F32)] * 2
        if last and n_dp == 8:
            outs = [((chunk, 2 * hidden), F32), ((chunk, 2 * hidden), BF)]
        return call(
            order,
            lambda *refs: remake_kernel(
                n_dp, spots, bool(own), bool(before), last, len(normed), 2 * half, *refs
            ),
            name,
            us,
            outs,
            [pick, up_weight, down_weight, bias_row, *normed, *grads, *own, *before],
            limit=40,
        )

    result, gate2_sum = call(
        order,
        lambda *refs: output_kernel(frames, spots, *refs),
        "output",
        2.0,
        [((half, width), BF), ((1, width), F32)],
        [lengths, tok, part2, part2_other, bias_row, mods, branch1, cot],
    )
    rows_yf = swap(behind(rows_f, gate2_sum), "dp", 1)
    sums2 = remake(
        "remake_near",
        [low2, rows_y, rows_f],
        [low_grad, grad_y, grad_f],
        [act, pre_own],
        [],
        False,
        us=1.0,
    )
    both, sums = call(
        order,
        lambda *refs: input_back_kernel(frames, *refs),
        "input_back",
        10.0,
        [((half, 2 * width), BF), ((16, width), F32)],
        [
            lengths, part4, part4_other, mods, normed1, inv1, mid_grad, cot,
            back_sums, gate2_sum, fc2_sum, pre_sums, result,
        ],
    )
    sums_other = swap(sums, "tensor", 1)
    sums2 = remake("remake_core0", [near_other], [near_other], [], sums2, False, us=2.0)
    (far_rows,) = call(
        order,
        rows_kernel,
        "rows_far",
        3.0,
        [((4 * half, width), BF)],
        [rows_f, rows_yf, grad_f, grad_yf],
        also=[sums_other],
    )
    far_rows_other = swap(far_rows, "tensor", 1)

    layout, at = {}, 0
    for name, size in (
        ("mod", ada_cols), ("fc2", width), ("proj", width), ("fc1", hidden), ("stack", n_qkv),
        ("cond", width), ("label", 128),
    ):
        layout[name] = (at, size)
        at += pad_lanes(size)
    (vector,) = call(
        order,
        lambda *refs: vector_kernel(layout, *refs),
        "vector",
        0.02,
        [((1, at), F32)],
        [labels, sums, sums_other, cond],
    )

    def stack(name, value, flip, us=0.02):
        n, cols = value.shape
        other = swap(value, "dp", flip)
        return call(order, stack_kernel, name, us, [((2 * n, cols), F32)], [value, other])[0]

    sums2 = remake("remake_yf", [rows_yf], [grad_yf], [], sums2, False)
    flips = [4, 1] + [1 << b for b in range(3, (n_dp - 1).bit_length())] + [2]
    mixed3, mixed1 = forward(
        "forward3",
        [
            [(0, s_wide, s_wide), (0, 2 * s_wide, wide), (1, s_wide, s_wide), (2, 0, wide)],
            [(3, n_att, att_core), (3, att_far, wide), (4, n_att, att_core), (5, 0, wide)],
        ],
        [far3, pack3, chunks3, far1, pack1, chunks1],
        us=3.0,
    )
    vector = stack("stack0", vector, flips[0], us=8.0)
    n_mix3 = s_wide + wide
    n_mix1 = att_core + wide
    left_qkv = ((1, 0), (7, n_mix1 + att_core), (2, att_far), (7, att_core))
    right_qkv = ((3, 0), (6, n_mix3), (5, 0), (6, 0))
    left_out = ((4, 0), (6, n_mix3 + s_wide), (5, 2 * s_wide), (6, s_wide))
    right_out = ((0, 0), (7, n_mix1), (2, 0), (7, 0))
    qkv_grad = first_grads(
        "qkv_grad",
        [(left_qkv, right_qkv, n_qkv), (left_out, right_out, n_att)],
        [pack1, chunks1, far1, pack3, chunks3, far3, mixed3, mixed1],
    )
    if n_dp == 8:
        far_other = swap(qkv_grad[1], "dp", 1)
    for i, flip in enumerate(flips[1:-1]):
        vector = stack("stack%d" % (i + 1), vector, flip, us=2.0)
    mlp_grad = remake("remake_core1", [far_rows_other], [far_rows_other], [], sums2, True)
    mlp_grad = (mlp_grad[0], swap(mlp_grad[1], "dp", 2) if n_dp == 8 else mlp_grad[1])
    both_other = swap(behind(both, mlp_grad[0]), "tensor", 1)
    if n_dp == 8:
        stay_far, send_far, stay_near, send_near = qkv_grad
        near_other = swap(send_near, "dp", 1)
        (send_far,) = call(
            order,
            halve_kernel,
            "qkv_halve",
            0.02,
            [(send_far.shape, BF)],
            [stay_far, far_other],
        )
        qkv_grad = stay_near, near_other, swap(send_far, "dp", 4)
    vector = stack("stack_last", vector, flips[-1])
    ada_grad, ada_bias_grad, qv_grad, proj_grad, fc1_grad, fc2_grad, stay, send, cond_cols, labels_all = call(
        order,
        lambda *refs: gathered_kernel(layout, n_dp, chunk, flips, *refs),
        "gathered",
        5.0,
        [((chunk, ada_cols), F32)]
        + [((n,), F32) for n in (ada_cols, qv_bias.shape[0], width, hidden, width)]
        + [((n_dp, 2 * pad_lanes(columns)), F32)] * 2
        + [((n_dp, columns), F32), ((n_dp, 128), F32)],
        [ada_weight.T, vector],
        [pltpu.VMEM((n_dp, at), F32)],
    )
    result, tokens_grad = call(
        order, join_kernel, "join", 0.02, [((rows, width), BF)] * 2, [both, both_other]
    )
    result, tokens_grad = result.reshape(tokens.shape), tokens_grad.reshape(tokens.shape)
    mine, send = call(
        order,
        middle_kernel,
        "middle",
        0.02,
        [((n_dp, columns), F32)] * 2,
        [stay, swap(send, "tensor", 1)],
    )
    (table_grad,) = call(
        order,
        table_kernel,
        "table",
        0.02,
        [((columns, n_classes), F32)],
        [mine, swap(send, "tensor", 2), cond_cols, labels_all],
    )
    if n_dp == 8:
        qkv_grad, out_grad = call(
            order,
            last_qkv_kernel,
            "qkv_add",
            0.02,
            [((chunk, w), F32) for w in (n_qkv, n_att)],
            qkv_grad,
        )
        down_grad, up_grad = call(
            order, last_mlp_kernel, "mlp_add", 0.02, [((chunk, hidden), F32)] * 2, mlp_grad
        )
    else:
        grad = halve_all(qkv_grad[0].reshape(n_dp // 2, chunk, -1), [1])
        qkv_grad, out_grad = grad[:, :n_qkv], grad[:, n_qkv:]
        down_grad, up_grad = (
            halve_all(g.reshape(n_dp // 4, chunk, hidden), [0, 2]) for g in mlp_grad
        )
    return (
        result,
        tokens_grad,
        qkv_grad,
        out_grad,
        up_grad,
        down_grad,
        ada_grad,
        table_grad.T,
        qv_grad,
        proj_grad,
        fc1_grad,
        fc2_grad,
        ada_bias_grad,
    )


def solution(mesh):
    placed = (
        P("dp", None, None, None),
        P("dp"),
        P("dp"),
        P("dp"),
        P(None, "tensor"),
        P(None, "tensor"),
        P("tensor"),
        P(None, "tensor"),
        P("tensor"),
        P(None, "tensor"),
        P(),
        P(None, "tensor"),
        P("tensor"),
        P(None, "tensor"),
        P(),
        P("dp", None, None, None),
    )
    return jax.shard_map(
        shards,
        mesh=mesh,
        in_specs=placed,
        out_specs=(
            P("dp", None, None, None),
            P("dp", None, None, None),
            P("dp", "tensor"),
            P("dp", "tensor"),
            P("dp", "tensor"),
            P("dp", "tensor"),
            P("dp", "tensor"),
            P(None, "tensor"),
            P("tensor"),
            P(),
            P("tensor"),
            P(),
            P("tensor"),
        ),
        check_vma=False,
    )
```
